128 devices in a mesh: fsdp: 16 (over z_hi, y, core), tp: 8 (over x, z_lo).
Axes of the slice: x: 4, y: 4, z: 4 (z_hi: 2, z_lo: 2; z = z_hi * 2 + z_lo), core: 2. Of those that a mesh axis runs over, the one named last changes fastest.
Arguments:
- inputs: bfloat16 [3, 16, 576, 1024], P(None, 'fsdp', 'tp'), may hold values from -6 to 6
- cotangent: bfloat16 [3, 16, 576, 1024], P(None, 'fsdp', 'tp'), may hold values from -6 to 6
- valid_slots: int32 [3, 16], P(None, 'fsdp'), may hold values 0 or 1
- ln1_gain: bfloat16 [1024], P(('fsdp', 'tp')), may hold values from 0.5 to 1.5
- ln1_bias: bfloat16 [1024], P(('fsdp', 'tp')), may hold values from -1 to 1
- qkv_weight: bfloat16 [3, 1024, 1024], P(None, 'fsdp', 'tp'), may hold values from -0.1875 to 0.1875
- qv_bias: bfloat16 [2, 16, 64], P(None, 'tp', 'fsdp'), may hold values from -0.59765625 to 0.59765625
- out_weight: bfloat16 [1024, 1024], P('tp', 'fsdp'), may hold values from -1 to 1
- out_bias: bfloat16 [1024], P(('fsdp', 'tp')), may hold values from -1 to 1
- ln2_gain: bfloat16 [1024], P(('fsdp', 'tp')), may hold values from 0.5 to 1.5
- ln2_bias: bfloat16 [1024], P(('fsdp', 'tp')), may hold values from -1 to 1
- fc1_weight: bfloat16 [1024, 4096], P('fsdp', 'tp'), may hold values from -0.1875 to 0.1875
- fc1_bias: bfloat16 [64, 64], P('tp', 'fsdp'), may hold values from -1 to 1
- fc2_weight: bfloat16 [4096, 1024], P('tp', 'fsdp'), may hold values from -0.09375 to 0.09375
- fc2_bias: bfloat16 [1024], P(('fsdp', 'tp')), may hold values from -1 to 1
Outputs:
- output_rows: bfloat16 [3, 16, 576, 1024], P(None, 'fsdp', 'tp')
- input_grad: bfloat16 [3, 16, 576, 1024], P(None, 'fsdp', 'tp')
- grad_ln1_gain: float32 [1024], P(('fsdp', 'tp'))
- grad_ln1_bias: float32 [1024], P(('fsdp', 'tp'))
- grad_qkv_weight: float32 [3, 1024, 1024], P(None, 'fsdp', 'tp')
- grad_qv_bias: float32 [2, 16, 64], P(None, 'tp', 'fsdp')
- grad_out_weight: float32 [1024, 1024], P('tp', 'fsdp')
- grad_out_bias: float32 [1024], P(('fsdp', 'tp'))
- grad_ln2_gain: float32 [1024], P(('fsdp', 'tp'))
- grad_ln2_bias: float32 [1024], P(('fsdp', 'tp'))
- grad_fc1_weight: float32 [1024, 4096], P('fsdp', 'tp')
- grad_fc1_bias: float32 [64, 64], P('tp', 'fsdp')
- grad_fc2_weight: float32 [4096, 1024], P('tp', 'fsdp')
- grad_fc2_bias: float32 [1024], P(('fsdp', 'tp'))
The draws below stay inside these ranges and needn't reach their ends.
Inputs may be any that keep to these rules, and one draw needn't show every extreme that they name: `valid_slots`: 1 marks a slot that holds an image, 0 an empty slot.
All inputs are finite; a program needn't handle non-finite values. No bound on the sum of `valid_slots` on one device may be relied on, other than what follows from the above.
Results may differ from the reference program's by a relative error of at most 0.025.
Values may be sent and summed in bfloat16 or wider, within the bound.
A program may use at most 128 MiB of HBM per device.

```python
import math
import jax
import jax.numpy as jnp
from jax import lax

D = 1024
HEADS = 16
HD = 64
FF = 4096
SEQ = 576
MICRO = 3
SLOTS_ALL = 16


def place_ends(values, key, low, largest):
    longest = values.shape.index(max(values.shape))
    spots = []
    for shift in (0, 1):
        where = [jax.random.randint(jax.random.fold_in(key, axis), (), 0, length) for axis, length in enumerate(values.shape)]
        where[longest] = (where[longest] + shift) % values.shape[longest]
        spots.append(tuple(where))
    return values.at[spots[0]].set(low).at[spots[1]].set(largest)


def raised(entries, stream_key, source, target, blocks, factor):
    def block_of(dim):
        return (jnp.arange(entries.shape[dim]) // (entries.shape[dim] // blocks)).reshape((-1,) + (1,) * (entries.ndim - 1 - dim))

    first = jax.random.permutation(stream_key, blocks)[block_of(target)]
    second = (block_of(target) + blocks // 2) % blocks
    return jnp.where((block_of(source) == first) | (block_of(source) == second), factor * entries, entries)


def level_of(rng, extent, shards, least, top_value):
    level, own = 1.0, jax.random.fold_in(rng, 6)
    for axis_at, parts in shards:
        heights = jnp.exp(jax.random.uniform(jax.random.fold_in(own, axis_at), (parts,), jnp.float32, least / len(shards), top_value / len(shards)))
        level = level * jnp.repeat(heights, extent[axis_at] // parts).reshape([-1 if axis == axis_at else 1 for axis in range(len(extent))])
    return level


def gaussian(key, dims, spread, most, shards=(), kind=jnp.bfloat16):
    gain = level_of(key, dims, shards, -0.22, 0.18) if shards else 1.0
    array = jax.random.normal(key, dims, jnp.float32) * spread * gain
    return jnp.minimum(jnp.maximum(array, -most), most).astype(kind)


def bell_draw_with(key, dims, scale, limit, pieces, heavy, dtype=jnp.bfloat16):
    array = scale * jax.random.normal(key, dims, jnp.float32)
    if pieces:
        array = array * level_of(key, dims, pieces, -0.22, 0.18)
    return jnp.clip(raised(array, jax.random.fold_in(key, 3), *heavy), -limit, limit).astype(dtype)


def setup_inputs(seed: int = 0) -> dict:
    splits = jax.random.split(jax.random.key(seed), 16)
    inputs = gaussian(splits[0], (MICRO, SLOTS_ALL, SEQ, D), 1.0, 6.0, ((1, 16), (2, 8)))
    cotangent = bell_draw_with(splits[1], (MICRO, SLOTS_ALL, SEQ, D), 1.0, 6.0, ((1, 16), (2, 8)), (1, 3, 16, 2.0))
    valid_slots = place_ends((jax.random.randint(splits[2], (MICRO, SLOTS_ALL), 0, 4) < 3).astype(jnp.int32), jax.random.fold_in(splits[2], 1), 0, 1)
    ln1_gain = jnp.clip(1.0 + 0.1 * jax.random.normal(splits[3], (D,), jnp.float32), 0.5, 1.5).astype(jnp.bfloat16)
    ln1_bias = gaussian(splits[4], (D,), 0.2, 1.0, ((0, 128),))
    qkv_weight = gaussian(splits[5], (3, D, D), D ** -0.5, 0.1875, ((1, 16), (2, 8)))
    qv_bias = gaussian(splits[6], (2, HEADS, HD), 0.1, 0.59765625, ((1, 8), (2, 16)))
    out_weight = gaussian(splits[7], (D, D), (D // 32) ** -0.5, 1.0, ((0, 8), (1, 16)))
    out_bias = gaussian(splits[8], (D,), 0.2, 1.0, ((0, 128),))
    ln2_gain = jnp.clip(1.0 + 0.1 * jax.random.normal(splits[9], (D,), jnp.float32), 0.5, 1.5).astype(jnp.bfloat16)
    ln2_bias = gaussian(splits[10], (D,), 0.2, 1.0, ((0, 128),))
    fc1_weight = gaussian(splits[11], (D, FF), D ** -0.5, 0.1875, ((0, 16), (1, 8)))
    fc1_bias = gaussian(splits[12], (FF // 64, 64), 0.2, 1.0, ((0, 8), (1, 16)))
    fc2_weight = gaussian(splits[13], (FF, D), FF ** -0.5, 0.09375, ((0, 8), (1, 16)))
    fc2_bias = gaussian(splits[14], (D,), 0.2, 1.0, ((0, 128),))
    return {"inputs": inputs, "cotangent": cotangent, "valid_slots": valid_slots, "ln1_gain": ln1_gain, "ln1_bias": ln1_bias, "qkv_weight": qkv_weight, "qv_bias": qv_bias, "out_weight": out_weight, "out_bias": out_bias, "ln2_gain": ln2_gain, "ln2_bias": ln2_bias, "fc1_weight": fc1_weight, "fc1_bias": fc1_bias, "fc2_weight": fc2_weight, "fc2_bias": fc2_bias}


@jax.custom_vjp
def low(v):
    return lax.optimization_barrier(v.astype(jnp.bfloat16)).astype(jnp.float32)

@jax.custom_vjp
def low_back(v):
    return v

def low_keep(v):
    return (low(v), None)

def low_pass(kept, grad):
    return (grad,)

def back_keep(v):
    return (v, None)

def back_low(kept, grad):
    return (low(grad),)
low.defvjp(low_keep, low_pass)
low_back.defvjp(back_keep, back_low)
highest = lax.Precision.HIGHEST
epsilon = 1e-05

def norm_rows(values, gain_vector, bias_vector):
    average = lax.optimization_barrier(jnp.mean(values, -1, keepdims=True))
    centered = values - average
    inverse = lax.rsqrt(lax.optimization_barrier(jnp.mean(centered * centered, -1, keepdims=True)) + epsilon)
    return centered * inverse * gain_vector + bias_vector

def round_both(values):
    return low(low_back(values))

def image_block(parameters, image_rows):
    gain_one, bias_one, qkv_full, pair_bias, out_full, bias_out, gain_two, bias_two, fc1_full, hidden_bias, fc2_full, bias_last = parameters
    normed_one = low(norm_rows(image_rows, gain_one, bias_one))
    projected = jnp.einsum('sd,kdc->ksc', normed_one, qkv_full, precision=highest)
    pair_flat = pair_bias.reshape(2, D)
    head_shape = (SEQ, HEADS, HD)
    queries = round_both(projected[0] + pair_flat[0]).reshape(head_shape)
    key_rows = round_both(projected[1]).reshape(head_shape)
    value_rows = round_both(projected[2] + pair_flat[1]).reshape(head_shape)
    scores = low_back(jnp.einsum('shd,thd->hst', queries, key_rows, precision=highest) / math.sqrt(HD))
    probabilities = low(jax.nn.softmax(scores, axis=-1))
    attended = round_both(jnp.einsum('hst,thd->shd', probabilities, value_rows, precision=highest).reshape(SEQ, D))
    branch = low_back(jnp.dot(attended, out_full, precision=highest))
    middle = image_rows + branch + bias_out
    normed_two = low(norm_rows(middle, gain_two, bias_two))
    up_proj = low_back(jnp.dot(normed_two, fc1_full, precision=highest) + hidden_bias.reshape(FF))
    activated = low(up_proj * jax.nn.sigmoid(1.702 * up_proj))
    mlp_out = low_back(jnp.dot(activated, fc2_full, precision=highest))
    return middle + mlp_out + bias_last

def forward(inputs_full, parameters):
    images = inputs_full.reshape(MICRO * SLOTS_ALL, SEQ, D)

    def one_image(image_rows):
        return image_block(parameters, image_rows)
    outputs = lax.map(jax.checkpoint(one_image), images)
    return outputs.reshape(inputs_full.shape)

def reference(inputs, cotangent, valid_slots, ln1_gain, ln1_bias, qkv_weight, qv_bias, out_weight, out_bias, ln2_gain, ln2_bias, fc1_weight, fc1_bias, fc2_weight, fc2_bias):
    parameters = tuple((weight_array.astype(jnp.float32) for weight_array in (ln1_gain, ln1_bias, qkv_weight, qv_bias, out_weight, out_bias, ln2_gain, ln2_bias, fc1_weight, fc1_bias, fc2_weight, fc2_bias)))
    output_rows, pullback = jax.vjp(forward, inputs.astype(jnp.float32), parameters)
    slot_weight = valid_slots.astype(jnp.float32)[:, :, None, None]
    input_grad, gradients = pullback(cotangent.astype(jnp.float32) * slot_weight)
    grad_ln1_gain, grad_ln1_bias, grad_qkv_weight, grad_qv_bias, grad_out_weight, grad_out_bias, grad_ln2_gain, grad_ln2_bias, grad_fc1_weight, grad_fc1_bias, grad_fc2_weight, grad_fc2_bias = gradients
    return (output_rows.astype(jnp.bfloat16), input_grad.astype(jnp.bfloat16), grad_ln1_gain, grad_ln1_bias, grad_qkv_weight, grad_qv_bias, grad_out_weight, grad_out_bias, grad_ln2_gain, grad_ln2_bias, grad_fc1_weight, grad_fc1_bias, grad_fc2_weight, grad_fc2_bias)
```

```python
import functools
import math

import jax
import jax.numpy as jnp
from jax import lax
from jax.experimental import pallas as pl
from jax.experimental.pallas import tpu as pltpu
from jax.sharding import PartitionSpec as P

MESH = pl.DeviceIdType.MESH
HD = 64
EPSILON = 1e-05
BF16 = jnp.bfloat16
F32 = jnp.float32
VMEM_LIMIT = 56 * 2**20
ORDERS = (("x", "y", "z"), ("y", "z", "x"), ("z", "x", "y"), ("x", "y", "z"))


def place():
    f, t = lax.axis_index("fsdp"), lax.axis_index("tp")
    return {
        "x": t // 2,
        "y": lax.rem(f // 2, 4),
        "z": (f // 8) * 2 + lax.rem(t, 2),
        "c": lax.rem(f, 2),
    }


def device_at(spot):
    return (
        (spot["z"] // 2) * 8 + spot["y"] * 2 + spot["c"],
        spot["x"] * 2 + lax.rem(spot["z"], 2),
    )


def shifted(spot, axis, by):
    return {**spot, axis: lax.rem(spot[axis] + by + 4, 4)}


def sibling(spot):
    return {**spot, "c": 1 - spot["c"]}


def greet(devices):
    barrier = pltpu.get_barrier_semaphore()
    for device in devices:
        pl.semaphore_signal(barrier, inc=1, device_id=device, device_id_type=MESH)
    pl.semaphore_wait(barrier, len(devices))


def greet_torus(spot):
    greet(
        [device_at(shifted(spot, axis, by)) for axis in "xyz" for by in (1, -1)]
        + [device_at(sibling(spot))]
    )


def view(ref, spot, full, core=None, rows=slice(None)):
    whole = slice(None)
    index = [
        whole if "x" in full else spot["x"],
        whole if "z" in full else lax.rem(spot["z"], 2),
        whole if "z" in full else spot["z"] // 2,
        whole if "y" in full else spot["y"],
    ]
    if core is not None:
        index.append(core)
    return ref.at[tuple(index) + (rows,)]


def gather_kernel(*refs):
    parts = len(ORDERS)
    ins, outs = refs[:parts], refs[parts : 2 * parts]
    local_sem, send_sem, recv_sem, sib_send, sib_recv = refs[2 * parts :]
    me = place()
    core = me["c"]
    greet_torus(me)
    other = device_at(sibling(me))
    sends = []

    def remote(src, dst, send, recv, device):
        copy = pltpu.make_async_remote_copy(
            src, dst, send, recv, device_id=device, device_id_type=MESH
        )
        copy.start()
        sends.append(copy)
        return copy

    shares = []

    def share(part, slot, piece):
        shares.append(
            remote(piece, piece, sib_send.at[part, slot], sib_recv.at[part, slot], other)
        )

    own = []
    for part in range(parts):
        copy = pltpu.make_async_copy(
            ins[part], view(outs[part], me, "", core), local_sem.at[part]
        )
        copy.start()
        own.append(copy)
    for part in range(parts):
        own[part].wait()
    for phase in range(3):
        near = {}
        for part in range(parts):
            order, out = ORDERS[part], outs[part]
            axis, full = order[phase], "".join(order[:phase])
            bundle = view(out, me, full, core)
            for way, by in enumerate((1, -1)):
                near[part, way] = remote(
                    bundle,
                    bundle,
                    send_sem.at[part, phase, way],
                    recv_sem.at[part, phase, way],
                    device_at(shifted(me, axis, by)),
                )
            if phase == 0:
                share(part, 0, bundle)
        far = {}
        for part in range(parts):
            order, out = ORDERS[part], outs[part]
            axis, full = order[phase], "".join(order[:phase])
            half = out.shape[-2] // 2
            for way, by in enumerate((1, -1)):
                near[part, way].wait_recv()
                piece = view(
                    out, shifted(me, axis, -by), full, core, pl.ds(way * half, half)
                )
                far[part, way] = remote(
                    piece,
                    piece,
                    send_sem.at[part, phase, 2 + way],
                    recv_sem.at[part, phase, 2 + way],
                    device_at(shifted(me, axis, by)),
                )
                share(part, 1 + 3 * phase + way, view(out, shifted(me, axis, -by), full, core))
        for part in range(parts):
            order, out = ORDERS[part], outs[part]
            axis, full = order[phase], "".join(order[:phase])
            for way in range(2):
                far[part, way].wait_recv()
            share(part, 3 + 3 * phase, view(out, shifted(me, axis, 2), full, core))
    for copy in sends:
        copy.wait_send()
    for copy in shares:
        copy.wait_recv()


def gather_weights(blocks):
    parts = len(blocks)
    return pl.pallas_call(
        gather_kernel,
        out_shape=[
            jax.ShapeDtypeStruct((4, 2, 2, 4, 2) + block.shape, block.dtype) for block in blocks
        ],
        in_specs=[pl.BlockSpec(memory_space=pl.ANY)] * parts,
        out_specs=[pl.BlockSpec(memory_space=pl.ANY)] * parts,
        scratch_shapes=[
            pltpu.SemaphoreType.DMA((parts,)),
            pltpu.SemaphoreType.DMA((parts, 3, 4)),
            pltpu.SemaphoreType.DMA((parts, 3, 4)),
            pltpu.SemaphoreType.DMA((parts, 10)),
            pltpu.SemaphoreType.DMA((parts, 10)),
        ],
        compiler_params=pltpu.CompilerParams(
            collective_id=0, has_side_effects=True, vmem_limit_bytes=VMEM_LIMIT
        ),
        name="gather_weights",
    )(*blocks)


def decode(number, spot, full):
    sizes = {"x": (4,), "z": (2, 2), "y": (4,)}
    at = {}
    for axis in "yzx":
        if axis in full:
            parts = []
            for size in reversed(sizes[axis]):
                parts.append(lax.rem(number, size))
                number = number // size
            at[axis] = tuple(reversed(parts))
    fixed = {"x": (spot["x"],), "z": (lax.rem(spot["z"], 2), spot["z"] // 2), "y": (spot["y"],)}
    index, inner = (), ()
    for axis in "xzy":
        index += at.get(axis, fixed[axis])
        inner += at.get(axis, ())
    return index, inner


def bundle_shape(full):
    sizes = {"x": (4,), "z": (2, 2), "y": (4,)}
    shape = ()
    for axis in "xzy":
        shape += sizes[axis] if axis in full else ()
    return shape


def scatter_kernel(*refs):
    parts = len(ORDERS)
    grads, outs = refs[:parts], refs[parts : 2 * parts]
    rest = refs[2 * parts :]
    accs, sibs = rest[:parts], rest[parts : 2 * parts]
    rest = rest[2 * parts :]
    nears = [rest[part * 3 : part * 3 + 3] for part in range(parts)]
    rest = rest[3 * parts :]
    fars = [rest[part * 3 : part * 3 + 3] for part in range(parts)]
    local_sem, sib_send, sib_recv, send_sem, recv_sem = rest[3 * parts :]
    me = place()
    core = me["c"]
    greet_torus(me)
    other = device_at(sibling(me))
    sends = []

    def remote(src, dst, send, recv, device):
        copy = pltpu.make_async_remote_copy(
            src, dst, send, recv, device_id=device, device_id_type=MESH
        )
        copy.start()
        sends.append(copy)
        return copy

    def add(part, spot, full, sources):
        acc = accs[part]
        count = math.prod(bundle_shape(full))

        def one(number, carry):
            index, inner = decode(number, spot, full)
            for first, rows, terms in sources:
                here = index + (pl.ds(first, rows),)
                total = acc[here].astype(F32)
                for ref, lead, base in terms:
                    place_in = index if lead is None else (lead,) + inner
                    total += ref[place_in + (pl.ds(base, rows),)].astype(F32)
                acc[here] = total.astype(acc.dtype)
            return carry

        lax.fori_loop(0, count, one, 0)

    distances = (2, 1, -1, 0)
    arrive = {}
    for slot, by in enumerate(distances):
        for part in range(parts):
            axis, full = ORDERS[part][2], "".join(ORDERS[part][:2])
            spot = shifted(me, axis, by)
            local = pltpu.make_async_copy(
                view(grads[part], spot, full, core),
                view(accs[part], spot, full),
                local_sem.at[part, slot],
            )
            local.start()
            share = remote(
                view(grads[part], spot, full, 1 - core),
                view(sibs[part], spot, full),
                sib_send.at[part, slot],
                sib_recv.at[part, slot],
                other,
            )
            arrive[part, slot] = (local, share)
    for phase in (2, 1, 0):
        copies = {}
        for slot, by in enumerate(distances):
            for part in range(parts):
                acc, near, far = accs[part], nears[part][phase], fars[part][phase]
                axis, full = ORDERS[part][phase], "".join(ORDERS[part][:phase])
                rows = acc.shape[-2]
                half = rows // 2
                spot = shifted(me, axis, by)
                first, second = [], []
                if phase == 2:
                    local, share = arrive[part, slot]
                    local.wait()
                    share.wait_recv()
                    first.append((sibs[part], None, 0))
                    second.append((sibs[part], None, half))
                if by == 1:
                    copies[part, 0].wait_recv()
                    first.append((far, 0, 0))
                if by == -1:
                    copies[part, 1].wait_recv()
                    second.append((far, 1, 0))
                if by == 0:
                    for way in range(2):
                        copies[part, 2 + way].wait_recv()
                        first.append((near, way, 0))
                        second.append((near, way, half))
                if phase == 0 and by == 0:
                    index, _ = decode(0, me, "")
                    outs[part][...] = (
                        acc[index].astype(F32) + near[0].astype(F32) + near[1].astype(F32)
                    )
                    continue
                sources = [
                    entry for entry in ((0, half, first), (half, half, second)) if entry[2]
                ]
                if sources:
                    add(part, spot, full, sources)
                if by == 2:
                    for way, step in enumerate((1, -1)):
                        copies[part, way] = remote(
                            view(acc, spot, full, None, pl.ds(way * half, half)),
                            far.at[way],
                            send_sem.at[part, phase, way],
                            recv_sem.at[part, phase, way],
                            device_at(shifted(me, axis, step)),
                        )
                if by in (1, -1):
                    way = 0 if by == 1 else 1
                    copies[part, 2 + way] = remote(
                        view(acc, spot, full),
                        near.at[way],
                        send_sem.at[part, phase, 2 + way],
                        recv_sem.at[part, phase, 2 + way],
                        device_at(shifted(me, axis, by)),
                    )
    for copy in sends:
        copy.wait_send()


def scatter_gradients(grads):
    parts = len(grads)
    blocks = [grad.shape[5:] for grad in grads]
    kinds = [grad.dtype for grad in grads]
    scratch = [pltpu.VMEM((4, 2, 2, 4) + b, k) for _ in range(2) for b, k in zip(blocks, kinds)]
    for pieces in (1, 2):
        for part in range(parts):
            rows, columns = blocks[part]
            for phase in range(3):
                lead = (2,) + bundle_shape(ORDERS[part][:phase])
                scratch.append(pltpu.VMEM(lead + (rows // pieces, columns), kinds[part]))
    return pl.pallas_call(
        scatter_kernel,
        out_shape=[jax.ShapeDtypeStruct(block, F32) for block in blocks],
        in_specs=[pl.BlockSpec(memory_space=pl.ANY)] * parts,
        out_specs=[pl.BlockSpec(memory_space=pltpu.VMEM)] * parts,
        scratch_shapes=scratch
        + [
            pltpu.SemaphoreType.DMA((parts, 4)),
            pltpu.SemaphoreType.DMA((parts, 4)),
            pltpu.SemaphoreType.DMA((parts, 4)),
            pltpu.SemaphoreType.DMA((parts, 3, 4)),
            pltpu.SemaphoreType.DMA((parts, 3, 4)),
        ],
        compiler_params=pltpu.CompilerParams(
            collective_id=1, has_side_effects=True, vmem_limit_bytes=VMEM_LIMIT
        ),
        name="scatter_gradients",
    )(*grads)


def exchange_kernel(in_ref, out_ref, local_sem, send_sem, recv_sem):
    f, t = lax.axis_index("fsdp"), lax.axis_index("tp")
    greet([(f, lax.rem(t + step, 8)) for step in range(1, 8)])
    own = pltpu.make_async_copy(in_ref.at[t], out_ref.at[t], local_sem)
    copies = []
    for step in (4, 5, 3, 7, 1, 6, 2):
        target = lax.rem(t + step, 8)
        copy = pltpu.make_async_remote_copy(
            in_ref.at[target],
            out_ref.at[t],
            send_sem.at[step],
            recv_sem.at[step],
            device_id=(f, target),
            device_id_type=MESH,
        )
        copy.start()
        copies.append(copy)
    own.start()
    own.wait()
    for copy in copies:
        copy.wait()


def exchange(slabs, collective_id):
    return pl.pallas_call(
        exchange_kernel,
        out_shape=jax.ShapeDtypeStruct(slabs.shape, slabs.dtype),
        in_specs=[pl.BlockSpec(memory_space=pl.ANY)],
        out_specs=pl.BlockSpec(memory_space=pl.ANY),
        scratch_shapes=[
            pltpu.SemaphoreType.DMA,
            pltpu.SemaphoreType.DMA((8,)),
            pltpu.SemaphoreType.DMA((8,)),
        ],
        compiler_params=pltpu.CompilerParams(
            collective_id=collective_id, has_side_effects=True
        ),
        name="exchange_%d" % slabs.shape[-1],
    )(slabs)


NN = (((1,), (0,)), ((), ()))
NT = (((1,), (1,)), ((), ()))
TN = (((0,), (0,)), ((), ()))


def mm(a, b, dims=NN):
    return lax.dot_general(a, b, dims, preferred_element_type=F32)


def plain(kernel, name, grid, in_specs, out_specs, out_shape, scratch=()):
    return pl.pallas_call(
        kernel,
        grid=grid,
        in_specs=in_specs,
        out_specs=out_specs,
        out_shape=out_shape,
        scratch_shapes=list(scratch),
        compiler_params=pltpu.CompilerParams(vmem_limit_bytes=VMEM_LIMIT),
        name=name,
    )


def project_kernel(rows_ref, weight_ref, bias_ref, out_ref):
    out_ref[0] = (mm(rows_ref[...], weight_ref[0]) + bias_ref[0]).astype(BF16)


def project(rows, weights, bias):
    count, width = rows.shape
    return plain(
        project_kernel,
        "project",
        (8,),
        [
            pl.BlockSpec((count, width), lambda t: (0, 0)),
            pl.BlockSpec((1, width, 384), lambda t: (t, 0, 0)),
            pl.BlockSpec((1, 1, 384), lambda t: (t, 0, 0)),
        ],
        pl.BlockSpec((1, count, 384), lambda t: (t, 0, 0)),
        jax.ShapeDtypeStruct((8, count, 384), BF16),
    )(rows, weights, bias)


SCALE = 1.0 / math.sqrt(HD)


def softmax_columns(key_rows, queries):
    scores = mm(key_rows, queries, NT)
    shifted_scores = scores - jnp.max(scores, 0, keepdims=True)
    powers = jnp.exp(shifted_scores * SCALE)
    return powers * (1.0 / jnp.sum(powers, 0, keepdims=True))


def attend_kernel(qkv_ref, out_ref):
    queries, key_rows, value_rows = (qkv_ref[0, :, 128 * i : 128 * i + 128] for i in range(3))
    lane = lax.broadcasted_iota(jnp.int32, (1, 128), 1)
    halves = []
    for head in range(2):
        mine = jnp.where(lane // HD == head, 1.0, 0.0).astype(BF16)
        probs = softmax_columns(key_rows, queries * mine).astype(BF16)
        halves.append(mm(probs, value_rows, TN))
    out_ref[0] = jnp.where(lane < HD, halves[0], halves[1]).astype(BF16)


def attend(qkv):
    images, seq, _ = qkv.shape
    return plain(
        attend_kernel,
        "attend",
        (images,),
        [pl.BlockSpec((1, seq, 384), lambda m: (m, 0, 0))],
        pl.BlockSpec((1, seq, 128), lambda m: (m, 0, 0)),
        jax.ShapeDtypeStruct((images, seq, 128), BF16),
    )(qkv)


def attend_back_kernel(qkv_ref, grad_ref, out_ref):
    queries, key_rows, value_rows = (qkv_ref[0, :, 128 * i : 128 * i + 128] for i in range(3))
    grads = grad_ref[0]
    lane = lax.broadcasted_iota(jnp.int32, (1, 128), 1)
    results = []
    for head in range(2):
        mine = jnp.where(lane // HD == head, 1.0, 0.0).astype(BF16)
        own_queries, own_grads = queries * mine, grads * mine
        probs = softmax_columns(key_rows, own_queries)
        d_probs = mm(value_rows, own_grads, NT)
        inner = jnp.sum(probs * d_probs, 0, keepdims=True)
        d_scores = (probs * (d_probs - inner)).astype(BF16)
        results.append(
            (
                mm(d_scores, key_rows, TN) * SCALE,
                mm(d_scores, queries) * SCALE,
                mm(probs.astype(BF16), grads),
            )
        )
    for i in range(3):
        out_ref[0, :, 128 * i : 128 * i + 128] = jnp.where(
            lane < HD, results[0][i], results[1][i]
        ).astype(BF16)


def attend_back(qkv, grads):
    images, seq, _ = qkv.shape
    return plain(
        attend_back_kernel,
        "attend_back",
        (images,),
        [
            pl.BlockSpec((1, seq, 384), lambda m: (m, 0, 0)),
            pl.BlockSpec((1, seq, 128), lambda m: (m, 0, 0)),
        ],
        pl.BlockSpec((1, seq, 384), lambda m: (m, 0, 0)),
        jax.ShapeDtypeStruct((images, seq, 384), BF16),
    )(qkv, grads)


def feed_forward_kernel(
    rows_ref,
    grads_ref,
    rows_t_ref,
    grads_t_ref,
    up_ref,
    down_ref,
    bias_ref,
    out_ref,
    back_ref,
    grad_up_ref,
    grad_down_ref,
    grad_bias_ref,
):
    step = pl.program_id(0)
    up_weight, down_weight = up_ref[0], down_ref[0]
    up_proj = mm(rows_ref[...], up_weight) + bias_ref[0]
    gate = jax.nn.sigmoid(1.702 * up_proj)
    activated = (up_proj * gate).astype(BF16)
    d_act = mm(grads_ref[...], down_weight)
    d_up_wide = d_act * (gate + 1.702 * up_proj * gate * (1.0 - gate))
    d_up = d_up_wide.astype(BF16)
    grad_bias_ref[0] = jnp.sum(d_up.astype(F32), 0, keepdims=True)
    forward = mm(activated, down_weight, NT)
    backward = mm(d_up, up_weight, NT)

    @pl.when(step == 0)
    def _():
        out_ref[...] = forward
        back_ref[...] = backward

    @pl.when(step > 0)
    def _():
        out_ref[...] += forward
        back_ref[...] += backward

    grad_up_ref[0] = mm(rows_t_ref[...], d_up).astype(BF16)
    grad_down_ref[0] = mm(grads_t_ref[...], activated).astype(BF16)


def feed_forward(rows, grads, up_weights, down_weights, bias):
    count, width = rows.shape
    hidden = up_weights.shape[2]
    whole = pl.BlockSpec((count, width), lambda t: (0, 0))
    turned = pl.BlockSpec((width, count), lambda t: (0, 0))
    slab = pl.BlockSpec((1, width, hidden), lambda t: (t, 0, 0))
    line = pl.BlockSpec((1, 1, hidden), lambda t: (t, 0, 0))
    return plain(
        feed_forward_kernel,
        "feed_forward",
        (8,),
        [whole, whole, turned, turned, slab, slab, line],
        [whole, whole, slab, slab, line],
        [
            jax.ShapeDtypeStruct((count, width), F32),
            jax.ShapeDtypeStruct((count, width), F32),
            jax.ShapeDtypeStruct((8, width, hidden), BF16),
            jax.ShapeDtypeStruct((8, width, hidden), BF16),
            jax.ShapeDtypeStruct((8, 1, hidden), F32),
        ],
    )(rows, grads, rows.T, grads.T, up_weights, down_weights, bias)


def project_back_kernel(
    grads_ref, attended_ref, weight_ref, rows_t_ref, middle_t_ref, back_ref, grad_ref
):
    step = pl.program_id(0)
    grads = grads_ref[0]
    backward = mm(grads, weight_ref[0], NT)

    @pl.when(step == 0)
    def _():
        back_ref[...] = backward

    @pl.when(step > 0)
    def _():
        back_ref[...] += backward

    grad_ref[0, :, :384] = mm(rows_t_ref[...], grads).astype(BF16)
    grad_ref[0, :, 384:] = mm(middle_t_ref[...], attended_ref[0]).astype(BF16)


def project_back(grads, attended, weights, rows, middle):
    count, width = rows.shape
    turned = pl.BlockSpec((width, count), lambda t: (0, 0))
    return plain(
        project_back_kernel,
        "project_back",
        (8,),
        [
            pl.BlockSpec((1, count, 384), lambda t: (t, 0, 0)),
            pl.BlockSpec((1, count, 128), lambda t: (t, 0, 0)),
            pl.BlockSpec((1, width, 384), lambda t: (t, 0, 0)),
            turned,
            turned,
        ],
        [
            pl.BlockSpec((count, width), lambda t: (0, 0)),
            pl.BlockSpec((1, width, 512), lambda t: (t, 0, 0)),
        ],
        [
            jax.ShapeDtypeStruct((count, width), F32),
            jax.ShapeDtypeStruct((8, width, 512), BF16),
        ],
    )(grads, attended, weights, rows.T, middle.T)


def norm_stats(values):
    average = jnp.mean(values, -1, keepdims=True)
    centered = values - average
    inverse = lax.rsqrt(jnp.mean(centered * centered, -1, keepdims=True) + EPSILON)
    return (centered * inverse, inverse)


def norm_back(upstream, normed, inverse, gain_vector):
    scaled = upstream * gain_vector
    return inverse * (
        scaled
        - jnp.mean(scaled, -1, keepdims=True)
        - normed * jnp.mean(scaled * normed, -1, keepdims=True)
    )


def per_device(
    inputs,
    cotangent,
    valid_slots,
    ln1_gain,
    ln1_bias,
    qkv_weight,
    qv_bias,
    out_weight,
    out_bias,
    ln2_gain,
    ln2_bias,
    fc1_weight,
    fc1_bias,
    fc2_weight,
    fc2_bias,
):
    micro, _, local_seq, width = inputs.shape
    tokens = micro * local_seq
    padded = -(-tokens // 16) * 16

    def pad(rows):
        return jnp.pad(rows, ((0, padded - tokens), (0, 0)))

    attention_block = jnp.concatenate(
        [qkv_weight[0], qkv_weight[1], qkv_weight[2], out_weight.T], axis=1
    )
    small = jnp.concatenate(
        [ln1_gain, ln1_bias, out_bias, ln2_gain, ln2_bias, fc2_bias]
        + [qv_bias.reshape(-1), fc1_bias.reshape(-1)]
    )
    small = jnp.pad(small.reshape(1, 96), ((0, 15), (0, 32)))
    gathered = gather_weights((attention_block, fc1_weight, fc2_weight.T, small))
    attention_w, up_w, down_w = (entry.reshape(8, width, 512) for entry in gathered[:3])
    vectors = gathered[3].reshape(8, 16, 16, 128)[:, :, 0, :96].astype(F32)
    gain_one, bias_one, bias_out, gain_two, bias_two, bias_last = (
        vectors[:, :, :48].reshape(8, 16, 6, 8).transpose(2, 1, 0, 3).reshape(6, width)
    )
    pair_bias = vectors[:, :, 48:64].reshape(8, 16, 2, 2, 4).transpose(2, 0, 3, 1, 4)
    pair_bias = pair_bias.reshape(2, 8, 1, 128)
    hidden_bias = vectors[:, :, 64:].reshape(8, 16, 8, 4).transpose(0, 2, 1, 3).reshape(8, 1, 512)
    project_bias = jnp.concatenate(
        [pair_bias[0], jnp.zeros((8, 1, 128), F32), pair_bias[1]], axis=-1
    )

    def to_images(slabs):
        columns = slabs.shape[-1]
        rows = slabs[:, :tokens].reshape(8, micro, local_seq, columns)
        return rows.transpose(1, 0, 2, 3).reshape(micro, 8 * local_seq, columns)

    def to_slabs(images):
        columns = images.shape[-1]
        rows = images.reshape(micro, 8, local_seq, columns).transpose(1, 0, 2, 3)
        rows = rows.reshape(8, tokens, columns)
        return jnp.pad(rows, ((0, 0), (0, padded - tokens), (0, 0)))

    block_rows = inputs.reshape(tokens, width).astype(F32)
    normed_one, inverse_one = norm_stats(block_rows)
    low_one = pad((normed_one * gain_one + bias_one).astype(BF16))
    qkv = to_images(exchange(project(low_one, attention_w, project_bias), 2))
    attended = exchange(to_slabs(attend(qkv)), 3)
    out_w = attention_w[:, :, 384:]
    branch = jnp.einsum("tnc,tdc->nd", attended, out_w, preferred_element_type=F32)[:tokens]
    middle = block_rows + branch + bias_out
    normed_two, inverse_two = norm_stats(middle)
    low_two = pad((normed_two * gain_two + bias_two).astype(BF16))
    slot_weight = valid_slots.astype(F32).reshape(micro, 1, 1)
    upstream = (cotangent.reshape(micro, local_seq, width).astype(F32) * slot_weight).reshape(
        tokens, width
    )
    upstream_low = pad(upstream.astype(BF16))
    mlp_out, d_norm_two, grad_up, grad_down, grad_hidden = feed_forward(
        low_two, upstream_low, up_w, down_w, hidden_bias
    )
    mlp_out, d_norm_two = mlp_out[:tokens], d_norm_two[:tokens]
    result = (middle + mlp_out + bias_last).astype(BF16)
    d_middle = upstream + norm_back(d_norm_two, normed_two, inverse_two, gain_two)
    middle_low = pad(d_middle.astype(BF16))
    d_attended = jnp.einsum("nd,tdc->tnc", middle_low, out_w, preferred_element_type=F32)
    d_attended = to_images(exchange(d_attended.astype(BF16), 3))
    d_project = exchange(to_slabs(attend_back(qkv, d_attended)), 2)
    d_norm_one, grad_attention = project_back(
        d_project, attended, attention_w, low_one, middle_low
    )
    d_norm_one = d_norm_one[:tokens]
    grad_rows = d_middle + norm_back(d_norm_one, normed_one, inverse_one, gain_one)
    pair_sums = jnp.sum(d_project.astype(F32), 1)
    pair_sums = jnp.stack([pair_sums[:, :128], pair_sums[:, 256:]])
    vector_sums = jnp.stack(
        [
            jnp.sum(d_norm_one * normed_one, 0),
            jnp.sum(d_norm_one, 0),
            jnp.sum(d_middle, 0),
            jnp.sum(d_norm_two * normed_two, 0),
            jnp.sum(d_norm_two, 0),
            jnp.sum(upstream, 0),
        ]
    )
    small_grads = jnp.concatenate(
        [
            vector_sums.reshape(6, 16, 8, 8).transpose(2, 1, 0, 3).reshape(8, 16, 48),
            pair_sums.reshape(2, 8, 2, 16, 4).transpose(1, 3, 0, 2, 4).reshape(8, 16, 16),
            grad_hidden.reshape(8, 8, 16, 4).transpose(0, 2, 1, 3).reshape(8, 16, 32),
        ],
        axis=-1,
    )
    small_grads = jnp.pad(small_grads[:, :, None], ((0, 0), (0, 0), (0, 15), (0, 32)))
    lead = (4, 2, 2, 4, 2)
    sums = scatter_gradients(
        (
            grad_attention.reshape(lead + (64, 512)),
            grad_up.reshape(lead + (64, 512)),
            grad_down.reshape(lead + (64, 512)),
            small_grads.reshape(lead + (16, 128)),
        )
    )
    own_attention, own_up, own_down, own_small = sums
    own_small = own_small[0]
    vector_grads = own_small[:48].reshape(6, 8)
    return (
        result.reshape(inputs.shape),
        grad_rows.astype(BF16).reshape(inputs.shape),
        vector_grads[0],
        vector_grads[1],
        jnp.stack([own_attention[:, 128 * i : 128 * i + 128] for i in range(3)]),
        own_small[48:64].reshape(2, 2, 4),
        own_attention[:, 384:].T,
        vector_grads[2],
        vector_grads[3],
        vector_grads[4],
        own_up,
        own_small[64:96].reshape(8, 4),
        own_down.T,
        vector_grads[5],
    )


def solution(mesh):
    in_specs = (
        P(None, "fsdp", "tp", None),
        P(None, "fsdp", "tp", None),
        P(None, "fsdp"),
        P(("fsdp", "tp")),
        P(("fsdp", "tp")),
        P(None, "fsdp", "tp"),
        P(None, "tp", "fsdp"),
        P("tp", "fsdp"),
        P(("fsdp", "tp")),
        P(("fsdp", "tp")),
        P(("fsdp", "tp")),
        P("fsdp", "tp"),
        P("tp", "fsdp"),
        P("tp", "fsdp"),
        P(("fsdp", "tp")),
    )
    out_specs = (
        P(None, "fsdp", "tp", None),
        P(None, "fsdp", "tp", None),
        P(("fsdp", "tp")),
        P(("fsdp", "tp")),
        P(None, "fsdp", "tp"),
        P(None, "tp", "fsdp"),
        P("tp", "fsdp"),
        P(("fsdp", "tp")),
        P(("fsdp", "tp")),
        P(("fsdp", "tp")),
        P("fsdp", "tp"),
        P("tp", "fsdp"),
        P("tp", "fsdp"),
        P(("fsdp", "tp")),
    )
    return jax.shard_map(
        per_device, mesh=mesh, in_specs=in_specs, out_specs=out_specs, check_vma=False
    )
```

```python
import functools
import math

import jax
import jax.numpy as jnp
from jax import lax
from jax.experimental import pallas as pl
from jax.experimental.pallas import tpu as pltpu
from jax.sharding import PartitionSpec as P

MESH = pl.DeviceIdType.MESH
HD = 64
SCALE = 1.0 / math.sqrt(HD)
EPSILON = 1e-05
BF16 = jnp.bfloat16
F32 = jnp.float32
VMEM_LIMIT = 62 * 2**20
MICRO, GROUP = 3, 8
ORDERS = (("x", "y", "z"), ("y", "z", "x"), ("z", "x", "y"))
SIZES = {"x": (4,), "z": (2, 2), "y": (4,)}
LEAD = (4, 2, 2, 4, 2)
STEPS = (1, -1, 2)
NN = (((1,), (0,)), ((), ()))
NT = (((1,), (1,)), ((), ()))
TN = (((0,), (0,)), ((), ()))


def mm(a, b, dims=NN):
    return lax.dot_general(a, b, dims, preferred_element_type=F32)


def place():
    f, t = lax.axis_index("fsdp"), lax.axis_index("tp")
    return {
        "x": t // 2,
        "y": lax.rem(f // 2, 4),
        "z": (f // 8) * 2 + lax.rem(t, 2),
        "c": lax.rem(f, 2),
    }


def device_at(spot):
    return (
        (spot["z"] // 2) * 8 + spot["y"] * 2 + spot["c"],
        spot["x"] * 2 + lax.rem(spot["z"], 2),
    )


def shifted(spot, axis, by):
    return {**spot, axis: lax.rem(spot[axis] + by + 4, 4)}


def sibling(spot):
    return {**spot, "c": 1 - spot["c"]}


def greet(me):
    f, t = lax.axis_index("fsdp"), lax.axis_index("tp")
    devices = [(f, lax.rem(t + step, GROUP)) for step in range(1, GROUP)]
    devices += [device_at(shifted(me, "y", by)) for by in STEPS]
    devices += [device_at(shifted(me, "z", 2))]
    devices += [device_at(shifted(me, "z", 2 * lax.rem(me["z"], 2) - 1))]
    devices += [device_at(sibling(me))]
    barrier = pltpu.get_barrier_semaphore()
    for device in devices:
        pl.semaphore_signal(barrier, inc=1, device_id=device, device_id_type=MESH)
    pl.semaphore_wait(barrier, len(devices))


def view(ref, spot, full, core=None, rows=slice(None)):
    whole = slice(None)
    index = [
        whole if "x" in full else spot["x"],
        whole if "z" in full else lax.rem(spot["z"], 2),
        whole if "z" in full else spot["z"] // 2,
        whole if "y" in full else spot["y"],
    ]
    if core is not None:
        index.append(core)
    return ref.at[tuple(index) + (rows,)]


def decode(number, spot, full):
    at = {}
    for axis in "yzx":
        if axis in full:
            parts = []
            for size in reversed(SIZES[axis]):
                parts.append(lax.rem(number, size))
                number = number // size
            at[axis] = tuple(reversed(parts))
    fixed = {"x": (spot["x"],), "z": (lax.rem(spot["z"], 2), spot["z"] // 2), "y": (spot["y"],)}
    index, inner = (), ()
    for axis in "xzy":
        index += at.get(axis, fixed[axis])
        inner += at.get(axis, ())
    return index, inner


def bundle_shape(full):
    shape = ()
    for axis in "xzy":
        shape += SIZES[axis] if axis in full else ()
    return shape


class Copies:
    def __init__(self, send, recv):
        self.send, self.recv = send, recv
        self.made = {}

    def start(self, name, src, dst, device):
        slot = len(self.made)
        self.made[name] = pltpu.make_async_remote_copy(
            src,
            dst,
            self.send.at[slot],
            self.recv.at[slot],
            device_id=device,
            device_id_type=MESH,
        )
        self.made[name].start()

    def arrived(self, name):
        self.made[name].wait_recv()

    def sent(self):
        for copy in self.made.values():
            copy.wait_send()


class Gather:
    slots = 38

    def __init__(self, me, order, block, out, send, recv, local):
        self.me, self.order, self.block, self.out = me, order, block, out
        self.copies = Copies(send, recv)
        self.local = local
        self.core = me["c"]
        self.half = out.shape[-2] // 2

    def piece(self, spot, full, rows=slice(None)):
        return view(self.out, spot, full, self.core, rows)

    def spread(self, name, spot, full, axis, by, rows=slice(None)):
        piece = self.piece(spot, full, rows)
        target = shifted(self.me, axis, by)
        self.copies.start(name, piece, piece, device_at(target))

    def share(self, name, spot, full):
        piece = self.piece(spot, full)
        self.copies.start(name, piece, piece, device_at(sibling(self.me)))

    def own(self):
        return pltpu.make_async_copy(
            self.block, view(self.out, self.me, "", self.core), self.local
        )

    def first(self):
        me, axis = self.me, self.order[0]
        self.own().start()
        for by in STEPS:
            target = shifted(me, axis, by)
            self.copies.start(
                ("first", by), self.block, self.piece(me, ""), device_at(target)
            )

    def second(self):
        full, axis = self.order[0], self.order[1]
        self.own().wait()
        for by in STEPS:
            self.copies.arrived(("first", by))
        for by in STEPS:
            self.spread(("second", by), self.me, full, axis, by)
        self.third(0)

    def third(self, group):
        full, axis = self.order[0], self.order[2]
        spot = self.spot(group)
        if group:
            self.copies.arrived(("second", STEPS[group - 1]))
        for by in (1, -1):
            self.spread(("near", group, by), spot, full, axis, by)
        self.share(("share", group), spot, full)

    def spot(self, group):
        return self.me if group == 0 else shifted(self.me, self.order[1], -STEPS[group - 1])

    def thirds(self):
        for group in (1, 2, 3):
            self.third(group)

    def far(self, groups=(0, 1, 2, 3)):
        full, axis = self.order[0], self.order[2]
        for group in groups:
            for way, by in enumerate((1, -1)):
                spot = shifted(self.spot(group), axis, -by)
                self.copies.arrived(("near", group, by))
                rows = pl.ds(way * self.half, self.half)
                self.spread(("far", group, by), spot, full, axis, by, rows)
                self.share(("share near", group, by), spot, full)

    def last(self):
        full, axis = self.order[0], self.order[2]
        for group in range(4):
            for by in (1, -1):
                self.copies.arrived(("far", group, by))
            self.share(("share far", group), shifted(self.spot(group), axis, 2), full)

    def done(self):
        for group in range(4):
            self.copies.arrived(("share", group))
            self.copies.arrived(("share near", group, 1))
            self.copies.arrived(("share near", group, -1))
            self.copies.arrived(("share far", group))

    def sent(self):
        self.copies.sent()


class Reduce:
    slots = 14

    def __init__(self, me, order, source, acc, sib, near, far, mid, tail, out, send, recv, local):
        self.me, self.order, self.source, self.acc, self.sib = me, order, source, acc, sib
        self.nears, self.fars, self.mid, self.tail, self.out = near, far, mid, tail, out
        self.copies = Copies(send, recv)
        self.local = local
        self.core = me["c"]
        self.half = acc.shape[-2] // 2
        self.inside = source is acc
        self.full = "".join(order[:2])

    def mine(self, spot, full, rows=slice(None)):
        return view(self.acc, spot, full, self.core if self.inside else None, rows)

    def chunk(self, by):
        return shifted(self.me, self.order[2], by)

    def fetch(self, slot, by):
        spot = self.chunk(by)
        return pltpu.make_async_copy(
            view(self.source, spot, self.full, self.core),
            view(self.acc, spot, self.full),
            self.local.at[slot],
        )

    def begin(self):
        for slot, by in enumerate((2, 1, -1, 0)):
            spot = self.chunk(by)
            if not self.inside:
                self.fetch(slot, by).start()
            self.copies.start(
                ("share", by),
                view(self.source, spot, self.full, 1 - self.core),
                view(self.sib, spot, self.full),
                device_at(sibling(self.me)),
            )

    def ready(self, slot, by):
        if not self.inside:
            self.fetch(slot, by).wait()
        self.copies.arrived(("share", by))

    def add(self, spot, full, sources, out=None):
        acc = self.acc
        count = math.prod(bundle_shape(full))

        def one(number, carry):
            index, inner = decode(number, spot, full)
            spot_in = index + ((self.core,) if self.inside else ())
            for first, rows, terms in sources:
                here = spot_in + (pl.ds(first, rows),)
                total = acc[here]
                if len(terms) > 1:
                    total = total.astype(F32)
                for ref, lead, base in terms:
                    place_in = index if lead is None else (lead,) + inner
                    term = ref[place_in + (pl.ds(base, rows),)]
                    total += term.astype(total.dtype)
                acc[here] = total.astype(acc.dtype)
            return carry

        if count == 1:
            one(0, 0)
        else:
            lax.fori_loop(0, count, one, 0)

    def stage_far(self):
        half = self.half
        spot = self.chunk(2)
        self.ready(0, 2)
        self.add(spot, self.full, [(0, 2 * half, [(self.sib, None, 0)])])
        for way, by in enumerate((1, -1)):
            target = shifted(self.me, self.order[2], by)
            rows = pl.ds(way * half, half)
            self.copies.start(
                ("far", by),
                self.mine(spot, self.full, rows),
                self.fars.at[way],
                device_at(target),
            )

    def stage_near(self):
        half = self.half
        for way, by in enumerate((1, -1)):
            spot = self.chunk(by)
            self.ready(1 + way, by)
            self.copies.arrived(("far", by))
            with_far = [(self.sib, None, way * half), (self.fars, way, 0)]
            without = [(self.sib, None, (1 - way) * half)]
            self.add(
                spot, self.full, [(way * half, half, with_far), ((1 - way) * half, half, without)]
            )
            self.copies.start(
                ("near", by),
                self.mine(spot, self.full),
                self.nears.at[way],
                device_at(spot),
            )

    def stage_mid(self):
        half, axis, full = self.half, self.order[1], self.order[0]
        self.ready(3, 0)
        self.copies.arrived(("near", 1))
        self.copies.arrived(("near", -1))
        terms = [(self.sib, None, 0), (self.nears, 0, 0), (self.nears, 1, 0)]
        self.add(self.me, self.full, [(0, 2 * half, terms)])
        for number, by in enumerate(STEPS):
            spot = shifted(self.me, axis, by)
            self.copies.start(
                ("mid", by),
                self.mine(spot, full),
                self.mid.at[number],
                device_at(spot),
            )

    def stage_tail(self):
        half, axis, full = self.half, self.order[0], self.order[0]
        for by in STEPS:
            self.copies.arrived(("mid", by))
        terms = [(self.mid, number, 0) for number in range(3)]
        self.add(self.me, full, [(0, 2 * half, terms)])
        for number, by in enumerate(STEPS):
            spot = shifted(self.me, axis, by)
            self.copies.start(
                ("tail", by),
                self.mine(spot, ""),
                self.tail.at[number],
                device_at(spot),
            )

    def stage_out(self):
        for by in STEPS:
            self.copies.arrived(("tail", by))
        index, _ = decode(0, self.me, "")
        index += (self.core,) if self.inside else ()
        total = self.acc[index].astype(F32)
        for number in range(3):
            total += self.tail[number].astype(F32)
        self.out[...] = total

    def sent(self):
        self.copies.sent()


def reduce_scratch(order, lanes, dtype, source_inside):
    full = bundle_shape(order[:2])
    kinds = [] if source_inside else [pltpu.VMEM((4, 2, 2, 4, 64, lanes), dtype)]
    return kinds + [
        pltpu.VMEM((4, 2, 2, 4, 64, lanes), dtype),
        pltpu.VMEM((2,) + full + (64, lanes), dtype),
        pltpu.VMEM((2,) + full + (32, lanes), dtype),
        pltpu.VMEM((3,) + bundle_shape(order[:1]) + (64, lanes), dtype),
        pltpu.VMEM((3, 64, lanes), dtype),
    ]


def norm_stats(values):
    average = jnp.mean(values, -1, keepdims=True)
    centered = values - average
    inverse = lax.rsqrt(jnp.mean(centered * centered, -1, keepdims=True) + EPSILON)
    return (centered * inverse, inverse)


def norm_back(upstream, normed, inverse, gain_vector):
    scaled = upstream * gain_vector
    return inverse * (
        scaled
        - jnp.mean(scaled, -1, keepdims=True)
        - normed * jnp.mean(scaled * normed, -1, keepdims=True)
    )


def softmax_columns(key_rows, queries, hidden):
    scores = mm(key_rows, queries, NT) + hidden
    powers = jnp.exp((scores - jnp.max(scores, 0, keepdims=True)) * SCALE)
    return powers * (1.0 / jnp.sum(powers, 0, keepdims=True))


def hidden_rows(seq, slot, tokens):
    row = lax.broadcasted_iota(jnp.int32, (seq, 1), 0)
    return jnp.where(lax.rem(row, slot) < tokens, 0.0, -1e30)


def head_lanes(head):
    lane = lax.broadcasted_iota(jnp.int32, (1, 128), 1)
    return jnp.where(lane // HD == head, 1.0, 0.0).astype(BF16)


def thirds(rows):
    return [rows[:, 128 * i : 128 * i + 128] for i in range(3)]


def attend(rows, hidden):
    queries, key_rows, value_rows = thirds(rows)

    def one_head(head, before):
        mine = head_lanes(head)
        probs = softmax_columns(key_rows, queries * mine, hidden).astype(BF16)
        return before + mm(probs, value_rows * mine, TN)

    return lax.fori_loop(0, 2, one_head, jnp.zeros(queries.shape, F32)).astype(BF16)


def attend_back(rows, grads, hidden):
    queries, key_rows, value_rows = thirds(rows)

    def one_head(head, before):
        mine = head_lanes(head)
        own_grads, own_queries = grads * mine, queries * mine
        probs = softmax_columns(key_rows, own_queries, hidden)
        d_probs = mm(value_rows, own_grads, NT)
        inner = jnp.sum(probs * d_probs, 0, keepdims=True)
        d_scores = (probs * (d_probs - inner)).astype(BF16)
        return (
            before[0] + mm(d_scores, key_rows * mine, TN),
            before[1] + mm(d_scores, own_queries),
            before[2] + mm(probs.astype(BF16), own_grads),
        )

    zero = jnp.zeros(queries.shape, F32)
    d_queries, d_keys, d_values = lax.fori_loop(0, 2, one_head, (zero, zero, zero))
    return [
        (d_queries * SCALE).astype(BF16),
        (d_keys * SCALE).astype(BF16),
        d_values.astype(BF16),
    ]


def padded_rows(ref, target):
    micro, tokens, width = ref.shape
    for m in range(micro):
        target[m, :tokens] = ref[m].astype(F32)
        target[m, tokens:] = jnp.zeros((target.shape[1] - tokens, width), F32)


def blocks_of(ref, index):
    value = ref[index // 2, lax.rem(index, 2)]
    return value.reshape(-1, value.shape[-1])


def forward_kernel(*refs):
    (
        x_ref,
        qkv_in,
        wide_1,
        wide_2,
        wide_3,
        small_in,
        low_out,
        images_out,
        attended_out,
        vectors_out,
        hidden_out,
        qkv_out,
        wide_out_1,
        wide_out_2,
        wide_out_3,
        rows,
        wq,
        wk,
        wv,
        small,
        bias,
        low,
        outbox,
        images,
        attended_box,
        attended,
        local_sem,
        gather_send,
        gather_recv,
        send_sem,
        recv_sem,
        back_send,
        back_recv,
        store_sem,
    ) = refs
    me = place()
    f, t = lax.axis_index("fsdp"), lax.axis_index("tp")
    greet(me)
    heads = [wq, wk, wv]
    narrow = [
        Gather(
            me,
            ORDERS[i],
            qkv_in.at[i],
            heads[i],
            gather_send.at[i],
            gather_recv.at[i],
            local_sem.at[i],
        )
        for i in range(3)
    ]
    vector = Gather(
        me, ORDERS[0], small_in, small, gather_send.at[3], gather_recv.at[3], local_sem.at[3]
    )
    wide = [
        Gather(
            me,
            ORDERS[i],
            (wide_1, wide_2, wide_3)[i],
            (wide_out_1, wide_out_2, wide_out_3)[i],
            gather_send.at[4 + i],
            gather_recv.at[4 + i],
            local_sem.at[4 + i],
        )
        for i in range(3)
    ]
    early = [vector] + narrow
    for part in early:
        part.first()
    padded_rows(x_ref, rows)
    values = rows[...].reshape(-1, rows.shape[-1])
    normed, _ = norm_stats(values)
    for part in early:
        part.second()
    for part in early:
        part.thirds()
    for part in wide:
        part.first()
    for part in early:
        part.far()
    for part in wide:
        part.second()
    vector.last()
    vector.done()
    table = jnp.sum(small[...].reshape(128, 32, 128).astype(F32), 1).astype(BF16)
    lane = lax.broadcasted_iota(jnp.int32, (128, 1024), 0)
    column = lax.broadcasted_iota(jnp.int32, (128, 1024), 1)
    row = lane
    owner = jnp.where(lax.rem(row, 16) * 8 + row // 16 == column // 8, 1.0, 0.0)
    for v in range(6):
        pick = jnp.where(lane == v * 8 + lax.rem(column, 8), 1.0, 0.0).astype(BF16)
        vectors_out[v : v + 1, :] = jnp.sum(mm(table, pick) * owner, 0, keepdims=True)
    vectors_out[6:8, :] = jnp.zeros((2, 1024), F32)

    def spread_bias(width, first):
        lane = lax.broadcasted_iota(jnp.int32, (128, width), 0)
        column = lax.broadcasted_iota(jnp.int32, (128, width), 1)
        pick = lane == first + (column // 64) * 4 + lax.rem(column, 4)
        owner = lax.rem(lane, 16) == lax.rem(column, 64) // 4
        values = mm(table, jnp.where(pick, 1.0, 0.0).astype(BF16))
        return jnp.sum(jnp.where(owner, values, 0.0).reshape(8, 16, width), 1)

    hidden_out[...] = spread_bias(512, 64)
    query_bias, value_bias = spread_bias(128, 48), spread_bias(128, 56)
    for i in range(8):
        bias[i, :, 0:128] = query_bias[i : i + 1]
        bias[i, :, 128:256] = jnp.zeros((1, 128), F32)
        bias[i, :, 256:384] = value_bias[i : i + 1]
    low[...] = (normed * vectors_out[0:1, :] + vectors_out[1:2, :]).astype(BF16)
    for part in narrow:
        part.last()
    for part in wide:
        part.thirds()
    for part in narrow:
        part.done()

    def letter(k):
        target = lax.rem(t + k + 1, GROUP)
        return pltpu.make_async_remote_copy(
            outbox.at[target],
            images.at[t],
            send_sem.at[k],
            recv_sem.at[k],
            device_id=(f, target),
            device_id_type=MESH,
        )

    def project(k, carry):
        target = lax.rem(t + k + 1, GROUP)
        weights = jnp.concatenate([blocks_of(w, target) for w in heads], axis=1)
        result = (mm(low[...], weights) + bias[target]).astype(BF16)
        outbox[target] = result.reshape(outbox.shape[1:])

        @pl.when(k < GROUP - 1)
        def _():
            letter(k).start()

        return carry

    lax.fori_loop(0, GROUP, project, 0)
    stores = [
        pltpu.make_async_copy(heads[i], qkv_out.at[i], store_sem.at[i]) for i in range(3)
    ] + [pltpu.make_async_copy(low, low_out, store_sem.at[3])]
    for store in stores:
        store.start()
    own = pltpu.make_async_copy(outbox.at[t], images.at[t], local_sem.at[7])
    own.start()
    own.wait()
    for part in wide:
        part.far((0,))
    for k in range(GROUP - 1):
        letter(k).wait_recv()
    keep = pltpu.make_async_copy(images, images_out, store_sem.at[4])
    keep.start()
    tokens, slot = x_ref.shape[1], rows.shape[1]
    hidden = hidden_rows(GROUP * slot, slot, tokens)

    def reply(m, k):
        target = lax.rem(t + k + 1, GROUP)
        return pltpu.make_async_remote_copy(
            attended_box.at[m, target],
            attended.at[t, m],
            back_send.at[m, k],
            back_recv.at[m, k],
            device_id=(f, target),
            device_id_type=MESH,
        )

    for m in range(MICRO):
        result = attend(images[:, m].reshape(GROUP * slot, 384), hidden)
        attended_box[m] = result.reshape(GROUP, slot, 128)
        for k in range(GROUP - 1):
            reply(m, k).start()
        attended[t, m] = attended_box[m, t]
        if m < MICRO - 1:
            for part in wide:
                part.far((1, 2, 3)[2 * m : 2 * m + 2])
    for part in wide:
        part.last()
    for m in range(MICRO):
        for k in range(GROUP - 1):
            reply(m, k).wait_recv()
    keep_attended = pltpu.make_async_copy(attended, attended_out, store_sem.at[5])
    keep_attended.start()
    for part in wide:
        part.done()
    for part in early + wide:
        part.sent()
    for k in range(GROUP - 1):
        letter(k).wait_send()
        for m in range(MICRO):
            reply(m, k).wait_send()
    for store in stores:
        store.wait()
    keep.wait()
    keep_attended.wait()


ANY = pl.BlockSpec(memory_space=pl.ANY)
VMEM = pl.BlockSpec(memory_space=pltpu.VMEM)


def forward(x, qkv_block, wide_blocks, small, slot):
    width = x.shape[-1]
    count = MICRO * slot
    lanes = qkv_block.shape[-1]
    wide = wide_blocks[0].shape[-1]
    images = (GROUP, MICRO, slot, 3 * lanes)
    attended = (GROUP, MICRO, slot, lanes)
    return pl.pallas_call(
        forward_kernel,
        out_shape=[
            jax.ShapeDtypeStruct((count, width), BF16),
            jax.ShapeDtypeStruct(images, BF16),
            jax.ShapeDtypeStruct(attended, BF16),
            jax.ShapeDtypeStruct((8, width), F32),
            jax.ShapeDtypeStruct((8, 512), F32),
            jax.ShapeDtypeStruct((3,) + LEAD + (64, lanes), BF16),
        ]
        + [jax.ShapeDtypeStruct(LEAD + (64, wide), BF16)] * 3,
        in_specs=[VMEM] + [ANY] * 5,
        out_specs=[ANY] * 3 + [VMEM] * 2 + [ANY] * 4,
        scratch_shapes=[
            pltpu.VMEM((MICRO, slot, width), F32),
            pltpu.VMEM(LEAD + (64, lanes), BF16),
            pltpu.VMEM(LEAD + (64, lanes), BF16),
            pltpu.VMEM(LEAD + (64, lanes), BF16),
            pltpu.VMEM(LEAD + (32, 128), BF16),
            pltpu.VMEM((GROUP, 1, 3 * lanes), F32),
            pltpu.VMEM((count, width), BF16),
            pltpu.VMEM(images, BF16),
            pltpu.VMEM(images, BF16),
            pltpu.VMEM((MICRO, GROUP, slot, lanes), BF16),
            pltpu.VMEM(attended, BF16),
            pltpu.SemaphoreType.DMA((8,)),
            pltpu.SemaphoreType.DMA((7, Gather.slots)),
            pltpu.SemaphoreType.DMA((7, Gather.slots)),
            pltpu.SemaphoreType.DMA((GROUP,)),
            pltpu.SemaphoreType.DMA((GROUP,)),
            pltpu.SemaphoreType.DMA((MICRO, GROUP)),
            pltpu.SemaphoreType.DMA((MICRO, GROUP)),
            pltpu.SemaphoreType.DMA((6,)),
        ],
        compiler_params=pltpu.CompilerParams(
            collective_id=0, has_side_effects=True, vmem_limit_bytes=VMEM_LIMIT
        ),
        name="forward",
    )(x, qkv_block, *wide_blocks, small)


def middle_kernel(
    x_ref,
    cot_ref,
    valid_ref,
    attended_ref,
    out_ref,
    wide_1,
    wide_2,
    wide_3,
    vectors_ref,
    hidden_ref,
    result_ref,
    d_middle_ref,
    low_middle_ref,
    d_attended_ref,
    grad_1,
    grad_2,
    grad_3,
    sums_ref,
    hidden_sums_ref,
    rows,
    middle,
    normed,
    inverse,
    low,
    low_t,
    upstream_low,
    upstream_t,
    forward_sum,
    back_sum,
):
    step = pl.program_id(0)
    micro, tokens, width = x_ref.shape
    count = micro * rows.shape[1]
    gain_two, bias_two = vectors_ref[3:4, :], vectors_ref[4:5, :]

    @pl.when(step == 0)
    def _():
        padded_rows(x_ref, rows)
        middle[...] = rows[...].reshape(count, width) + vectors_ref[2:3, :]

        def project(pair, carry):
            both = [attended_ref[2 * pair + i].reshape(count, 128) for i in range(2)]
            weights = [out_ref[2 * pair + i] for i in range(2)]
            middle[...] += mm(
                jnp.concatenate(both, axis=1), jnp.concatenate(weights, axis=1), NT
            )
            return carry

        lax.fori_loop(0, GROUP // 2, project, 0)
        normed[...], inverse[...] = norm_stats(middle[...])
        low[...] = (normed[...] * gain_two + bias_two).astype(BF16)
        low_t[...] = low[...].T
        for m in range(micro):
            slot = valid_ref[m, 0].astype(F32)
            rows[m, :tokens] = cot_ref[m].astype(F32) * slot
        values = rows[...].reshape(count, width)
        sums_ref[5:6, :] = jnp.sum(values, 0, keepdims=True)
        upstream_low[...] = values.astype(BF16)
        upstream_t[...] = upstream_low[...].T
        forward_sum[...] = jnp.zeros_like(forward_sum)
        back_sum[...] = jnp.zeros_like(back_sum)

    up_weight = jnp.concatenate([wide_1[0, :, 128:], wide_2[0, :, :256]], axis=1)
    down_weight = jnp.concatenate([wide_2[0, :, 256:], wide_3[0]], axis=1)
    up_proj = mm(low[...], up_weight) + hidden_ref[0]
    gate = jax.nn.sigmoid(1.702 * up_proj)
    activated = (up_proj * gate).astype(BF16)
    d_act = mm(upstream_low[...], down_weight)
    d_up = (d_act * (gate + 1.702 * up_proj * gate * (1.0 - gate))).astype(BF16)
    hidden_sums_ref[0] = jnp.sum(d_up.astype(F32), 0, keepdims=True)
    forward_sum[...] += mm(activated, down_weight, NT)
    back_sum[...] += mm(d_up, up_weight, NT)
    grad_up = mm(low_t[...], d_up).astype(BF16)
    grad_1[0] = grad_up[:, :384]
    grad_2[0, :, :128] = grad_up[:, 384:]
    grad_down = mm(upstream_t[...], activated).astype(BF16)
    grad_2[0, :, 128:] = grad_down[:, :256]
    grad_3[0] = grad_down[:, 256:]

    @pl.when(step == GROUP - 1)
    def _():
        output = (middle[...] + forward_sum[...] + vectors_ref[5:6, :]).reshape(rows.shape)
        result_ref[...] = output[:, :tokens].astype(BF16)
        d_norm = back_sum[...]
        upstream = rows[...].reshape(count, width)
        d_middle = upstream + norm_back(d_norm, normed[...], inverse[...], gain_two)
        d_middle_ref[...] = d_middle
        low_middle = d_middle.astype(BF16)
        low_middle_ref[...] = low_middle
        sums_ref[0:2, :] = jnp.zeros((2, width), F32)
        sums_ref[2:3, :] = jnp.sum(d_middle, 0, keepdims=True)
        sums_ref[3:4, :] = jnp.sum(d_norm * normed[...], 0, keepdims=True)
        sums_ref[4:5, :] = jnp.sum(d_norm, 0, keepdims=True)
        sums_ref[6:8, :] = jnp.zeros((2, width), F32)

        def project_back(pair, carry):
            weights = [out_ref[2 * pair + i] for i in range(2)]
            both = mm(low_middle_ref[...], jnp.concatenate(weights, axis=1)).astype(BF16)
            for i in range(2):
                d_attended_ref[2 * pair + i] = both[:, 128 * i : 128 * i + 128].reshape(
                    d_attended_ref.shape[1:]
                )
            return carry

        lax.fori_loop(0, GROUP // 2, project_back, 0)


def middle_part(x, cotangent, valid, attended, wide, vectors, hidden):
    micro, tokens, width = x.shape
    slot = attended.shape[2]
    count = micro * slot
    whole = lambda shape: pl.BlockSpec(shape, lambda t: (0,) * len(shape))
    slab = lambda lanes: pl.BlockSpec((1, width, lanes), lambda t: (t, 0, 0))
    line = pl.BlockSpec((1, 1, 512), lambda t: (t, 0, 0))
    return pl.pallas_call(
        middle_kernel,
        grid=(GROUP,),
        in_specs=[
            whole(x.shape),
            whole(x.shape),
            pl.BlockSpec(memory_space=pltpu.SMEM),
            whole(attended.shape),
            whole((GROUP, width, 128)),
            slab(384),
            slab(384),
            slab(384),
            whole(vectors.shape),
            line,
        ],
        out_specs=[
            whole(x.shape),
            whole((count, width)),
            whole((count, width)),
            whole(attended.shape),
            slab(384),
            slab(384),
            slab(256),
            whole((8, width)),
            line,
        ],
        out_shape=[
            jax.ShapeDtypeStruct(x.shape, BF16),
            jax.ShapeDtypeStruct((count, width), F32),
            jax.ShapeDtypeStruct((count, width), BF16),
            jax.ShapeDtypeStruct(attended.shape, BF16),
            jax.ShapeDtypeStruct((GROUP, width, 384), BF16),
            jax.ShapeDtypeStruct((GROUP, width, 384), BF16),
            jax.ShapeDtypeStruct((GROUP, width, 256), BF16),
            jax.ShapeDtypeStruct((8, width), F32),
            jax.ShapeDtypeStruct((GROUP, 1, 512), F32),
        ],
        scratch_shapes=[
            pltpu.VMEM((micro, slot, width), F32),
            pltpu.VMEM((count, width), F32),
            pltpu.VMEM((count, width), F32),
            pltpu.VMEM((count, 1), F32),
            pltpu.VMEM((count, width), BF16),
            pltpu.VMEM((width, count), BF16),
            pltpu.VMEM((count, width), BF16),
            pltpu.VMEM((width, count), BF16),
            pltpu.VMEM((count, width), F32),
            pltpu.VMEM((count, width), F32),
        ],
        compiler_params=pltpu.CompilerParams(vmem_limit_bytes=VMEM_LIMIT),
        name="middle",
    )(x, cotangent, valid, attended, wide[0], *wide, vectors, hidden)


def backward_kernel(*refs):
    (
        d_attended_in,
        images_in,
        low_in,
        low_middle_in,
        attended_in,
        d_middle_ref,
        x_ref,
        vectors_ref,
        sums_ref,
        hidden_sums_ref,
        qkv_in,
        grad_1,
        grad_2,
        grad_3,
        input_grad_out,
        sum_1,
        sum_2,
        sum_3,
        sum_o,
        sum_q,
        sum_k,
        sum_v,
        payload_out,
        rows,
        wq,
        wk,
        wv,
        low,
        low_middle,
        attended,
        images,
        d_attended,
        outbox,
        d_images,
        d_norm,
        go,
        gq,
        gk,
        gv,
        payload,
        payload_in,
        *rest,
    ) = refs
    rest = list(rest)
    me = place()
    f, t = lax.axis_index("fsdp"), lax.axis_index("tp")
    greet(me)
    kinds = [
        (grad_1, None, sum_1, 0),
        (grad_2, None, sum_2, 1),
        (grad_3, None, sum_3, 2),
        (go, go, sum_o, 2),
        (gq, gq, sum_q, 0),
        (gk, gk, sum_k, 1),
        (gv, gv, sum_v, 2),
    ]
    pieces = []
    for source, acc, out, _ in kinds:
        if acc is None:
            acc = rest.pop(0)
        pieces.append([source, acc] + [rest.pop(0) for _ in range(5)] + [out])
    (
        load_sem,
        fetch_sem,
        reduce_send,
        reduce_recv,
        send_sem,
        recv_sem,
        back_send,
        back_recv,
        sum_send,
        sum_recv,
    ) = rest
    parts = [
        Reduce(
            me,
            ORDERS[kinds[i][3]],
            *pieces[i],
            reduce_send.at[i],
            reduce_recv.at[i],
            fetch_sem.at[i],
        )
        for i in range(7)
    ]
    wide, late = parts[:4], parts[4:]
    heads = [wq, wk, wv]

    def letter(k):
        target = lax.rem(t + k + 1, GROUP)
        return pltpu.make_async_remote_copy(
            d_attended_in.at[target],
            d_attended.at[t],
            send_sem.at[k],
            recv_sem.at[k],
            device_id=(f, target),
            device_id_type=MESH,
        )

    for k in range(GROUP - 1):
        letter(k).start()
    loads = [
        (d_attended_in.at[t], d_attended.at[t]),
        (images_in, images),
        (low_middle_in, low_middle),
        (attended_in, attended),
        (low_in, low),
        (qkv_in.at[0], wq),
        (qkv_in.at[1], wk),
        (qkv_in.at[2], wv),
    ]
    loads = [
        pltpu.make_async_copy(src, dst, load_sem.at[i]) for i, (src, dst) in enumerate(loads)
    ]
    for load in loads:
        load.start()
    for part in wide[:3]:
        part.begin()
    loads[2].wait()
    loads[3].wait()
    turned = low_middle[...].T
    count = low_middle.shape[0]

    def out_gradient(index, carry):
        result = mm(turned, attended[index].reshape(count, 128)).astype(BF16)
        go[index // 2, lax.rem(index, 2)] = result.reshape(go.shape[2:])
        return carry

    lax.fori_loop(0, GROUP, out_gradient, 0)
    wide[3].begin()
    for part in wide:
        part.stage_far()
    loads[0].wait()
    loads[1].wait()
    for k in range(GROUP - 1):
        letter(k).wait_recv()
    tokens, slot = x_ref.shape[1], rows.shape[1]
    hidden = hidden_rows(GROUP * slot, slot, tokens)

    def reply(m, k):
        target = lax.rem(t + k + 1, GROUP)
        return pltpu.make_async_remote_copy(
            outbox.at[m, target],
            d_images.at[t, m],
            back_send.at[m, k],
            back_recv.at[m, k],
            device_id=(f, target),
            device_id_type=MESH,
        )

    for m in range(MICRO):
        results = attend_back(
            images[:, m].reshape(GROUP * slot, 384),
            d_attended[:, m].reshape(GROUP * slot, 128),
            hidden,
        )
        for i in range(3):
            outbox[m, :, :, 128 * i : 128 * i + 128] = results[i].reshape(GROUP, slot, 128)
        for k in range(GROUP - 1):
            reply(m, k).start()
        d_images[t, m] = outbox[m, t]
        if m == 0:
            for part in wide:
                part.stage_near()
    for part in wide:
        part.stage_mid()
    padded_rows(x_ref, rows)
    normed, inverse = norm_stats(rows[...].reshape(count, rows.shape[-1]))
    for load in loads[4:]:
        load.wait()
    low_t = low[...].T
    d_norm[...] = jnp.zeros_like(d_norm)
    for m in range(MICRO):
        for k in range(GROUP - 1):
            reply(m, k).wait_recv()
    for part in wide:
        part.stage_tail()

    def project_back(index, carry):
        grads = d_images[index].reshape(count, 384)
        weights = jnp.concatenate([blocks_of(w, index) for w in heads], axis=1)
        d_norm[...] += mm(grads, weights, NT)
        result = mm(low_t, grads).astype(BF16)
        for i, g in enumerate((gq, gk, gv)):
            g[index // 2, lax.rem(index, 2)] = result[:, 128 * i : 128 * i + 128].reshape(
                g.shape[2:]
            )
        return carry

    lax.fori_loop(0, GROUP, project_back, 0)
    for part in late:
        part.begin()
    gain_one = vectors_ref[0:1, :]
    gradient = d_norm[...]
    payload[0, 0:8, :] = sums_ref[...]
    payload[0, 0:1, :] = jnp.sum(gradient * normed, 0, keepdims=True)
    payload[0, 1:2, :] = jnp.sum(gradient, 0, keepdims=True)
    for index in range(GROUP):
        grads = jnp.sum(d_images[index].reshape(count, 384).astype(F32), 0, keepdims=True)
        payload[0, 6:7, 128 * index : 128 * index + 128] = grads[:, :128]
        payload[0, 7:8, 128 * index : 128 * index + 128] = grads[:, 256:]
        at = 8 + index // 2
        payload[0, at : at + 1, 512 * (index % 2) : 512 * (index % 2) + 512] = hidden_sums_ref[
            index
        ]
    payload[0, 12:16, :] = jnp.zeros((4, payload.shape[-1]), F32)

    rounds = [[shifted(me, axis, by) for by in STEPS] for axis in "xyz"] + [[sibling(me)]]

    def tell(number, i):
        return pltpu.make_async_remote_copy(
            payload.at[number],
            payload_in.at[number, i],
            sum_send.at[number, i],
            sum_recv.at[number, i],
            device_id=device_at(rounds[number][i]),
            device_id_type=MESH,
        )

    def speak(number):
        for i in range(len(rounds[number])):
            tell(number, i).start()

    def hear(number):
        total = payload[number]
        for i in range(len(rounds[number])):
            tell(number, i).wait_recv()
            total += payload_in[number, i]
        payload[number + 1] = total

    speak(0)
    for part in wide:
        part.stage_out()
    for part in late:
        part.stage_far()
    hear(0)
    speak(1)
    result = d_middle_ref[...] + norm_back(gradient, normed, inverse, gain_one)
    input_grad_out[...] = result.reshape(rows.shape)[:, :tokens].astype(BF16)
    hear(1)
    speak(2)
    for part in late:
        part.stage_near()
    hear(2)
    speak(3)
    for part in late:
        part.stage_mid()
    hear(3)
    payload_out[...] = payload[4]
    for part in late:
        part.stage_tail()
    for part in late:
        part.stage_out()
    for part in parts:
        part.sent()
    for k in range(GROUP - 1):
        letter(k).wait_send()
        for m in range(MICRO):
            reply(m, k).wait_send()
    for number in range(4):
        for i in range(len(rounds[number])):
            tell(number, i).wait_send()


def backward(
    d_attended, images, low, low_middle, attended, d_middle, x, vectors, sums, hidden_sums, qkv, grads
):
    width = x.shape[-1]
    count = low.shape[0]
    slot = count // MICRO
    lanes = [g.shape[-1] for g in grads]
    orders = (0, 1, 2, 2, 0, 1, 2)
    scratch = []
    for i in range(7):
        scratch += reduce_scratch(ORDERS[orders[i]], lanes[i] if i < 3 else 128, BF16, i >= 3)
    return pl.pallas_call(
        backward_kernel,
        out_shape=[jax.ShapeDtypeStruct(x.shape, BF16)]
        + [jax.ShapeDtypeStruct((64, n), F32) for n in lanes + [128] * 4]
        + [jax.ShapeDtypeStruct((16, width), F32)],
        in_specs=[ANY] * 5 + [VMEM] * 5 + [ANY] * 4,
        out_specs=[VMEM] * 9,
        scratch_shapes=[
            pltpu.VMEM((MICRO, slot, width), F32),
            pltpu.VMEM(LEAD + (64, 128), BF16),
            pltpu.VMEM(LEAD + (64, 128), BF16),
            pltpu.VMEM(LEAD + (64, 128), BF16),
            pltpu.VMEM(low.shape, BF16),
            pltpu.VMEM(low_middle.shape, BF16),
            pltpu.VMEM(attended.shape, BF16),
            pltpu.VMEM(images.shape, BF16),
            pltpu.VMEM(d_attended.shape, BF16),
            pltpu.VMEM((MICRO, GROUP, slot, 384), BF16),
            pltpu.VMEM(images.shape, BF16),
            pltpu.VMEM((count, width), F32),
            pltpu.VMEM(LEAD + (64, 128), BF16),
            pltpu.VMEM(LEAD + (64, 128), BF16),
            pltpu.VMEM(LEAD + (64, 128), BF16),
            pltpu.VMEM(LEAD + (64, 128), BF16),
            pltpu.VMEM((5, 16, width), F32),
            pltpu.VMEM((4, 3, 16, width), F32),
        ]
        + scratch
        + [
            pltpu.SemaphoreType.DMA((8,)),
            pltpu.SemaphoreType.DMA((7, 4)),
            pltpu.SemaphoreType.DMA((7, Reduce.slots)),
            pltpu.SemaphoreType.DMA((7, Reduce.slots)),
            pltpu.SemaphoreType.DMA((GROUP,)),
            pltpu.SemaphoreType.DMA((GROUP,)),
            pltpu.SemaphoreType.DMA((MICRO, GROUP)),
            pltpu.SemaphoreType.DMA((MICRO, GROUP)),
            pltpu.SemaphoreType.DMA((4, 3)),
            pltpu.SemaphoreType.DMA((4, 3)),
        ],
        compiler_params=pltpu.CompilerParams(
            collective_id=1, has_side_effects=True, vmem_limit_bytes=VMEM_LIMIT
        ),
        name="backward",
    )(
        d_attended,
        images,
        low,
        low_middle,
        attended,
        d_middle,
        x,
        vectors,
        sums,
        hidden_sums,
        qkv,
        *(g.reshape(LEAD + (64, g.shape[-1])) for g in grads),
    )


def per_device(
    inputs,
    cotangent,
    valid_slots,
    ln1_gain,
    ln1_bias,
    qkv_weight,
    qv_bias,
    out_weight,
    out_bias,
    ln2_gain,
    ln2_bias,
    fc1_weight,
    fc1_bias,
    fc2_weight,
    fc2_bias,
):
    micro, _, tokens, width = inputs.shape
    slot = -(-tokens // 16) * 16
    x = inputs.reshape(micro, tokens, width)
    small = jnp.concatenate(
        [ln1_gain, ln1_bias, out_bias, ln2_gain, ln2_bias, fc2_bias]
        + [qv_bias.reshape(-1), fc1_bias.reshape(-1)]
    )
    small = jnp.pad(small.reshape(1, 96), ((0, 31), (0, 32)))
    down = fc2_weight.T
    wide_blocks = [
        jnp.concatenate([out_weight.T, fc1_weight[:, :256]], axis=1),
        jnp.concatenate([fc1_weight[:, 256:], down[:, :128]], axis=1),
        down[:, 128:],
    ]
    low, images, attended, vectors, hidden, qkv, *wide = forward(
        x, qkv_weight, wide_blocks, small, slot
    )
    wide = [w.reshape(GROUP, width, 384) for w in wide]
    result, d_middle, low_middle, d_attended, *grads, sums, hidden_sums = middle_part(
        x,
        cotangent.reshape(x.shape),
        valid_slots,
        attended,
        wide,
        vectors,
        hidden.reshape(GROUP, 1, 512),
    )
    input_grad, sum_1, sum_2, sum_3, sum_o, sum_q, sum_k, sum_v, total = backward(
        d_attended,
        images,
        low,
        low_middle,
        attended,
        d_middle,
        x,
        vectors,
        sums,
        hidden_sums,
        qkv,
        grads,
    )
    f, t = lax.axis_index("fsdp"), lax.axis_index("tp")
    own = lax.dynamic_slice(total, (0, (f * 8 + t) * 8), (6, 8))
    pair = lax.dynamic_slice(total[6:8].reshape(2, 16, 64), (0, 2 * t, 4 * f), (2, 2, 4))
    hidden_grad = lax.dynamic_slice(total[8:12].reshape(64, 64), (8 * t, 4 * f), (8, 4))
    return (
        result.reshape(inputs.shape),
        input_grad.reshape(inputs.shape),
        own[0],
        own[1],
        jnp.stack([sum_q, sum_k, sum_v]),
        pair,
        sum_o.T,
        own[2],
        own[3],
        own[4],
        jnp.concatenate([sum_1, sum_2[:, :128]], axis=1),
        hidden_grad,
        jnp.concatenate([sum_2[:, 128:], sum_3], axis=1).T,
        own[5],
    )


def solution(mesh):
    in_specs = (
        P(None, "fsdp", "tp", None),
        P(None, "fsdp", "tp", None),
        P(None, "fsdp"),
        P(("fsdp", "tp")),
        P(("fsdp", "tp")),
        P(None, "fsdp", "tp"),
        P(None, "tp", "fsdp"),
        P("tp", "fsdp"),
        P(("fsdp", "tp")),
        P(("fsdp", "tp")),
        P(("fsdp", "tp")),
        P("fsdp", "tp"),
        P("tp", "fsdp"),
        P("tp", "fsdp"),
        P(("fsdp", "tp")),
    )
    out_specs = (
        P(None, "fsdp", "tp", None),
        P(None, "fsdp", "tp", None),
        P(("fsdp", "tp")),
        P(("fsdp", "tp")),
        P(None, "fsdp", "tp"),
        P(None, "tp", "fsdp"),
        P("tp", "fsdp"),
        P(("fsdp", "tp")),
        P(("fsdp", "tp")),
        P(("fsdp", "tp")),
        P("fsdp", "tp"),
        P("tp", "fsdp"),
        P("tp", "fsdp"),
        P(("fsdp", "tp")),
    )
    return jax.shard_map(
        per_device, mesh=mesh, in_specs=in_specs, out_specs=out_specs, check_vma=False
    )
```

```python
import functools
import math

import jax
import jax.numpy as jnp
from jax import lax
from jax.experimental import pallas as pl
from jax.experimental.pallas import tpu as pltpu
from jax.sharding import PartitionSpec as P

MESH = pl.DeviceIdType.MESH
HD = 64
SCALE = 1.0 / math.sqrt(HD)
EPSILON = 1e-05
BF16 = jnp.bfloat16
F32 = jnp.float32
VMEM_LIMIT = 62 * 2**20
MICRO, GROUP = 3, 8
ORDERS = (("x", "y", "z"), ("y", "z", "x"), ("z", "x", "y"))
SIZES = {"x": (4,), "z": (2, 2), "y": (4,)}
LEAD = (4, 2, 2, 4, 2)
STEPS = (1, -1, 2)
NN = (((1,), (0,)), ((), ()))
NT = (((1,), (1,)), ((), ()))
TN = (((0,), (0,)), ((), ()))


def mm(a, b, dims=NN):
    return lax.dot_general(a, b, dims, preferred_element_type=F32)


def place():
    f, t = lax.axis_index("fsdp"), lax.axis_index("tp")
    return {
        "x": t // 2,
        "y": lax.rem(f // 2, 4),
        "z": (f // 8) * 2 + lax.rem(t, 2),
        "c": lax.rem(f, 2),
    }


def device_at(spot):
    return (
        (spot["z"] // 2) * 8 + spot["y"] * 2 + spot["c"],
        spot["x"] * 2 + lax.rem(spot["z"], 2),
    )


def shifted(spot, axis, by):
    return {**spot, axis: lax.rem(spot[axis] + by + 4, 4)}


def sibling(spot):
    return {**spot, "c": 1 - spot["c"]}


def greet(me):
    f, t = lax.axis_index("fsdp"), lax.axis_index("tp")
    devices = [(f, lax.rem(t + step, GROUP)) for step in range(1, GROUP)]
    devices += [device_at(shifted(me, "y", by)) for by in STEPS]
    devices += [device_at(shifted(me, "z", 2))]
    devices += [device_at(shifted(me, "z", 2 * lax.rem(me["z"], 2) - 1))]
    devices += [device_at(sibling(me))]
    barrier = pltpu.get_barrier_semaphore()
    for device in devices:
        pl.semaphore_signal(barrier, inc=1, device_id=device, device_id_type=MESH)
    pl.semaphore_wait(barrier, len(devices))


def view(ref, spot, full, core=None, rows=slice(None)):
    whole = slice(None)
    index = [
        whole if "x" in full else spot["x"],
        whole if "z" in full else lax.rem(spot["z"], 2),
        whole if "z" in full else spot["z"] // 2,
        whole if "y" in full else spot["y"],
    ]
    if core is not None:
        index.append(core)
    return ref.at[tuple(index) + (rows,)]


def decode(number, spot, full):
    at = {}
    for axis in "yzx":
        if axis in full:
            parts = []
            for size in reversed(SIZES[axis]):
                parts.append(lax.rem(number, size))
                number = number // size
            at[axis] = tuple(reversed(parts))
    fixed = {"x": (spot["x"],), "z": (lax.rem(spot["z"], 2), spot["z"] // 2), "y": (spot["y"],)}
    index, inner = (), ()
    for axis in "xzy":
        index += at.get(axis, fixed[axis])
        inner += at.get(axis, ())
    return index, inner


def bundle_shape(full):
    shape = ()
    for axis in "xzy":
        shape += SIZES[axis] if axis in full else ()
    return shape


class Copies:
    def __init__(self, send, recv):
        self.send, self.recv = send, recv
        self.made = {}

    def start(self, name, src, dst, device):
        slot = len(self.made)
        self.made[name] = pltpu.make_async_remote_copy(
            src,
            dst,
            self.send.at[slot],
            self.recv.at[slot],
            device_id=device,
            device_id_type=MESH,
        )
        self.made[name].start()

    def arrived(self, name):
        self.made[name].wait_recv()

    def sent(self):
        for copy in self.made.values():
            copy.wait_send()


class Gather:
    slots = 38

    def __init__(self, me, order, block, out, send, recv, local):
        self.me, self.order, self.block, self.out = me, order, block, out
        self.copies = Copies(send, recv)
        self.local = local
        self.core = me["c"]
        self.half = out.shape[-2] // 2

    def piece(self, spot, full, rows=slice(None)):
        return view(self.out, spot, full, self.core, rows)

    def spread(self, name, spot, full, axis, by, rows=slice(None)):
        piece = self.piece(spot, full, rows)
        target = shifted(self.me, axis, by)
        self.copies.start(name, piece, piece, device_at(target))

    def share(self, name, spot, full):
        piece = self.piece(spot, full)
        self.copies.start(name, piece, piece, device_at(sibling(self.me)))

    def own(self):
        return pltpu.make_async_copy(
            self.block, view(self.out, self.me, "", self.core), self.local
        )

    def first(self):
        me, axis = self.me, self.order[0]
        self.own().start()
        for by in STEPS:
            target = shifted(me, axis, by)
            self.copies.start(
                ("first", by), self.block, self.piece(me, ""), device_at(target)
            )

    def second(self):
        full, axis = self.order[0], self.order[1]
        self.own().wait()
        for by in STEPS:
            self.copies.arrived(("first", by))
        for by in STEPS:
            self.spread(("second", by), self.me, full, axis, by)
        self.third(0)

    def third(self, group):
        full, axis = self.order[0], self.order[2]
        spot = self.spot(group)
        if group:
            self.copies.arrived(("second", STEPS[group - 1]))
        for by in (1, -1):
            self.spread(("near", group, by), spot, full, axis, by)
        self.share(("share", group), spot, full)

    def spot(self, group):
        return self.me if group == 0 else shifted(self.me, self.order[1], -STEPS[group - 1])

    def thirds(self):
        for group in (1, 2, 3):
            self.third(group)

    def far(self, groups=(0, 1, 2, 3)):
        full, axis = self.order[0], self.order[2]
        for group in groups:
            for way, by in enumerate((1, -1)):
                spot = shifted(self.spot(group), axis, -by)
                self.copies.arrived(("near", group, by))
                rows = pl.ds(way * self.half, self.half)
                self.spread(("far", group, by), spot, full, axis, by, rows)
                self.share(("share near", group, by), spot, full)

    def last(self):
        full, axis = self.order[0], self.order[2]
        for group in range(4):
            for by in (1, -1):
                self.copies.arrived(("far", group, by))
            self.share(("share far", group), shifted(self.spot(group), axis, 2), full)

    def done(self):
        for group in range(4):
            self.copies.arrived(("share", group))
            self.copies.arrived(("share near", group, 1))
            self.copies.arrived(("share near", group, -1))
            self.copies.arrived(("share far", group))

    def sent(self):
        self.copies.sent()


class Reduce:
    slots = 10

    def __init__(self, me, order, acc, near, far, mid, tail, send, recv):
        self.me, self.order, self.acc = me, order, acc
        self.nears, self.fars, self.mid, self.tail = near, far, mid, tail
        self.copies = Copies(send, recv)
        self.half = acc.shape[-2] // 2
        self.full = "".join(order[:2])

    def chunk(self, by):
        return shifted(self.me, self.order[2], by)

    def add(self, spot, full, sources):
        acc = self.acc

        def one(number, carry):
            index, inner = decode(number, spot, full)
            for first, rows, terms in sources:
                here = index + (pl.ds(first, rows),)
                total = acc[here]
                if len(terms) > 1:
                    total = total.astype(F32)
                for ref, lead, base in terms:
                    term = ref[(lead,) + inner + (pl.ds(base, rows),)]
                    total += term.astype(total.dtype)
                acc[here] = total.astype(acc.dtype)
            return carry

        lax.fori_loop(0, math.prod(bundle_shape(full)), one, 0)

    def stage_far(self):
        spot = self.chunk(2)
        for way, by in enumerate((1, -1)):
            self.copies.start(
                ("far", by),
                view(self.acc, spot, self.full, None, pl.ds(way * self.half, self.half)),
                self.fars.at[way],
                device_at(self.chunk(by)),
            )

    def stage_near(self):
        half = self.half
        for way, by in enumerate((1, -1)):
            spot = self.chunk(by)
            self.copies.arrived(("far", by))
            self.add(spot, self.full, [(way * half, half, [(self.fars, way, 0)])])
            self.copies.start(
                ("near", by),
                view(self.acc, spot, self.full),
                self.nears.at[way],
                device_at(spot),
            )

    def spread(self, name, axis, full, target):
        for number, by in enumerate(STEPS):
            spot = shifted(self.me, axis, by)
            self.copies.start(
                (name, by), view(self.acc, spot, full), target.at[number], device_at(spot)
            )

    def stage_mid(self):
        self.copies.arrived(("near", 1))
        self.copies.arrived(("near", -1))
        terms = [(self.nears, 0, 0), (self.nears, 1, 0)]
        self.add(self.me, self.full, [(0, 2 * self.half, terms)])
        self.spread("mid", self.order[1], self.order[0], self.mid)

    def stage_tail(self):
        for by in STEPS:
            self.copies.arrived(("mid", by))
        terms = [(self.mid, number, 0) for number in range(3)]
        self.add(self.me, self.order[0], [(0, 2 * self.half, terms)])
        self.spread("tail", self.order[0], "", self.tail)

    def stage_out(self):
        for by in STEPS:
            self.copies.arrived(("tail", by))
        index, _ = decode(0, self.me, "")
        total = self.acc[index].astype(F32)
        for number in range(3):
            total += self.tail[number].astype(F32)
        return total

    def sent(self):
        self.copies.sent()


def reduce_scratch(order, lanes):
    full = bundle_shape(order[:2])
    return [
        pltpu.VMEM((4, 2, 2, 4, 64, lanes), BF16),
        pltpu.VMEM((2,) + full + (64, lanes), BF16),
        pltpu.VMEM((2,) + full + (32, lanes), BF16),
        pltpu.VMEM((3,) + bundle_shape(order[:1]) + (64, lanes), BF16),
        pltpu.VMEM((3, 64, lanes), BF16),
    ]


class Totals:
    def __init__(self, me, sums, inbox, send, recv):
        self.rounds = [[shifted(me, axis, by) for by in STEPS] for axis in "xyz"] + [[sibling(me)]]
        self.sums, self.inbox, self.send, self.recv = sums, inbox, send, recv
        self.made = {}

    def speak(self, number):
        for i, spot in enumerate(self.rounds[number]):
            copy = pltpu.make_async_remote_copy(
                self.sums.at[number],
                self.inbox.at[number, i],
                self.send.at[number, i],
                self.recv.at[number, i],
                device_id=device_at(spot),
                device_id_type=MESH,
            )
            copy.start()
            self.made[number, i] = copy

    def hear(self, number):
        total = self.sums[number]
        for i in range(len(self.rounds[number])):
            self.made[number, i].wait_recv()
            total += self.inbox[number, i]
        self.sums[number + 1] = total

    def pass_on(self, number):
        self.hear(number)
        self.speak(number + 1)

    def sent(self):
        for copy in self.made.values():
            copy.wait_send()


def norm_stats(values):
    average = jnp.mean(values, -1, keepdims=True)
    centered = values - average
    inverse = lax.rsqrt(jnp.mean(centered * centered, -1, keepdims=True) + EPSILON)
    return (centered * inverse, inverse)


def norm_back(upstream, normed, inverse, gain_vector):
    scaled = upstream * gain_vector
    return inverse * (
        scaled
        - jnp.mean(scaled, -1, keepdims=True)
        - normed * jnp.mean(scaled * normed, -1, keepdims=True)
    )


def softmax_columns(key_rows, queries, hidden):
    scores = mm(key_rows, queries, NT) + hidden
    powers = jnp.exp((scores - jnp.max(scores, 0, keepdims=True)) * SCALE)
    return powers * (1.0 / jnp.sum(powers, 0, keepdims=True))


def hidden_rows(seq, slot, tokens):
    row = lax.broadcasted_iota(jnp.int32, (seq, 1), 0)
    return jnp.where(lax.rem(row, slot) < tokens, 0.0, -1e30)


def head_lanes(head):
    lane = lax.broadcasted_iota(jnp.int32, (1, 128), 1)
    return jnp.where(lane // HD == head, 1.0, 0.0).astype(BF16)


def thirds(rows):
    return [rows[:, 128 * i : 128 * i + 128] for i in range(3)]


def attend(rows, hidden):
    queries, key_rows, value_rows = thirds(rows)

    def one_head(head, before):
        mine = head_lanes(head)
        probs = softmax_columns(key_rows, queries * mine, hidden).astype(BF16)
        return before + mm(probs, value_rows * mine, TN)

    return lax.fori_loop(0, 2, one_head, jnp.zeros(queries.shape, F32)).astype(BF16)


def attend_back(rows, grads, hidden):
    queries, key_rows, value_rows = thirds(rows)

    def one_head(head, before):
        mine = head_lanes(head)
        own_grads, own_queries = grads * mine, queries * mine
        probs = softmax_columns(key_rows, own_queries, hidden)
        d_probs = mm(value_rows, own_grads, NT)
        inner = jnp.sum(probs * d_probs, 0, keepdims=True)
        d_scores = (probs * (d_probs - inner)).astype(BF16)
        return (
            before[0] + mm(d_scores, key_rows * mine, TN),
            before[1] + mm(d_scores, own_queries),
            before[2] + mm(probs.astype(BF16), own_grads),
        )

    zero = jnp.zeros(queries.shape, F32)
    d_queries, d_keys, d_values = lax.fori_loop(0, 2, one_head, (zero, zero, zero))
    return [
        (d_queries * SCALE).astype(BF16),
        (d_keys * SCALE).astype(BF16),
        d_values.astype(BF16),
    ]


def padded_rows(ref, target):
    micro, tokens, width = ref.shape
    for m in range(micro):
        target[m, :tokens] = ref[m].astype(F32)
        target[m, tokens:] = jnp.zeros((target.shape[1] - tokens, width), F32)


def blocks_of(ref, index):
    value = ref[index // 2, lax.rem(index, 2)]
    return value.reshape(-1, value.shape[-1])


def half_planes(ref, value, kind, count):
    padded = jnp.concatenate(
        [value, jnp.zeros((ref.shape[-1] - count, value.shape[1]), value.dtype)], axis=0
    )
    ref[kind] = padded.T.reshape(ref.shape[1:])


def forward_kernel(*refs):
    (
        x_ref,
        cot_ref,
        valid_ref,
        qkv_in,
        out_in,
        fc1_in,
        fc2_in,
        small_in,
        result_out,
        d_middle_out,
        vectors,
        sums_out,
        d_attended_out,
        images_out,
        attended_out,
        turned_out,
        act_out,
        dup_out,
        qkv_out,
        rows,
        upstream,
        wq,
        wk,
        wv,
        wide_y,
        wide_x,
        wide_z,
        stage_y,
        stage_x,
        stage_z,
        small,
        bias,
        hidden_bias,
        low,
        outbox,
        images,
        attended_box,
        attended,
        middle,
        normed_two,
        low_two,
        upstream_low,
        turned,
        forward_sum,
        back_sum,
        act_box,
        dup_box,
        hidden_sums,
        local_sem,
        gather_send,
        gather_recv,
        send_sem,
        recv_sem,
        back_send,
        back_recv,
        store_sem,
        sib_send,
        sib_recv,
        ff_local,
        ff_send,
        ff_recv,
    ) = refs
    me = place()
    f, t = lax.axis_index("fsdp"), lax.axis_index("tp")
    core = me["c"]
    other = device_at(sibling(me))
    micro, tokens, width = x_ref.shape
    slot = rows.shape[1]
    count = micro * slot
    greet(me)
    heads = [wq, wk, wv]

    def gather(i, order, block, out):
        return Gather(
            me, order, block, out, gather_send.at[i], gather_recv.at[i], local_sem.at[i]
        )

    narrow = [gather(i, ORDERS[i], qkv_in.at[i], heads[i]) for i in range(3)]
    vector = gather(3, ORDERS[0], small_in, small)
    part_y = gather(4, ORDERS[2], stage_y, wide_y)
    part_x = gather(5, ORDERS[1], stage_x, wide_x)
    part_z = gather(6, ORDERS[0], stage_z, wide_z)
    wide = [part_z, part_y, part_x]
    early = [vector] + narrow
    stores = []

    def store(src, dst):
        copy = pltpu.make_async_copy(src, dst, store_sem.at[len(stores)])
        copy.start()
        stores.append(copy)

    shared = []

    def share(src, dst):
        slot_of = len(shared)
        copy = pltpu.make_async_remote_copy(
            src,
            dst,
            sib_send.at[slot_of],
            sib_recv.at[slot_of],
            device_id=other,
            device_id_type=MESH,
        )
        copy.start()
        shared.append(copy)

    def turn(kind, value):
        half_planes(turned, value, kind, count)
        store(turned.at[kind, :, core], turned_out.at[kind, 0])
        share(turned.at[kind, :, 1 - core], turned_out.at[kind, 1])

    for part in early:
        part.first()
    padded_rows(x_ref, rows)
    normed, _ = norm_stats(rows[...].reshape(count, width))
    for part in early:
        part.second()
    fc2_t = fc2_in[...].T
    stage_y[:, :512] = fc1_in[...]
    stage_y[:, 512:] = fc2_t[:, :128]
    stage_x[...] = fc2_t[:, 128:384]
    stage_z[:, :128] = fc2_t[:, 384:]
    stage_z[:, 128:] = out_in[...].T
    for part in early:
        part.thirds()
    for part in wide:
        part.first()
    for part in early:
        part.far()
    for part in wide:
        part.second()
    vector.last()
    vector.done()
    table = jnp.sum(small[...].reshape(128, 32, 128).astype(F32), 1).astype(BF16)
    lane = lax.broadcasted_iota(jnp.int32, (128, 1024), 0)
    column = lax.broadcasted_iota(jnp.int32, (128, 1024), 1)
    owner = jnp.where(lax.rem(lane, 16) * 8 + lane // 16 == column // 8, 1.0, 0.0)
    for v in range(6):
        pick = jnp.where(lane == v * 8 + lax.rem(column, 8), 1.0, 0.0).astype(BF16)
        vectors[v : v + 1, :] = jnp.sum(mm(table, pick) * owner, 0, keepdims=True)
    vectors[6:8, :] = jnp.zeros((2, 1024), F32)

    def spread_bias(lanes, first):
        lane = lax.broadcasted_iota(jnp.int32, (128, lanes), 0)
        column = lax.broadcasted_iota(jnp.int32, (128, lanes), 1)
        pick = lane == first + (column // 64) * 4 + lax.rem(column, 4)
        owner = lax.rem(lane, 16) == lax.rem(column, 64) // 4
        values = mm(table, jnp.where(pick, 1.0, 0.0).astype(BF16))
        return jnp.sum(jnp.where(owner, values, 0.0).reshape(8, 16, lanes), 1)

    hidden_value = spread_bias(512, 64)
    query_bias, value_bias = spread_bias(128, 48), spread_bias(128, 56)
    for i in range(GROUP):
        hidden_bias[i] = hidden_value[i : i + 1]
        bias[i, :, 0:128] = query_bias[i : i + 1]
        bias[i, :, 128:256] = jnp.zeros((1, 128), F32)
        bias[i, :, 256:384] = value_bias[i : i + 1]
    low[...] = (normed * vectors[0:1, :] + vectors[1:2, :]).astype(BF16)
    for part in narrow:
        part.last()
    for part in wide:
        part.thirds()
    for part in narrow:
        part.done()

    def letter(k, m):
        target = lax.rem(t + k + 1, GROUP)
        return pltpu.make_async_remote_copy(
            outbox.at[target, m],
            images.at[t, m],
            send_sem.at[k, m],
            recv_sem.at[k, m],
            device_id=(f, target),
            device_id_type=MESH,
        )

    def project(k, carry):
        target = lax.rem(t + k + 1, GROUP)
        weights = jnp.concatenate([blocks_of(w, target) for w in heads], axis=1)
        result = (mm(low[...], weights) + bias[target]).astype(BF16)
        outbox[target] = result.reshape(outbox.shape[1:])

        @pl.when(k < GROUP - 1)
        def _():
            letter(k, 0).start()

        return carry

    lax.fori_loop(0, GROUP, project, 0)
    for m in range(1, MICRO):
        for k in range(GROUP - 1):
            letter(k, m).start()
    own = pltpu.make_async_copy(outbox.at[t], images.at[t], local_sem.at[7])
    own.start()
    for i in range(3):
        store(heads[i], qkv_out.at[i])
    for part in wide:
        part.far((0,))
    turn(0, low[...])
    for m in range(micro):
        scale = valid_ref[m, 0].astype(F32)
        upstream[m, :tokens] = cot_ref[m].astype(F32) * scale
        upstream[m, tokens:] = jnp.zeros((slot - tokens, width), F32)
    upstream_rows = upstream[...].reshape(count, width)
    sums_out[3:4, :] = jnp.sum(upstream_rows, 0, keepdims=True)
    upstream_low[...] = upstream_rows.astype(BF16)
    turn(1, upstream_low[...])
    own.wait()
    hidden = hidden_rows(GROUP * slot, slot, tokens)

    def reply(m, k):
        target = lax.rem(t + k + 1, GROUP)
        return pltpu.make_async_remote_copy(
            attended_box.at[m, target],
            attended.at[t, m],
            back_send.at[m, k],
            back_recv.at[m, k],
            device_id=(f, target),
            device_id_type=MESH,
        )

    for m in range(MICRO):
        for k in range(GROUP - 1):
            letter(k, m).wait_recv()
        result = attend(images[:, m].reshape(GROUP * slot, 384), hidden)
        attended_box[m] = result.reshape(GROUP, slot, 128)
        for k in range(GROUP - 1):
            reply(m, k).start()
        attended[t, m] = attended_box[m, t]
        if m < MICRO - 1:
            for part in wide:
                part.far((1, 2, 3)[2 * m : 2 * m + 2])
    store(images, images_out)
    part_z.last()
    for m in range(MICRO):
        for k in range(GROUP - 1):
            reply(m, k).wait_recv()
    store(attended, attended_out.at[0])
    share(attended, attended_out.at[1])
    part_z.done()
    part_y.last()
    part_x.last()
    middle[...] = rows[...].reshape(count, width) + vectors[2:3, :]

    def out_weights(pair):
        both = [blocks_of(wide_z, 2 * pair + i)[:, 128:] for i in range(2)]
        return jnp.concatenate(both, axis=1)

    def out_project(pair, carry):
        both = [attended[2 * pair + i].reshape(count, 128) for i in range(2)]
        middle[...] += mm(jnp.concatenate(both, axis=1), out_weights(pair), NT)
        return carry

    lax.fori_loop(0, GROUP // 2, out_project, 0)
    normed, inverse = norm_stats(middle[...])
    normed_two[...] = normed
    low_two[...] = (normed * vectors[3:4, :] + vectors[4:5, :]).astype(BF16)
    turn(2, low_two[...])
    forward_sum[...] = jnp.zeros_like(forward_sum)
    back_sum[...] = jnp.zeros_like(back_sum)
    part_y.done()
    part_x.done()

    def copies(i):
        result = []
        for n, (box, out) in enumerate(((act_box, act_out), (dup_box, dup_out))):
            result.append(pltpu.make_async_copy(box.at[i], out.at[0, i], ff_local.at[n, i]))
            result.append(
                pltpu.make_async_remote_copy(
                    box.at[i],
                    out.at[1, i],
                    ff_send.at[n, i],
                    ff_recv.at[n, i],
                    device_id=other,
                    device_id_type=MESH,
                )
            )
        return result

    def feed_forward(i, carry):
        first = blocks_of(wide_y, i)
        up_weight = first[:, :512]
        down_weight = jnp.concatenate(
            [first[:, 512:], blocks_of(wide_x, i), blocks_of(wide_z, i)[:, :128]], axis=1
        )
        up_proj = mm(low_two[...], up_weight) + hidden_bias[i]
        gate = jax.nn.sigmoid(1.702 * up_proj)
        activated = (up_proj * gate).astype(BF16)
        d_act = mm(upstream_low[...], down_weight)
        d_up = (d_act * (gate + 1.702 * up_proj * gate * (1.0 - gate))).astype(BF16)
        for j in range(4):
            act_box[i, count * j : count * (j + 1)] = activated[:, 128 * j : 128 * (j + 1)]
            dup_box[i, count * j : count * (j + 1)] = d_up[:, 128 * j : 128 * (j + 1)]
        for copy in copies(i):
            copy.start()
        hidden_sums[i] = jnp.sum(d_up.astype(F32), 0, keepdims=True)
        forward_sum[...] += mm(activated, down_weight, NT)
        back_sum[...] += mm(d_up, up_weight, NT)
        return carry

    lax.fori_loop(0, GROUP, feed_forward, 0)
    d_norm = back_sum[...]
    normed = normed_two[...]
    d_middle = upstream[...].reshape(count, width) + norm_back(
        d_norm, normed, inverse, vectors[3:4, :]
    )
    d_middle_out[...] = d_middle
    low[...] = d_middle.astype(BF16)

    def project_back(pair, carry):
        both = mm(low[...], out_weights(pair)).astype(BF16)
        for i in range(2):
            d_attended_out[2 * pair + i] = both[:, 128 * i : 128 * i + 128].reshape(
                d_attended_out.shape[1:]
            )
        return carry

    lax.fori_loop(0, GROUP // 2, project_back, 0)
    turn(3, low[...])
    sums_out[0:1, :] = jnp.sum(d_middle, 0, keepdims=True)
    sums_out[1:2, :] = jnp.sum(d_norm * normed, 0, keepdims=True)
    sums_out[2:3, :] = jnp.sum(d_norm, 0, keepdims=True)
    for i in range(GROUP):
        at = 4 + i // 2
        sums_out[at : at + 1, 512 * (i % 2) : 512 * (i % 2) + 512] = hidden_sums[i]
    output = (middle[...] + forward_sum[...] + vectors[5:6, :]).reshape(rows.shape)
    result_out[...] = output[:, :tokens].astype(BF16)
    for copy in shared:
        copy.wait()
    for i in range(GROUP):
        for copy in copies(i):
            copy.wait()
    for part in early + wide:
        part.sent()
    for k in range(GROUP - 1):
        for m in range(MICRO):
            letter(k, m).wait_send()
            reply(m, k).wait_send()
    for copy in stores:
        copy.wait()


ANY = pl.BlockSpec(memory_space=pl.ANY)
VMEM = pl.BlockSpec(memory_space=pltpu.VMEM)
SMEM = pl.BlockSpec(memory_space=pltpu.SMEM)
WIDE = (640, 256, 256)


def forward(x, cotangent, valid, qkv_block, out_block, fc1_block, fc2_block, small, slot):
    width = x.shape[-1]
    count = MICRO * slot
    images = (GROUP, MICRO, slot, 384)
    attended = (GROUP, MICRO, slot, 128)
    acts = (2, GROUP, 4 * count, 128)
    return pl.pallas_call(
        forward_kernel,
        out_shape=[
            jax.ShapeDtypeStruct(x.shape, BF16),
            jax.ShapeDtypeStruct((count, width), F32),
            jax.ShapeDtypeStruct((8, width), F32),
            jax.ShapeDtypeStruct((8, width), F32),
            jax.ShapeDtypeStruct(attended, BF16),
            jax.ShapeDtypeStruct(images, BF16),
            jax.ShapeDtypeStruct((2,) + attended, BF16),
            jax.ShapeDtypeStruct((4, 2, 8, 64, 256), BF16),
            jax.ShapeDtypeStruct(acts, BF16),
            jax.ShapeDtypeStruct(acts, BF16),
            jax.ShapeDtypeStruct((3,) + LEAD + (64, 128), BF16),
        ],
        in_specs=[VMEM, VMEM, SMEM, ANY, VMEM, VMEM, VMEM, ANY],
        out_specs=[VMEM] * 5 + [ANY] * 6,
        scratch_shapes=[
            pltpu.VMEM((MICRO, slot, width), F32),
            pltpu.VMEM((MICRO, slot, width), F32),
            pltpu.VMEM(LEAD + (64, 128), BF16),
            pltpu.VMEM(LEAD + (64, 128), BF16),
            pltpu.VMEM(LEAD + (64, 128), BF16),
            pltpu.VMEM(LEAD + (64, WIDE[0]), BF16),
            pltpu.VMEM(LEAD + (64, WIDE[1]), BF16),
            pltpu.VMEM(LEAD + (64, WIDE[2]), BF16),
            pltpu.VMEM((64, WIDE[0]), BF16),
            pltpu.VMEM((64, WIDE[1]), BF16),
            pltpu.VMEM((64, WIDE[2]), BF16),
            pltpu.VMEM(LEAD + (32, 128), BF16),
            pltpu.VMEM((GROUP, 1, 384), F32),
            pltpu.VMEM((GROUP, 1, 512), F32),
            pltpu.VMEM((count, width), BF16),
            pltpu.VMEM(images, BF16),
            pltpu.VMEM(images, BF16),
            pltpu.VMEM((MICRO, GROUP, slot, 128), BF16),
            pltpu.VMEM(attended, BF16),
            pltpu.VMEM((count, width), F32),
            pltpu.VMEM((count, width), F32),
            pltpu.VMEM((count, width), BF16),
            pltpu.VMEM((count, width), BF16),
            pltpu.VMEM((4, 8, 2, 64, 256), BF16),
            pltpu.VMEM((count, width), F32),
            pltpu.VMEM((count, width), F32),
            pltpu.VMEM(acts[1:], BF16),
            pltpu.VMEM(acts[1:], BF16),
            pltpu.VMEM((GROUP, 1, 512), F32),
            pltpu.SemaphoreType.DMA((8,)),
            pltpu.SemaphoreType.DMA((7, Gather.slots)),
            pltpu.SemaphoreType.DMA((7, Gather.slots)),
            pltpu.SemaphoreType.DMA((GROUP, MICRO)),
            pltpu.SemaphoreType.DMA((GROUP, MICRO)),
            pltpu.SemaphoreType.DMA((MICRO, GROUP)),
            pltpu.SemaphoreType.DMA((MICRO, GROUP)),
            pltpu.SemaphoreType.DMA((9,)),
            pltpu.SemaphoreType.DMA((5,)),
            pltpu.SemaphoreType.DMA((5,)),
            pltpu.SemaphoreType.DMA((2, GROUP)),
            pltpu.SemaphoreType.DMA((2, GROUP)),
            pltpu.SemaphoreType.DMA((2, GROUP)),
        ],
        compiler_params=pltpu.CompilerParams(
            collective_id=0, has_side_effects=True, vmem_limit_bytes=VMEM_LIMIT
        ),
        name="forward",
    )(x, cotangent, valid, qkv_block, out_block, fc1_block, fc2_block, small)


def backward_kernel(*refs):
    (
        d_attended_in,
        images_in,
        attended_in,
        turned_in,
        act_in,
        dup_in,
        qkv_in,
        d_middle_ref,
        x_ref,
        vectors_ref,
        sums_ref,
        input_grad_out,
        qkv_grad,
        out_grad,
        fc1_grad,
        fc2_grad,
        totals_out,
        rows,
        pool,
        turned,
        attended,
        images,
        d_attended,
        outbox,
        d_images,
        d_norm,
        down_grad,
        sums,
        sums_in,
        *rest,
    ) = refs
    scratch, sems = rest[:30], rest[30:]
    (
        load_sem,
        reduce_send,
        reduce_recv,
        send_sem,
        recv_sem,
        back_send,
        back_recv,
        sib_send,
        sib_recv,
        sum_send,
        sum_recv,
    ) = sems
    me = place()
    f, t = lax.axis_index("fsdp"), lax.axis_index("tp")
    other = device_at(sibling(me))
    greet(me)
    tokens, slot = x_ref.shape[1], rows.shape[1]
    count = MICRO * slot
    parts = [
        Reduce(
            me,
            REDUCED[i][0],
            *scratch[5 * i : 5 * i + 5],
            reduce_send.at[i],
            reduce_recv.at[i],
        )
        for i in range(6)
    ]
    part_y, part_x, part_z = parts[:3]
    late = parts[3:]
    totals = [
        Totals(me, sums.at[i], sums_in.at[i], sum_send.at[i], sum_recv.at[i]) for i in range(2)
    ]

    def letter(k, m):
        target = lax.rem(t + k + 1, GROUP)
        return pltpu.make_async_remote_copy(
            d_attended_in.at[target, m],
            d_attended.at[t, m],
            send_sem.at[k, m],
            recv_sem.at[k, m],
            device_id=(f, target),
            device_id_type=MESH,
        )

    for m in range(MICRO):
        for k in range(GROUP - 1):
            letter(k, m).start()
    loads = {}

    def load(name, src, dst):
        loads[name] = pltpu.make_async_copy(src, dst, load_sem.at[len(loads)])
        loads[name].start()

    kept = pl.ds(0, 4 * count)
    load("turned", turned_in, turned)
    for i in range(2):
        load(("dup", i), dup_in.at[i], pool.at[2 + i, :, kept])
    for i in range(2):
        load(("act", i), act_in.at[i], pool.at[i, :, kept])
    load("attended", attended_in, attended)
    load("images", images_in, images)
    load("own", d_attended_in.at[t], d_attended.at[t])
    sums[0, 0] = sums_ref[...]
    totals[0].speak(0)
    loads["turned"].wait()

    def both_cores(kind, values):
        total = 0.0
        for i in range(2):
            left = turned[kind, i].reshape(512, 256)[:, :count]
            total += mm(left, values[i])
        return total.astype(BF16)

    def pooled(first, index, lanes):
        return [
            jnp.concatenate(
                [pool[first + i, index, count * j : count * (j + 1)] for j in lanes], axis=1
            )
            for i in range(2)
        ]

    def spot_of(index):
        return (index // 2, lax.rem(index, 2))

    def grads_y(index, carry):
        up = both_cores(2, pooled(2, index, range(4)))
        down = both_cores(1, pooled(0, index, (0,)))
        acc = part_y.acc
        acc[spot_of(index)] = jnp.concatenate([up, down], axis=1).reshape(acc.shape[2:])
        return carry

    def grads_xz(index, carry):
        down = both_cores(1, pooled(0, index, (1, 2, 3)))
        out = both_cores(3, [attended[i, index].reshape(count, 128) for i in range(2)])
        acc = part_x.acc
        acc[spot_of(index)] = down[:, :256].reshape(acc.shape[2:])
        acc = part_z.acc
        acc[spot_of(index)] = jnp.concatenate([down[:, 256:], out], axis=1).reshape(acc.shape[2:])
        return carry

    for i in range(2):
        loads["dup", i].wait()
        loads["act", i].wait()
    lax.fori_loop(0, GROUP, grads_y, 0)
    part_y.stage_far()
    loads["attended"].wait()
    lax.fori_loop(0, GROUP, grads_xz, 0)
    part_x.stage_far()
    part_z.stage_far()
    for i in range(3):
        load(("weight", i), qkv_in.at[i], pool.at[i])
    totals[0].pass_on(0)
    loads["images"].wait()
    loads["own"].wait()
    hidden = hidden_rows(GROUP * slot, slot, tokens)

    def reply(m, k):
        target = lax.rem(t + k + 1, GROUP)
        return pltpu.make_async_remote_copy(
            outbox.at[m, target],
            d_images.at[0, t, m],
            back_send.at[m, k],
            back_recv.at[m, k],
            device_id=(f, target),
            device_id_type=MESH,
        )

    for m in range(MICRO):
        for k in range(GROUP - 1):
            letter(k, m).wait_recv()
        results = attend_back(
            images[:, m].reshape(GROUP * slot, 384),
            d_attended[:, m].reshape(GROUP * slot, 128),
            hidden,
        )
        for i in range(3):
            outbox[m, :, :, 128 * i : 128 * i + 128] = results[i].reshape(GROUP, slot, 128)
        for k in range(GROUP - 1):
            reply(m, k).start()
        d_images[0, t, m] = outbox[m, t]
        if m == 0:
            part_y.stage_near()
            totals[0].pass_on(1)
        if m == 1:
            totals[0].pass_on(2)
    part_x.stage_near()
    part_z.stage_near()
    padded_rows(x_ref, rows)
    normed, inverse = norm_stats(rows[...].reshape(count, rows.shape[-1]))
    totals[0].hear(3)
    part_y.stage_mid()

    def share(k):
        source = lax.rem(t + k + 1, GROUP)
        return pltpu.make_async_remote_copy(
            d_images.at[0, source],
            d_images.at[1, source],
            sib_send.at[k],
            sib_recv.at[k],
            device_id=other,
            device_id_type=MESH,
        )

    share(GROUP - 1).start()
    for k in reversed(range(GROUP - 1)):
        for m in range(MICRO):
            reply(m, GROUP - 2 - k).wait_recv()
        share(k).start()
    for k in range(GROUP):
        share(k).wait_recv()

    def grads_late(index, carry):
        result = both_cores(0, [d_images[i, index].reshape(count, 384) for i in range(2)])
        for i, part in enumerate(late):
            part.acc[spot_of(index)] = result[:, 128 * i : 128 * i + 128].reshape(
                part.acc.shape[2:]
            )
        return carry

    lax.fori_loop(0, GROUP, grads_late, 0)
    for part in late:
        part.stage_far()
    part_x.stage_mid()
    part_z.stage_mid()
    for i in range(3):
        loads["weight", i].wait()
    d_norm[...] = jnp.zeros_like(d_norm)

    def project_back(index, carry):
        weights = jnp.concatenate([pool[i, index] for i in range(3)], axis=1)
        d_norm[...] += mm(d_images[0, index].reshape(count, 384), weights, NT)
        return carry

    lax.fori_loop(0, GROUP, project_back, 0)
    part_y.stage_tail()
    for part in late:
        part.stage_near()
    gradient = d_norm[...]
    sums[1, 0, 0:1, :] = jnp.sum(gradient * normed, 0, keepdims=True)
    sums[1, 0, 1:2, :] = jnp.sum(gradient, 0, keepdims=True)
    for index in range(GROUP):
        grads = jnp.sum(d_images[0, index].reshape(count, 384).astype(F32), 0, keepdims=True)
        sums[1, 0, 2:3, 128 * index : 128 * index + 128] = grads[:, :128]
        sums[1, 0, 3:4, 128 * index : 128 * index + 128] = grads[:, 256:]
    sums[1, 0, 4:8, :] = jnp.zeros((4, sums.shape[-1]), F32)
    totals[1].speak(0)
    part_x.stage_tail()
    part_z.stage_tail()
    result = d_middle_ref[...] + norm_back(gradient, normed, inverse, vectors_ref[0:1, :])
    input_grad_out[...] = result.reshape(rows.shape)[:, :tokens].astype(BF16)
    totals[1].pass_on(0)
    for part in late:
        part.stage_mid()
    totals[1].pass_on(1)
    wide = part_y.stage_out()
    fc1_grad[...] = wide[:, :512]
    down_grad[:, :128] = wide[:, 512:]
    down_grad[:, 128:384] = part_x.stage_out()
    wide = part_z.stage_out()
    down_grad[:, 384:] = wide[:, :128]
    out_grad[...] = wide[:, 128:].T
    fc2_grad[...] = down_grad[...].T
    for part in late:
        part.stage_tail()
    totals[1].pass_on(2)
    for i in range(3):
        qkv_grad[i] = late[i].stage_out()
    totals[1].hear(3)
    totals_out[0:8, :] = sums[0, 4]
    totals_out[8:16, :] = sums[1, 4]
    for part in parts:
        part.sent()
    for total in totals:
        total.sent()
    for k in range(GROUP):
        share(k).wait_send()
    for k in range(GROUP - 1):
        for m in range(MICRO):
            letter(k, m).wait_send()
            reply(m, k).wait_send()


REDUCED = (
    (ORDERS[2], WIDE[0]),
    (ORDERS[1], WIDE[1]),
    (ORDERS[0], WIDE[2]),
    (ORDERS[0], 128),
    (ORDERS[1], 128),
    (ORDERS[2], 128),
)


def backward(d_attended, images, attended, turned, act, dup, qkv, d_middle, x, vectors, sums, slot):
    width = x.shape[-1]
    count = MICRO * slot
    scratch = []
    for order, lanes in REDUCED:
        scratch += reduce_scratch(order, lanes)
    return pl.pallas_call(
        backward_kernel,
        out_shape=[
            jax.ShapeDtypeStruct(x.shape, BF16),
            jax.ShapeDtypeStruct((3, 64, 128), F32),
            jax.ShapeDtypeStruct((128, 64), F32),
            jax.ShapeDtypeStruct((64, 512), F32),
            jax.ShapeDtypeStruct((512, 64), F32),
            jax.ShapeDtypeStruct((16, width), F32),
        ],
        in_specs=[ANY] * 7 + [VMEM] * 4,
        out_specs=[VMEM] * 6,
        scratch_shapes=[
            pltpu.VMEM((MICRO, slot, width), F32),
            pltpu.VMEM((4, GROUP, width, 128), BF16),
            pltpu.VMEM(turned.shape, BF16),
            pltpu.VMEM(attended.shape, BF16),
            pltpu.VMEM(images.shape, BF16),
            pltpu.VMEM(d_attended.shape, BF16),
            pltpu.VMEM((MICRO, GROUP, slot, 384), BF16),
            pltpu.VMEM((2,) + images.shape, BF16),
            pltpu.VMEM((count, width), F32),
            pltpu.VMEM((64, 512), F32),
            pltpu.VMEM((2, 5, 8, width), F32),
            pltpu.VMEM((2, 4, 3, 8, width), F32),
        ]
        + scratch
        + [
            pltpu.SemaphoreType.DMA((11,)),
            pltpu.SemaphoreType.DMA((6, Reduce.slots)),
            pltpu.SemaphoreType.DMA((6, Reduce.slots)),
            pltpu.SemaphoreType.DMA((GROUP, MICRO)),
            pltpu.SemaphoreType.DMA((GROUP, MICRO)),
            pltpu.SemaphoreType.DMA((MICRO, GROUP)),
            pltpu.SemaphoreType.DMA((MICRO, GROUP)),
            pltpu.SemaphoreType.DMA((GROUP,)),
            pltpu.SemaphoreType.DMA((GROUP,)),
            pltpu.SemaphoreType.DMA((2, 4, 3)),
            pltpu.SemaphoreType.DMA((2, 4, 3)),
        ],
        compiler_params=pltpu.CompilerParams(
            collective_id=1, has_side_effects=True, vmem_limit_bytes=VMEM_LIMIT
        ),
        name="backward",
    )(d_attended, images, attended, turned, act, dup, qkv, d_middle, x, vectors, sums)


def per_device(
    inputs,
    cotangent,
    valid_slots,
    ln1_gain,
    ln1_bias,
    qkv_weight,
    qv_bias,
    out_weight,
    out_bias,
    ln2_gain,
    ln2_bias,
    fc1_weight,
    fc1_bias,
    fc2_weight,
    fc2_bias,
):
    micro, _, tokens, width = inputs.shape
    slot = -(-tokens // 16) * 16
    x = inputs.reshape(micro, tokens, width)
    small = jnp.concatenate(
        [ln1_gain, ln1_bias, out_bias, ln2_gain, ln2_bias, fc2_bias]
        + [qv_bias.reshape(-1), fc1_bias.reshape(-1)]
    )
    small = jnp.pad(small.reshape(1, 96), ((0, 31), (0, 32)))
    (
        result,
        d_middle,
        vectors,
        sums,
        d_attended,
        images,
        attended,
        turned,
        act,
        dup,
        qkv,
    ) = forward(
        x,
        cotangent.reshape(x.shape),
        valid_slots,
        qkv_weight,
        out_weight,
        fc1_weight,
        fc2_weight,
        small,
        slot,
    )
    input_grad, qkv_grad, out_grad, fc1_grad, fc2_grad, total = backward(
        d_attended,
        images,
        attended,
        turned,
        act,
        dup,
        qkv.reshape(3, GROUP, width, 128),
        d_middle,
        x,
        vectors,
        sums,
        slot,
    )
    f, t = lax.axis_index("fsdp"), lax.axis_index("tp")
    own = lax.dynamic_slice(total, (0, (f * 8 + t) * 8), (16, 8))
    pair = lax.dynamic_slice(total[10:12].reshape(2, 16, 64), (0, 2 * t, 4 * f), (2, 2, 4))
    hidden_grad = lax.dynamic_slice(total[4:8].reshape(64, 64), (8 * t, 4 * f), (8, 4))
    return (
        result.reshape(inputs.shape),
        input_grad.reshape(inputs.shape),
        own[8],
        own[9],
        qkv_grad,
        pair,
        out_grad,
        own[0],
        own[1],
        own[2],
        fc1_grad,
        hidden_grad,
        fc2_grad,
        own[3],
    )


def solution(mesh):
    in_specs = (
        P(None, "fsdp", "tp", None),
        P(None, "fsdp", "tp", None),
        P(None, "fsdp"),
        P(("fsdp", "tp")),
        P(("fsdp", "tp")),
        P(None, "fsdp", "tp"),
        P(None, "tp", "fsdp"),
        P("tp", "fsdp"),
        P(("fsdp", "tp")),
        P(("fsdp", "tp")),
        P(("fsdp", "tp")),
        P("fsdp", "tp"),
        P("tp", "fsdp"),
        P("tp", "fsdp"),
        P(("fsdp", "tp")),
    )
    out_specs = (
        P(None, "fsdp", "tp", None),
        P(None, "fsdp", "tp", None),
        P(("fsdp", "tp")),
        P(("fsdp", "tp")),
        P(None, "fsdp", "tp"),
        P(None, "tp", "fsdp"),
        P("tp", "fsdp"),
        P(("fsdp", "tp")),
        P(("fsdp", "tp")),
        P(("fsdp", "tp")),
        P("fsdp", "tp"),
        P("tp", "fsdp"),
        P("tp", "fsdp"),
        P(("fsdp", "tp")),
    )
    return jax.shard_map(
        per_device, mesh=mesh, in_specs=in_specs, out_specs=out_specs, check_vma=False
    )
```

```python
import functools
import math

import jax
import jax.numpy as jnp
from jax import lax
from jax.experimental import pallas as pl
from jax.experimental.pallas import tpu as pltpu
from jax.sharding import PartitionSpec as P

MESH = pl.DeviceIdType.MESH
HD = 64
SCALE = 1.0 / math.sqrt(HD)
EPSILON = 1e-05
BF16 = jnp.bfloat16
F32 = jnp.float32
VMEM_LIMIT = 62 * 2**20
MICRO, GROUP = 3, 8
ORDERS = (("x", "y", "z"), ("y", "z", "x"), ("z", "x", "y"))
SIZES = {"x": (4,), "z": (2, 2), "y": (4,)}
LEAD = (4, 2, 2, 4, 2)
STEPS = (1, -1, 2)
NN = (((1,), (0,)), ((), ()))
NT = (((1,), (1,)), ((), ()))
TN = (((0,), (0,)), ((), ()))


def mm(a, b, dims=NN):
    return lax.dot_general(a, b, dims, preferred_element_type=F32)


def place():
    f, t = lax.axis_index("fsdp"), lax.axis_index("tp")
    return {
        "x": t // 2,
        "y": lax.rem(f // 2, 4),
        "z": (f // 8) * 2 + lax.rem(t, 2),
        "c": lax.rem(f, 2),
    }


def device_at(spot):
    return (
        (spot["z"] // 2) * 8 + spot["y"] * 2 + spot["c"],
        spot["x"] * 2 + lax.rem(spot["z"], 2),
    )


def shifted(spot, axis, by):
    return {**spot, axis: lax.rem(spot[axis] + by + 4, 4)}


def sibling(spot):
    return {**spot, "c": 1 - spot["c"]}


def greet(me):
    f, t = lax.axis_index("fsdp"), lax.axis_index("tp")
    devices = [(f, lax.rem(t + step, GROUP)) for step in range(1, GROUP)]
    devices += [device_at(shifted(me, "y", by)) for by in STEPS]
    devices += [device_at(shifted(me, "z", 2))]
    devices += [device_at(shifted(me, "z", 2 * lax.rem(me["z"], 2) - 1))]
    devices += [device_at(sibling(me))]
    barrier = pltpu.get_barrier_semaphore()
    for device in devices:
        pl.semaphore_signal(barrier, inc=1, device_id=device, device_id_type=MESH)
    return lambda: pl.semaphore_wait(barrier, len(devices))


def view(ref, spot, full, core=None, rows=slice(None)):
    whole = slice(None)
    index = [
        whole if "x" in full else spot["x"],
        whole if "z" in full else lax.rem(spot["z"], 2),
        whole if "z" in full else spot["z"] // 2,
        whole if "y" in full else spot["y"],
    ]
    if core is not None:
        index.append(core)
    return ref.at[tuple(index) + (rows,)]


def decode(number, spot, full):
    at = {}
    for axis in "yzx":
        if axis in full:
            parts = []
            for size in reversed(SIZES[axis]):
                parts.append(lax.rem(number, size))
                number = number // size
            at[axis] = tuple(reversed(parts))
    fixed = {"x": (spot["x"],), "z": (lax.rem(spot["z"], 2), spot["z"] // 2), "y": (spot["y"],)}
    index, inner = (), ()
    for axis in "xzy":
        index += at.get(axis, fixed[axis])
        inner += at.get(axis, ())
    return index, inner


def bundle_shape(full):
    shape = ()
    for axis in "xzy":
        shape += SIZES[axis] if axis in full else ()
    return shape


def remote(src, dst, send, recv, device):
    copy = pltpu.make_async_remote_copy(
        src, dst, send, recv, device_id=device, device_id_type=MESH
    )
    copy.start()
    return copy


def take(ref, semaphore):
    pltpu.make_async_copy(ref, ref, semaphore).wait()


class Gather:
    sends, recvs = 5, 8

    def __init__(self, me, order, block, out, send, recv, local):
        self.me, self.order, self.block, self.out = me, order, block, out
        self.send, self.recv, self.local = send, recv, local
        self.core = me["c"]
        self.half = out.shape[-2] // 2
        self.plane = "".join(order[:2])

    def piece(self, spot, full, rows=slice(None)):
        return view(self.out, spot, full, self.core, rows)

    def spread(self, spot, full, axis, by, send, recv, rows=slice(None)):
        piece = self.piece(spot, full, rows)
        target = device_at(shifted(self.me, axis, by))
        remote(piece, piece, self.send.at[send], self.recv.at[recv], target)

    def share(self, spot):
        piece = self.piece(spot, self.plane)
        remote(piece, piece, self.send.at[4], self.recv.at[7], device_at(sibling(self.me)))

    def own(self):
        return pltpu.make_async_copy(
            self.block, view(self.out, self.me, "", self.core), self.local
        )

    def first(self):
        me, axis = self.me, self.order[0]
        self.own().start()
        for by in STEPS:
            target = device_at(shifted(me, axis, by))
            remote(self.block, self.piece(me, ""), self.send.at[0], self.recv.at[0], target)

    def second(self):
        self.own().wait()
        take(self.out.at[:3, 0, 0, 0, 0], self.recv.at[0])
        for by in STEPS:
            self.spread(self.me, self.order[0], self.order[1], by, 1, 1)

    def rows(self, way):
        return pl.ds(way * self.half, self.half)

    def third(self):
        take(self.out.at[:3, 0, 0, :, 0], self.recv.at[1])
        axis = self.order[2]
        for number, (by, way) in enumerate(((1, 0), (-1, 1), (1, 1), (-1, 0))):
            self.spread(self.me, self.plane, axis, by, 2, 2 + number, self.rows(way))
        self.share(self.me)

    def far(self):
        axis = self.order[2]
        for way, by in enumerate((1, -1)):
            take(self.out.at[:, 0, 0, :, 0, : self.half], self.recv.at[2 + way])
            spot = shifted(self.me, axis, -by)
            self.spread(spot, self.plane, axis, by, 3, 6, self.rows(way))

    def rest(self):
        for way, by in enumerate((1, -1)):
            take(self.out.at[:, 0, 0, :, 0, : self.half], self.recv.at[4 + way])
            self.share(shifted(self.me, self.order[2], -by))

    def last(self):
        take(self.out.at[:, 0, 0, :, 0], self.recv.at[6])
        self.share(shifted(self.me, self.order[2], 2))

    def done(self):
        take(self.out.at[:, :, :, :, 0], self.recv.at[7])

    def sent(self):
        out = self.out
        take(out.at[:3, 0, 0, 0, 0], self.send.at[0])
        take(out.at[:3, 0, 0, :, 0], self.send.at[1])
        take(out.at[:, :, 0, :, 0], self.send.at[2])
        take(out.at[:, 0, 0, :, 0], self.send.at[3])
        take(out.at[:, :, :, :, 0], self.send.at[4])


class Reduce:
    sends, recvs = 4, 5

    def __init__(self, me, order, acc, near, far, mid, tail, send, recv):
        self.me, self.order, self.acc = me, order, acc
        self.nears, self.fars, self.mid, self.tail = near, far, mid, tail
        self.send, self.recv = send, recv
        self.half = acc.shape[-2] // 2
        self.full = "".join(order[:2])

    def chunk(self, by):
        return shifted(self.me, self.order[2], by)

    def rows(self, way):
        return pl.ds(way * self.half, self.half)

    def add(self, spot, full, first, rows, terms):
        acc = self.acc

        def one(number, carry):
            index, inner = decode(number, spot, full)
            here = index + (pl.ds(first, rows),)
            total = acc[here]
            if len(terms) > 1:
                total = total.astype(F32)
            for ref, lead in terms:
                rows_there = pl.ds(first, rows) if ref.shape[-2] == acc.shape[-2] else slice(None)
                total += ref[(lead,) + inner + (rows_there,)].astype(total.dtype)
            acc[here] = total.astype(acc.dtype)
            return carry

        lax.fori_loop(0, math.prod(bundle_shape(full)), one, 0)

    def near(self, by, way):
        spot = self.chunk(by)
        box = self.nears.at[0 if by == 1 else 1]
        lead = (slice(None),) * (len(self.nears.shape) - 3)
        remote(
            view(self.acc, spot, self.full, None, self.rows(way)),
            box.at[lead + (self.rows(way),)],
            self.send.at[1],
            self.recv.at[2],
            device_at(spot),
        )

    def stage_far(self):
        spot = self.chunk(2)
        for way, by in enumerate((1, -1)):
            remote(
                view(self.acc, spot, self.full, None, self.rows(way)),
                self.fars.at[way],
                self.send.at[0],
                self.recv.at[way],
                device_at(self.chunk(by)),
            )
        for way, by in enumerate((1, -1)):
            self.near(by, 1 - way)

    def stage_near(self):
        for way, by in enumerate((1, -1)):
            take(self.fars.at[way], self.recv.at[way])
            self.add(self.chunk(by), self.full, way * self.half, self.half, [(self.fars, way)])
            self.near(by, way)

    def spread(self, axis, full, target, send, recv):
        for number, by in enumerate(STEPS):
            spot = shifted(self.me, axis, by)
            remote(
                view(self.acc, spot, full),
                target.at[number],
                self.send.at[send],
                self.recv.at[recv],
                device_at(spot),
            )

    def stage_mid(self):
        take(self.nears, self.recv.at[2])
        self.add(self.me, self.full, 0, 2 * self.half, [(self.nears, 0), (self.nears, 1)])
        self.spread(self.order[1], self.order[0], self.mid, 2, 3)

    def stage_tail(self):
        take(self.mid, self.recv.at[3])
        self.add(self.me, self.order[0], 0, 2 * self.half, [(self.mid, i) for i in range(3)])
        self.spread(self.order[0], "", self.tail, 3, 4)

    def stage_out(self):
        take(self.tail, self.recv.at[4])
        index, _ = decode(0, self.me, "")
        total = self.acc[index].astype(F32)
        for number in range(3):
            total += self.tail[number].astype(F32)
        return total

    def sent(self):
        take(self.fars, self.send.at[0])
        take(self.nears, self.send.at[1])
        take(self.mid, self.send.at[2])
        take(self.tail, self.send.at[3])


def reduce_scratch(order, lanes):
    full = bundle_shape(order[:2])
    return [
        pltpu.VMEM((4, 2, 2, 4, 64, lanes), BF16),
        pltpu.VMEM((2,) + full + (64, lanes), BF16),
        pltpu.VMEM((2,) + full + (32, lanes), BF16),
        pltpu.VMEM((3,) + bundle_shape(order[:1]) + (64, lanes), BF16),
        pltpu.VMEM((3, 64, lanes), BF16),
    ]


class Totals:
    def __init__(self, me, sums, inbox, send, recv):
        self.rounds = [[shifted(me, axis, by) for by in STEPS] for axis in "xyz"] + [[sibling(me)]]
        self.sums, self.inbox, self.send, self.recv = sums, inbox, send, recv

    def heard(self, number):
        return self.inbox.at[number, pl.ds(0, len(self.rounds[number]))]

    def speak(self, number):
        for i, spot in enumerate(self.rounds[number]):
            remote(
                self.sums.at[number],
                self.inbox.at[number, i],
                self.send.at[number],
                self.recv.at[number],
                device_at(spot),
            )

    def hear(self, number):
        take(self.heard(number), self.recv.at[number])
        total = self.sums[number]
        for i in range(len(self.rounds[number])):
            total += self.inbox[number, i]
        self.sums[number + 1] = total

    def pass_on(self, number):
        self.hear(number)
        self.speak(number + 1)

    def sent(self):
        for number in range(4):
            take(self.heard(number), self.send.at[number])


def norm_stats(values):
    average = jnp.mean(values, -1, keepdims=True)
    centered = values - average
    inverse = lax.rsqrt(jnp.mean(centered * centered, -1, keepdims=True) + EPSILON)
    return (centered * inverse, inverse)


def norm_back(upstream, normed, inverse, gain_vector):
    scaled = upstream * gain_vector
    return inverse * (
        scaled
        - jnp.mean(scaled, -1, keepdims=True)
        - normed * jnp.mean(scaled * normed, -1, keepdims=True)
    )


def softmax_columns(key_rows, queries, hidden):
    scores = mm(key_rows, queries, NT) + hidden
    powers = jnp.exp((scores - jnp.max(scores, 0, keepdims=True)) * SCALE)
    return powers * (1.0 / jnp.sum(powers, 0, keepdims=True))


def hidden_rows(seq, slot, tokens):
    row = lax.broadcasted_iota(jnp.int32, (seq, 1), 0)
    return jnp.where(lax.rem(row, slot) < tokens, 0.0, -1e30)


def head_lanes(head):
    lane = lax.broadcasted_iota(jnp.int32, (1, 128), 1)
    return jnp.where(lane // HD == head, 1.0, 0.0).astype(BF16)


def thirds(rows):
    return [rows[:, 128 * i : 128 * i + 128] for i in range(3)]


def attend(rows, hidden):
    queries, key_rows, value_rows = thirds(rows)

    def one_head(head, before):
        mine = head_lanes(head)
        probs = softmax_columns(key_rows, queries * mine, hidden).astype(BF16)
        return before + mm(probs, value_rows * mine, TN)

    return lax.fori_loop(0, 2, one_head, jnp.zeros(queries.shape, F32)).astype(BF16)


def attend_back(rows, grads, hidden):
    queries, key_rows, value_rows = thirds(rows)

    def one_head(head, before):
        mine = head_lanes(head)
        own_grads, own_queries = grads * mine, queries * mine
        probs = softmax_columns(key_rows, own_queries, hidden)
        d_probs = mm(value_rows, own_grads, NT)
        inner = jnp.sum(probs * d_probs, 0, keepdims=True)
        d_scores = (probs * (d_probs - inner)).astype(BF16)
        return (
            before[0] + mm(d_scores, key_rows * mine, TN),
            before[1] + mm(d_scores, own_queries),
            before[2] + mm(probs.astype(BF16), own_grads),
        )

    zero = jnp.zeros(queries.shape, F32)
    d_queries, d_keys, d_values = lax.fori_loop(0, 2, one_head, (zero, zero, zero))
    return [
        (d_queries * SCALE).astype(BF16),
        (d_keys * SCALE).astype(BF16),
        d_values.astype(BF16),
    ]


def padded_rows(ref, target):
    micro, tokens, width = ref.shape
    for m in range(micro):
        target[m, :tokens] = ref[m].astype(F32)
        target[m, tokens:] = jnp.zeros((target.shape[1] - tokens, width), F32)


def blocks_of(ref, index):
    value = ref[index // 2, lax.rem(index, 2)]
    return value.reshape(-1, value.shape[-1])


def half_planes(ref, value, kind, count):
    padded = jnp.concatenate(
        [value, jnp.zeros((ref.shape[-1] - count, value.shape[1]), value.dtype)], axis=0
    )
    ref[kind] = padded.T.reshape(ref.shape[1:])


def forward_kernel(*refs):
    (x_ref, cot_ref, valid_ref, qkv_in, out_in, fc1_in, fc2_in), refs = refs[:7], refs[7:]
    small_in, refs = refs[:8], refs[8:]
    (
        result_out,
        d_middle_out,
        vectors,
        sums_out,
        d_attended_out,
        images_out,
        attended_out,
        turned_out,
        act_out,
        qkv_out,
        rows,
        upstream,
        wq,
        wk,
        wv,
        up_a,
        up_b,
        down_xa,
        down_za,
        down_xb,
        down_zb,
        up_own,
        small_own,
        small,
        bias,
        hidden_bias,
        low,
        outbox,
        images,
        attended_box,
        attended,
        middle,
        normed_two,
        low_two,
        upstream_low,
        turned,
        forward_sum,
        back_sum,
        act_box,
        d_outbox,
        hidden_sums,
        local_sem,
        gather_send,
        gather_recv,
        send_sem,
        recv_sem,
        back_send,
        back_recv,
        store_sem,
        sib_send,
        sib_recv,
        ff_local,
        ff_send,
        ff_recv,
        call_send,
        call_recv,
    ) = refs
    me = place()
    f, t = lax.axis_index("fsdp"), lax.axis_index("tp")
    core = me["c"]
    other = device_at(sibling(me))
    micro, tokens, width = x_ref.shape
    slot = rows.shape[1]
    count = micro * slot
    met = greet(me)
    heads = [wq, wk, wv]
    made = []

    def gather(order, block, out):
        i = len(made)
        made.append(
            Gather(me, order, block, out, gather_send.at[i], gather_recv.at[i], local_sem.at[i])
        )
        return made[-1]

    narrow = [gather(ORDERS[i], qkv_in.at[i], heads[i]) for i in range(3)]
    vector = gather(ORDERS[0], small_own, small)
    early = [vector] + narrow
    first_half = [
        gather(ORDERS[2], up_own, up_a),
        gather(ORDERS[1], fc2_in.at[:, :128], down_xa),
        gather(ORDERS[0], fc2_in.at[:, 128:256], down_za),
    ]
    second_half = [
        gather(ORDERS[2], fc1_in.at[:, 256:], up_b),
        gather(ORDERS[1], fc2_in.at[:, 256:384], down_xb),
        gather(ORDERS[0], fc2_in.at[:, 384:], down_zb),
    ]
    stores = []

    def store(src, dst):
        copy = pltpu.make_async_copy(src, dst, store_sem.at[len(stores)])
        copy.start()
        stores.append(copy)

    shared = []

    def share(src, dst):
        slot_of = len(shared)
        copy = pltpu.make_async_remote_copy(
            src,
            dst,
            sib_send.at[slot_of],
            sib_recv.at[slot_of],
            device_id=other,
            device_id_type=MESH,
        )
        copy.start()
        shared.append(copy)

    def turn(kind, value):
        half_planes(turned, value, kind, count)
        store(turned.at[kind, :, core], turned_out.at[kind, 0])
        share(turned.at[kind, :, 1 - core], turned_out.at[kind, 1])

    padded_rows(x_ref, rows)
    up_own[:, :128] = out_in[...]
    up_own[:, 128:] = fc1_in[:, :256]
    small_own[...] = jnp.zeros_like(small_own)
    for v in range(6):
        small_own[0:1, 8 * v : 8 * v + 8] = small_in[v][...]
    for i in range(2):
        for j in range(2):
            at = 48 + 8 * i + 4 * j
            small_own[0:1, at : at + 4] = small_in[6][i, j : j + 1]
    for i in range(4):
        small_own[0:1, 64 + 8 * i : 72 + 8 * i] = small_in[7][i : i + 1]
    met()
    for part in early:
        part.first()
    normed, _ = norm_stats(rows[...].reshape(count, width))
    for part in first_half:
        part.first()
    for part in early:
        part.second()
    for part in second_half:
        part.first()
    for part in early:
        part.third()
    for part in first_half:
        part.second()
    for part in early:
        part.far()
    for part in first_half:
        part.third()
    vector.rest()
    vector.last()
    vector.done()
    table = jnp.sum(small[...].reshape(128, 32, 128).astype(F32), 1).astype(BF16)
    lane = lax.broadcasted_iota(jnp.int32, (128, 1024), 0)
    column = lax.broadcasted_iota(jnp.int32, (128, 1024), 1)
    owner = jnp.where(lax.rem(lane, 16) * 8 + lane // 16 == column // 8, 1.0, 0.0)
    for v in range(6):
        pick = jnp.where(lane == v * 8 + lax.rem(column, 8), 1.0, 0.0).astype(BF16)
        vectors[v : v + 1, :] = jnp.sum(mm(table, pick) * owner, 0, keepdims=True)
    vectors[6:8, :] = jnp.zeros((2, 1024), F32)

    def spread_bias(lanes, first, major, minor):
        lane = lax.broadcasted_iota(jnp.int32, (128, lanes), 0)
        column = lax.broadcasted_iota(jnp.int32, (128, lanes), 1)
        pick = lane == first + (column // 64) * major + lax.rem(column, 4) * minor
        owner = lax.rem(lane, 16) == lax.rem(column, 64) // 4
        values = mm(table, jnp.where(pick, 1.0, 0.0).astype(BF16))
        return jnp.sum(jnp.where(owner, values, 0.0).reshape(8, 16, lanes), 1)

    hidden_value = spread_bias(512, 64, 1, 8)
    query_bias, value_bias = spread_bias(128, 48, 4, 1), spread_bias(128, 56, 4, 1)
    for i in range(GROUP):
        hidden_bias[i] = hidden_value[i : i + 1]
        bias[i, :, 0:128] = query_bias[i : i + 1]
        bias[i, :, 128:256] = jnp.zeros((1, 128), F32)
        bias[i, :, 256:384] = value_bias[i : i + 1]
    low[...] = (normed * vectors[0:1, :] + vectors[1:2, :]).astype(BF16)
    for part in second_half:
        part.second()
    for part in narrow:
        part.rest()
    for part in narrow:
        part.last()
    for part in first_half:
        part.far()
    for part in narrow:
        part.done()

    def letter(k, m):
        target = lax.rem(t + k + 1, GROUP)
        return pltpu.make_async_remote_copy(
            outbox.at[target, m],
            images.at[t, m],
            send_sem,
            recv_sem.at[m],
            device_id=(f, target),
            device_id_type=MESH,
        )

    def project(k, carry):
        target = lax.rem(t + k + 1, GROUP)
        weights = jnp.concatenate([blocks_of(w, target) for w in heads], axis=1)
        result = (mm(low[...], weights) + bias[target]).astype(BF16)
        outbox[target] = result.reshape(outbox.shape[1:])

        @pl.when(k < GROUP - 1)
        def _():
            letter(k, 0).start()

        return carry

    lax.fori_loop(0, GROUP, project, 0)
    for m in range(1, MICRO):
        for k in range(GROUP - 1):
            letter(k, m).start()
    own = pltpu.make_async_copy(outbox.at[t], images.at[t], local_sem.at[len(made)])
    own.start()
    for i in range(3):
        store(heads[i], qkv_out.at[i])
    for part in second_half:
        part.third()
    turn(0, low[...])
    for m in range(micro):
        scale = valid_ref[0, m].astype(F32)
        upstream[m, :tokens] = cot_ref[m].astype(F32) * scale
        upstream[m, tokens:] = jnp.zeros((slot - tokens, width), F32)
    upstream_rows = upstream[...].reshape(count, width)
    sums_out[3:4, :] = jnp.sum(upstream_rows, 0, keepdims=True)
    upstream_low[...] = upstream_rows.astype(BF16)
    turn(1, upstream_low[...])
    own.wait()
    hidden = hidden_rows(GROUP * slot, slot, tokens)

    def reply(m, k):
        target = lax.rem(t + k + 1, GROUP)
        return pltpu.make_async_remote_copy(
            attended_box.at[m, target],
            attended.at[t, m],
            back_send,
            back_recv,
            device_id=(f, target),
            device_id_type=MESH,
        )

    for m in range(MICRO):
        take(images.at[: GROUP - 1, m], recv_sem.at[m])
        result = attend(images[:, m].reshape(GROUP * slot, 384), hidden)
        attended_box[m] = result.reshape(GROUP, slot, 128)
        for k in range(GROUP - 1):
            reply(m, k).start()
        attended[t, m] = attended_box[m, t]
        if m == 0:
            for part in first_half:
                part.rest()
            for part in second_half:
                part.far()
        if m == 1:
            for part in first_half:
                part.last()
    store(images, images_out)
    for part in second_half:
        part.rest()
    take(attended.at[: GROUP - 1], back_recv)
    store(attended, attended_out.at[0])
    share(attended, attended_out.at[1])
    for part in first_half:
        part.done()
    middle[...] = rows[...].reshape(count, width) + vectors[2:3, :]

    def out_weights(pair):
        both = [blocks_of(up_a, 2 * pair + i)[:, :128] for i in range(2)]
        return jnp.concatenate(both, axis=1)

    def out_project(pair, carry):
        both = [attended[2 * pair + i].reshape(count, 128) for i in range(2)]
        middle[...] += mm(jnp.concatenate(both, axis=1), out_weights(pair), NT)
        return carry

    lax.fori_loop(0, GROUP // 2, out_project, 0)
    normed, inverse = norm_stats(middle[...])
    normed_two[...] = normed
    low_two[...] = (normed * vectors[3:4, :] + vectors[4:5, :]).astype(BF16)
    turn(2, low_two[...])
    forward_sum[...] = jnp.zeros_like(forward_sum)
    back_sum[...] = jnp.zeros_like(back_sum)

    def ship(pair, h):
        piece = act_box.at[pl.ds(2 * pair, 2), :, pl.ds(2 * count * h, 2 * count)]
        at = (pl.ds(2 * pair, 2), slice(None), pl.ds(2 * count * h, 2 * count))
        pltpu.make_async_copy(piece, act_out.at[(0,) + at], ff_local).start()
        remote(piece, act_out.at[(1,) + at], ff_send, ff_recv, other)

    for h in range(2):
        if h == 1:
            for part in second_half:
                part.last()
            for part in second_half:
                part.done()

        def feed_forward(i, carry):
            up_weight = blocks_of(up_a, i)[:, 128:] if h == 0 else blocks_of(up_b, i)
            down_weight = jnp.concatenate(
                [blocks_of((down_xa, down_xb)[h], i), blocks_of((down_za, down_zb)[h], i)], axis=1
            )
            up_proj = mm(low_two[...], up_weight) + hidden_bias[i, :, 256 * h : 256 * h + 256]
            gate = jax.nn.sigmoid(1.702 * up_proj)
            activated = (up_proj * gate).astype(BF16)
            d_act = mm(upstream_low[...], down_weight)
            d_up = (d_act * (gate + 1.702 * up_proj * gate * (1.0 - gate))).astype(BF16)
            for j in range(2):
                at = pl.ds(count * (2 * h + j), count)
                act_box[i, 0, at] = activated[:, 128 * j : 128 * (j + 1)]
                act_box[i, 1, at] = d_up[:, 128 * j : 128 * (j + 1)]

            @pl.when(lax.rem(i, 2) == 1)
            def _():
                ship(i // 2, h)

            hidden_sums[i, :, 256 * h : 256 * h + 256] = jnp.sum(
                d_up.astype(F32), 0, keepdims=True
            )
            forward_sum[...] += mm(activated, down_weight, NT)
            back_sum[...] += mm(d_up, up_weight, NT)
            return carry

        lax.fori_loop(0, GROUP, feed_forward, 0)
    d_norm = back_sum[...]
    normed = normed_two[...]
    d_middle = upstream[...].reshape(count, width) + norm_back(
        d_norm, normed, inverse, vectors[3:4, :]
    )
    d_middle_out[...] = d_middle
    low[...] = d_middle.astype(BF16)

    def call(k):
        target = lax.rem(t + k + 1, GROUP)
        return pltpu.make_async_remote_copy(
            d_outbox.at[target],
            d_attended_out.at[t],
            call_send,
            call_recv,
            device_id=(f, target),
            device_id_type=MESH,
        )

    def project_back(pair, carry):
        both = mm(low[...], out_weights(pair)).astype(BF16)
        for i in range(2):
            d_outbox[2 * pair + i] = both[:, 128 * i : 128 * i + 128].reshape(d_outbox.shape[1:])
        return carry

    lax.fori_loop(0, GROUP // 2, project_back, 0)
    for k in range(GROUP - 1):
        call(k).start()
    store(d_outbox.at[t], d_attended_out.at[t])
    turn(3, low[...])
    sums_out[0:1, :] = jnp.sum(d_middle, 0, keepdims=True)
    sums_out[1:2, :] = jnp.sum(d_norm * normed, 0, keepdims=True)
    sums_out[2:3, :] = jnp.sum(d_norm, 0, keepdims=True)
    for i in range(GROUP):
        at = 4 + i // 2
        sums_out[at : at + 1, 512 * (i % 2) : 512 * (i % 2) + 512] = hidden_sums[i]
    output = (middle[...] + forward_sum[...] + vectors[5:6, :]).reshape(rows.shape)
    result_out[...] = output[:, :tokens].astype(BF16)
    for copy in shared:
        copy.wait()
    take(act_box, ff_local)
    take(act_box, ff_send)
    take(act_box, ff_recv)
    for part in made:
        part.sent()
    take(outbox.at[: GROUP - 1], send_sem)
    take(attended_box.at[:, : GROUP - 1], back_send)
    take(d_outbox.at[: GROUP - 1], call_send)
    take(d_outbox.at[: GROUP - 1], call_recv)
    for copy in stores:
        copy.wait()


ANY = pl.BlockSpec(memory_space=pl.ANY)
VMEM = pl.BlockSpec(memory_space=pltpu.VMEM)
SMEM = pl.BlockSpec(memory_space=pltpu.SMEM)


def forward(x, cotangent, valid, qkv_block, out_block, fc1_block, fc2_block, small, slot):
    width = x.shape[-1]
    count = MICRO * slot
    images = (GROUP, MICRO, slot, 384)
    attended = (GROUP, MICRO, slot, 128)
    acts = (2, GROUP, 2, 4 * count, 128)
    return pl.pallas_call(
        forward_kernel,
        out_shape=[
            jax.ShapeDtypeStruct(x.shape, BF16),
            jax.ShapeDtypeStruct((count, width), F32),
            jax.ShapeDtypeStruct((8, width), F32),
            jax.ShapeDtypeStruct((8, width), F32),
            jax.ShapeDtypeStruct(attended, BF16),
            jax.ShapeDtypeStruct(images, BF16),
            jax.ShapeDtypeStruct((2,) + attended, BF16),
            jax.ShapeDtypeStruct((4, 2, 8, 64, 256), BF16),
            jax.ShapeDtypeStruct(acts, BF16),
            jax.ShapeDtypeStruct((3,) + LEAD + (64, 128), BF16),
        ],
        in_specs=[VMEM, VMEM, SMEM, ANY, VMEM, VMEM, ANY] + [VMEM] * 8,
        out_specs=[VMEM] * 4 + [ANY] * 6,
        scratch_shapes=[
            pltpu.VMEM((MICRO, slot, width), F32),
            pltpu.VMEM((MICRO, slot, width), F32),
            pltpu.VMEM(LEAD + (64, 128), BF16),
            pltpu.VMEM(LEAD + (64, 128), BF16),
            pltpu.VMEM(LEAD + (64, 128), BF16),
            pltpu.VMEM(LEAD + (64, 384), BF16),
            pltpu.VMEM(LEAD + (64, 256), BF16),
            pltpu.VMEM(LEAD + (64, 128), BF16),
            pltpu.VMEM(LEAD + (64, 128), BF16),
            pltpu.VMEM(LEAD + (64, 128), BF16),
            pltpu.VMEM(LEAD + (64, 128), BF16),
            pltpu.VMEM((64, 384), BF16),
            pltpu.VMEM((32, 128), BF16),
            pltpu.VMEM(LEAD + (32, 128), BF16),
            pltpu.VMEM((GROUP, 1, 384), F32),
            pltpu.VMEM((GROUP, 1, 512), F32),
            pltpu.VMEM((count, width), BF16),
            pltpu.VMEM(images, BF16),
            pltpu.VMEM(images, BF16),
            pltpu.VMEM((MICRO, GROUP, slot, 128), BF16),
            pltpu.VMEM(attended, BF16),
            pltpu.VMEM((count, width), F32),
            pltpu.VMEM((count, width), F32),
            pltpu.VMEM((count, width), BF16),
            pltpu.VMEM((count, width), BF16),
            pltpu.VMEM((4, 8, 2, 64, 256), BF16),
            pltpu.VMEM((count, width), F32),
            pltpu.VMEM((count, width), F32),
            pltpu.VMEM(acts[1:], BF16),
            pltpu.VMEM(attended, BF16),
            pltpu.VMEM((GROUP, 1, 512), F32),
            pltpu.SemaphoreType.DMA((12,)),
            pltpu.SemaphoreType.DMA((10, Gather.sends)),
            pltpu.SemaphoreType.DMA((10, Gather.recvs)),
            pltpu.SemaphoreType.DMA,
            pltpu.SemaphoreType.DMA((MICRO,)),
            pltpu.SemaphoreType.DMA,
            pltpu.SemaphoreType.DMA,
            pltpu.SemaphoreType.DMA((10,)),
            pltpu.SemaphoreType.DMA((5,)),
            pltpu.SemaphoreType.DMA((5,)),
            pltpu.SemaphoreType.DMA,
            pltpu.SemaphoreType.DMA,
            pltpu.SemaphoreType.DMA,
            pltpu.SemaphoreType.DMA,
            pltpu.SemaphoreType.DMA,
        ],
        compiler_params=pltpu.CompilerParams(
            collective_id=0, has_side_effects=True, vmem_limit_bytes=VMEM_LIMIT
        ),
        name="forward",
    )(x, cotangent, valid, qkv_block, out_block, fc1_block, fc2_block, *small)


def backward_kernel(*refs):
    (
        d_attended_in,
        images_in,
        attended_in,
        turned_in,
        act_in,
        qkv_in,
        d_middle_ref,
        x_ref,
        vectors_ref,
        sums_ref,
        input_grad_out,
        qkv_grad,
        out_grad,
        fc1_grad,
        fc2_grad,
        totals_out,
        rows,
        pool,
        turned,
        attended,
        images,
        d_attended,
        outbox,
        d_images,
        d_norm,
        sums,
        sums_in,
        *rest,
    ) = refs
    scratch, sems = rest[: 5 * len(REDUCED)], rest[5 * len(REDUCED) :]
    (
        load_sem,
        reduce_send,
        reduce_recv,
        back_send,
        back_recv,
        sib_send,
        sib_recv,
        sum_send,
        sum_recv,
    ) = sems
    me = place()
    f, t = lax.axis_index("fsdp"), lax.axis_index("tp")
    other = device_at(sibling(me))
    met = greet(me)
    tokens, slot = x_ref.shape[1], rows.shape[1]
    count = MICRO * slot
    parts = [
        Reduce(
            me,
            REDUCED[i][0],
            *scratch[5 * i : 5 * i + 5],
            reduce_send.at[i],
            reduce_recv.at[i],
        )
        for i in range(len(REDUCED))
    ]
    late = parts[-3:]
    wide = parts[:-3]
    totals = [
        Totals(me, sums.at[i], sums_in.at[i], sum_send.at[i], sum_recv.at[i]) for i in range(2)
    ]
    loads = {}

    def load(name, src, dst):
        loads[name] = pltpu.make_async_copy(src, dst, load_sem.at[len(loads)])
        loads[name].start()

    kept = pl.ds(0, 4 * count)
    load("turned", turned_in, turned)
    for i in range(2):
        load(("dup", i), act_in.at[i, :, 1], pool.at[2 + i, :, kept])
    load("images", images_in, images)
    load("d_attended", d_attended_in, d_attended)
    for i in range(2):
        load(("act", i), act_in.at[i, :, 0], pool.at[i, :, kept])
    load("attended", attended_in, attended)
    sums[0, 0] = sums_ref[...]

    def both_cores(kind, values):
        total = 0.0
        for i in range(2):
            left = turned[kind, i].reshape(512, 256)[:, :count]
            total += mm(left, values[i])
        return total.astype(BF16)

    def pooled(first, index, lanes):
        return [
            jnp.concatenate(
                [pool[first + i, index, count * j : count * (j + 1)] for j in lanes], axis=1
            )
            for i in range(2)
        ]

    def spot_of(index):
        return (index // 2, lax.rem(index, 2))

    def fill(part, index, lanes, value):
        acc = part.acc
        acc[spot_of(index) + (slice(None),) * 3 + (lanes,)] = value.reshape(
            acc.shape[2:-1] + (value.shape[-1],)
        )

    def grads_up(half):
        def one(index, carry):
            value = both_cores(2, pooled(2, index, (2 * half, 2 * half + 1)))
            fill(wide[half], index, slice(0, 256), value)
            return carry

        return one

    def grads_down(index, carry):
        value = both_cores(1, pooled(0, index, range(4)))
        fill(wide[2], index, slice(0, 128), value[:, :128])
        fill(wide[3], index, slice(0, 256), value[:, 128:384])
        fill(wide[4], index, slice(0, 128), value[:, 384:])
        value = both_cores(3, [attended[i, index].reshape(count, 128) for i in range(2)])
        fill(wide[4], index, slice(128, 256), value)
        return carry

    loads["turned"].wait()
    for i in range(2):
        loads["dup", i].wait()
    lax.fori_loop(0, GROUP, grads_up(0), 0)
    met()
    wide[0].stage_far()
    totals[0].speak(0)
    lax.fori_loop(0, GROUP, grads_up(1), 0)
    wide[1].stage_far()
    loads["images"].wait()
    loads["d_attended"].wait()
    hidden = hidden_rows(GROUP * slot, slot, tokens)

    def reply(m, k):
        target = lax.rem(t + k + 1, GROUP)
        return pltpu.make_async_remote_copy(
            outbox.at[m, target],
            d_images.at[0, t, m],
            back_send,
            back_recv.at[k],
            device_id=(f, target),
            device_id_type=MESH,
        )

    for m in range(MICRO):
        results = attend_back(
            images[:, m].reshape(GROUP * slot, 384),
            d_attended[:, m].reshape(GROUP * slot, 128),
            hidden,
        )
        for i in range(3):
            outbox[m, :, :, 128 * i : 128 * i + 128] = results[i].reshape(GROUP, slot, 128)
        for k in range(GROUP - 1):
            reply(m, k).start()
        d_images[0, t, m] = outbox[m, t]
        if m == 0:
            for i in range(2):
                loads["act", i].wait()
            loads["attended"].wait()
            lax.fori_loop(0, GROUP, grads_down, 0)
            for part in wide[2:]:
                part.stage_far()
            for i in range(3):
                load(("weight", i), qkv_in.at[i], pool.at[i])
            wide[0].stage_near()
            totals[0].pass_on(0)
        if m == 1:
            wide[1].stage_near()
            totals[0].pass_on(1)
    for part in wide[2:]:
        part.stage_near()
    padded_rows(x_ref, rows)
    normed, inverse = norm_stats(rows[...].reshape(count, rows.shape[-1]))
    totals[0].pass_on(2)
    wide[0].stage_mid()

    def share(k):
        source = lax.rem(t + k + 1, GROUP)
        remote(d_images.at[0, source], d_images.at[1, source], sib_send, sib_recv, other)

    share(GROUP - 1)
    for k in reversed(range(GROUP - 1)):
        take(d_images.at[0, 0], back_recv.at[GROUP - 2 - k])
        share(k)
    wide[1].stage_mid()
    take(d_images.at[1], sib_recv)

    def grads_late(index, carry):
        value = both_cores(0, [d_images[i, index].reshape(count, 384) for i in range(2)])
        for i, part in enumerate(late):
            fill(part, index, slice(None), value[:, 128 * i : 128 * i + 128])
        return carry

    lax.fori_loop(0, GROUP, grads_late, 0)
    for part in late:
        part.stage_far()
    for part in wide[2:]:
        part.stage_mid()
    for i in range(3):
        loads["weight", i].wait()
    d_norm[...] = jnp.zeros_like(d_norm)

    def project_back(index, carry):
        weights = jnp.concatenate([pool[i, index] for i in range(3)], axis=1)
        d_norm[...] += mm(d_images[0, index].reshape(count, 384), weights, NT)
        return carry

    lax.fori_loop(0, GROUP, project_back, 0)
    for part in late:
        part.stage_near()
    for part in wide[:2]:
        part.stage_tail()
    gradient = d_norm[...]
    sums[1, 0, 0:1, :] = jnp.sum(gradient * normed, 0, keepdims=True)
    sums[1, 0, 1:2, :] = jnp.sum(gradient, 0, keepdims=True)
    for index in range(GROUP):
        grads = jnp.sum(d_images[0, index].reshape(count, 384).astype(F32), 0, keepdims=True)
        sums[1, 0, 2:3, 128 * index : 128 * index + 128] = grads[:, :128]
        sums[1, 0, 3:4, 128 * index : 128 * index + 128] = grads[:, 256:]
    sums[1, 0, 4:8, :] = jnp.zeros((4, sums.shape[-1]), F32)
    totals[1].speak(0)
    totals[0].hear(3)
    result = d_middle_ref[...] + norm_back(gradient, normed, inverse, vectors_ref[0:1, :])
    input_grad_out[...] = result.reshape(rows.shape)[:, :tokens].astype(BF16)
    totals[1].pass_on(0)
    for part in late:
        part.stage_mid()
    for part in wide[2:]:
        part.stage_tail()
    totals[1].pass_on(1)
    for part in late:
        part.stage_tail()
    fc1_grad[:, :256] = wide[0].stage_out()
    fc1_grad[:, 256:] = wide[1].stage_out()
    fc2_grad[:, :128] = wide[2].stage_out()
    fc2_grad[:, 128:384] = wide[3].stage_out()
    value = wide[4].stage_out()
    fc2_grad[:, 384:] = value[:, :128]
    out_grad[...] = value[:, 128:]
    totals[1].pass_on(2)
    for i in range(3):
        qkv_grad[i] = late[i].stage_out()
    totals[1].hear(3)
    totals_out[0:8, :] = sums[0, 4]
    totals_out[8:16, :] = sums[1, 4]
    for part in parts:
        part.sent()
    for total in totals:
        total.sent()
    take(d_images.at[1], sib_send)
    take(outbox.at[:, : GROUP - 1], back_send)


REDUCED = (
    (ORDERS[2], 256),
    (ORDERS[2], 256),
    (ORDERS[2], 128),
    (ORDERS[1], 256),
    (ORDERS[0], 256),
    (ORDERS[0], 128),
    (ORDERS[1], 128),
    (ORDERS[2], 128),
)


def backward(d_attended, images, attended, turned, act, qkv, d_middle, x, vectors, sums, slot):
    width = x.shape[-1]
    count = MICRO * slot
    scratch = []
    for order, lanes in REDUCED:
        scratch += reduce_scratch(order, lanes)
    return pl.pallas_call(
        backward_kernel,
        out_shape=[
            jax.ShapeDtypeStruct(x.shape, BF16),
            jax.ShapeDtypeStruct((3, 64, 128), F32),
            jax.ShapeDtypeStruct((64, 128), F32),
            jax.ShapeDtypeStruct((64, 512), F32),
            jax.ShapeDtypeStruct((64, 512), F32),
            jax.ShapeDtypeStruct((16, width), F32),
        ],
        in_specs=[ANY] * 6 + [VMEM] * 4,
        out_specs=[VMEM] * 6,
        scratch_shapes=[
            pltpu.VMEM((MICRO, slot, width), F32),
            pltpu.VMEM((4, GROUP, width, 128), BF16),
            pltpu.VMEM(turned.shape, BF16),
            pltpu.VMEM(attended.shape, BF16),
            pltpu.VMEM(images.shape, BF16),
            pltpu.VMEM(d_attended.shape, BF16),
            pltpu.VMEM((MICRO, GROUP, slot, 384), BF16),
            pltpu.VMEM((2,) + images.shape, BF16),
            pltpu.VMEM((count, width), F32),
            pltpu.VMEM((2, 5, 8, width), F32),
            pltpu.VMEM((2, 4, 3, 8, width), F32),
        ]
        + scratch
        + [
            pltpu.SemaphoreType.DMA((11,)),
            pltpu.SemaphoreType.DMA((len(REDUCED), Reduce.sends)),
            pltpu.SemaphoreType.DMA((len(REDUCED), Reduce.recvs)),
            pltpu.SemaphoreType.DMA,
            pltpu.SemaphoreType.DMA((GROUP,)),
            pltpu.SemaphoreType.DMA,
            pltpu.SemaphoreType.DMA,
            pltpu.SemaphoreType.DMA((2, 4)),
            pltpu.SemaphoreType.DMA((2, 4)),
        ],
        compiler_params=pltpu.CompilerParams(
            collective_id=1, has_side_effects=True, vmem_limit_bytes=VMEM_LIMIT
        ),
        name="backward",
    )(d_attended, images, attended, turned, act, qkv, d_middle, x, vectors, sums)


def finish_kernel(
    result,
    input_grad,
    qkv_grad,
    out_grad,
    fc1_grad,
    fc2_grad,
    totals,
    result_out,
    input_grad_out,
    qkv_out,
    out_out,
    fc1_out,
    fc2_out,
    vectors_out,
    pair_out,
    hidden_out,
):
    f, t = lax.axis_index("fsdp"), lax.axis_index("tp")
    result_out[...] = result[...]
    input_grad_out[...] = input_grad[...]
    qkv_out[...] = qkv_grad[...]
    out_out[...] = out_grad[...]
    fc1_out[...] = fc1_grad[...]
    fc2_out[...] = fc2_grad[...]
    width = totals.shape[-1]
    own = pltpu.roll(totals[...], lax.rem(width - (f * 8 + t) * 8, width), 1)
    for number, row in enumerate((8, 9, 0, 1, 2, 3)):
        vectors_out[number] = own[row : row + 1, :8]
    own = pltpu.roll(totals[...], lax.rem(width - t * 128 - f * 4, width), 1)
    for kind in range(2):
        for head in range(2):
            pair_out[kind, head : head + 1, :] = own[
                10 + kind : 11 + kind, HD * head : HD * head + 4
            ]
    row = totals[4:8, :]
    mine = lax.broadcasted_iota(jnp.int32, row.shape, 0) == t // 2
    row = jnp.sum(jnp.where(mine, row, 0.0), 0, keepdims=True)
    row = pltpu.roll(
        jnp.broadcast_to(row, (8, width)), lax.rem(width - 512 * lax.rem(t, 2) - f * 4, width), 1
    )
    for j in range(8):
        hidden_out[j : j + 1, :] = row[0:1, 64 * j : 64 * j + 4]


def finish(result, input_grad, qkv_grad, out_grad, fc1_grad, fc2_grad, totals):
    arrays = (result, input_grad, qkv_grad, out_grad, fc1_grad, fc2_grad)
    shapes = [jax.ShapeDtypeStruct(a.shape, a.dtype) for a in arrays]
    shapes += [
        jax.ShapeDtypeStruct((6, 1, 8), F32),
        jax.ShapeDtypeStruct((2, 2, 4), F32),
        jax.ShapeDtypeStruct((8, 4), F32),
    ]
    return pl.pallas_call(
        finish_kernel,
        out_shape=shapes,
        in_specs=[VMEM] * 7,
        out_specs=[VMEM] * 9,
        compiler_params=pltpu.CompilerParams(vmem_limit_bytes=VMEM_LIMIT),
        name="finish",
    )(*arrays, totals)


def per_device(
    inputs,
    cotangent,
    valid_slots,
    ln1_gain,
    ln1_bias,
    qkv_weight,
    qv_bias,
    out_weight,
    out_bias,
    ln2_gain,
    ln2_bias,
    fc1_weight,
    fc1_bias,
    fc2_weight,
    fc2_bias,
):
    micro, _, tokens, width = inputs.shape
    slot = -(-tokens // 16) * 16
    x = inputs.reshape(micro, tokens, width)
    small = [ln1_gain, ln1_bias, out_bias, ln2_gain, ln2_bias, fc2_bias]
    small = [v.reshape(1, 8) for v in small] + [qv_bias, fc1_bias.T]
    (
        result,
        d_middle,
        vectors,
        sums,
        d_attended,
        images,
        attended,
        turned,
        act,
        qkv,
    ) = forward(
        x,
        cotangent.reshape(x.shape),
        valid_slots.T,
        qkv_weight,
        out_weight.T,
        fc1_weight,
        fc2_weight.T,
        small,
        slot,
    )
    input_grad, qkv_grad, out_grad, fc1_grad, fc2_grad, total = backward(
        d_attended,
        images,
        attended,
        turned,
        act,
        qkv.reshape(3, GROUP, width, 128),
        d_middle,
        x,
        vectors,
        sums,
        slot,
    )
    result, input_grad, qkv_grad, out_grad, fc1_grad, fc2_grad, own, pair, hidden_grad = finish(
        result, input_grad, qkv_grad, out_grad, fc1_grad, fc2_grad, total
    )
    own = [own[i].reshape(8) for i in range(6)]
    return (
        result.reshape(inputs.shape),
        input_grad.reshape(inputs.shape),
        own[0],
        own[1],
        qkv_grad,
        pair,
        out_grad.T,
        own[2],
        own[3],
        own[4],
        fc1_grad,
        hidden_grad,
        fc2_grad.T,
        own[5],
    )


def solution(mesh):
    in_specs = (
        P(None, "fsdp", "tp", None),
        P(None, "fsdp", "tp", None),
        P(None, "fsdp"),
        P(("fsdp", "tp")),
        P(("fsdp", "tp")),
        P(None, "fsdp", "tp"),
        P(None, "tp", "fsdp"),
        P("tp", "fsdp"),
        P(("fsdp", "tp")),
        P(("fsdp", "tp")),
        P(("fsdp", "tp")),
        P("fsdp", "tp"),
        P("tp", "fsdp"),
        P("tp", "fsdp"),
        P(("fsdp", "tp")),
    )
    out_specs = (
        P(None, "fsdp", "tp", None),
        P(None, "fsdp", "tp", None),
        P(("fsdp", "tp")),
        P(("fsdp", "tp")),
        P(None, "fsdp", "tp"),
        P(None, "tp", "fsdp"),
        P("tp", "fsdp"),
        P(("fsdp", "tp")),
        P(("fsdp", "tp")),
        P(("fsdp", "tp")),
        P("fsdp", "tp"),
        P("tp", "fsdp"),
        P("tp", "fsdp"),
        P(("fsdp", "tp")),
    )
    return jax.shard_map(
        per_device, mesh=mesh, in_specs=in_specs, out_specs=out_specs, check_vma=False
    )
```

```python
import functools
import math

import jax
import jax.numpy as jnp
from jax import lax
from jax.experimental import pallas as pl
from jax.experimental.pallas import tpu as pltpu
from jax.sharding import PartitionSpec as P

MESH = pl.DeviceIdType.MESH
HD = 64
SCALE = 1.0 / math.sqrt(HD)
EPSILON = 1e-05
BF16 = jnp.bfloat16
F32 = jnp.float32
VMEM_LIMIT = 62 * 2**20
MICRO, GROUP, TOKENS = 3, 8, 72
ORDERS = (("x", "y", "z"), ("y", "z", "x"), ("z", "x", "y"))
SIZES = {"x": (4,), "z": (2, 2), "y": (4,)}
LEAD = (4, 2, 2, 4, 2)
STEPS = (1, -1, 2)
NN = (((1,), (0,)), ((), ()))
NT = (((1,), (1,)), ((), ()))
TN = (((0,), (0,)), ((), ()))


def mm(a, b, dims=NN):
    return lax.dot_general(a, b, dims, preferred_element_type=F32)


def place():
    f, t = lax.axis_index("fsdp"), lax.axis_index("tp")
    return {
        "x": t // 2,
        "y": lax.rem(f // 2, 4),
        "z": (f // 8) * 2 + lax.rem(t, 2),
        "c": lax.rem(f, 2),
    }


def device_at(spot):
    return (
        (spot["z"] // 2) * 8 + spot["y"] * 2 + spot["c"],
        spot["x"] * 2 + lax.rem(spot["z"], 2),
    )


def shifted(spot, axis, by):
    return {**spot, axis: lax.rem(spot[axis] + by + 4, 4)}


def sibling(spot):
    return {**spot, "c": 1 - spot["c"]}


def member(me, number):
    return device_at({**me, "x": number // 2, "c": lax.rem(number, 2)})


def crossed(me):
    return device_at({**me, "z": me["z"] + 1 - 2 * lax.rem(me["z"], 2), "c": 1 - me["c"]})


def greet(me):
    rank = 2 * me["x"] + me["c"]
    devices = [member(me, lax.rem(rank + step, GROUP)) for step in range(1, GROUP)]
    devices += [device_at(shifted(me, axis, by)) for axis in "yz" for by in STEPS]
    devices += [crossed(me)]
    barrier = pltpu.get_barrier_semaphore()
    for device in devices:
        pl.semaphore_signal(barrier, inc=1, device_id=device, device_id_type=MESH)
    return lambda: pl.semaphore_wait(barrier, len(devices))


def view(ref, spot, full, core=None, rows=slice(None)):
    whole = slice(None)
    index = [
        whole if "x" in full else spot["x"],
        whole if "z" in full else lax.rem(spot["z"], 2),
        whole if "z" in full else spot["z"] // 2,
        whole if "y" in full else spot["y"],
    ]
    if core is not None:
        index.append(core)
    return ref.at[tuple(index) + (rows,)]


def decode(number, spot, full):
    at = {}
    for axis in "yzx":
        if axis in full:
            parts = []
            for size in reversed(SIZES[axis]):
                parts.append(lax.rem(number, size))
                number = number // size
            at[axis] = tuple(reversed(parts))
    fixed = {"x": (spot["x"],), "z": (lax.rem(spot["z"], 2), spot["z"] // 2), "y": (spot["y"],)}
    index, inner = (), ()
    for axis in "xzy":
        index += at.get(axis, fixed[axis])
        inner += at.get(axis, ())
    return index, inner


def bundle_shape(full):
    shape = ()
    for axis in "xzy":
        shape += SIZES[axis] if axis in full else ()
    return shape


def remote(src, dst, send, recv, device):
    copy = pltpu.make_async_remote_copy(
        src, dst, send, recv, device_id=device, device_id_type=MESH
    )
    copy.start()
    return copy


def take(ref, semaphore):
    pltpu.make_async_copy(ref, ref, semaphore).wait()


class Gather:
    sends, recvs = 5, 8

    def __init__(self, me, order, block, out, send, recv, local):
        self.me, self.order, self.block, self.out = me, order, block, out
        self.send, self.recv, self.local = send, recv, local
        self.core = me["c"]
        self.half = out.shape[-2] // 2
        self.plane = "".join(order[:2])

    def piece(self, spot, full, rows=slice(None)):
        return view(self.out, spot, full, self.core, rows)

    def spread(self, spot, full, axis, by, send, recv, rows=slice(None)):
        piece = self.piece(spot, full, rows)
        target = device_at(shifted(self.me, axis, by))
        remote(piece, piece, self.send.at[send], self.recv.at[recv], target)

    def share(self, spot):
        piece = self.piece(spot, self.plane)
        remote(piece, piece, self.send.at[4], self.recv.at[7], device_at(sibling(self.me)))

    def own(self):
        return pltpu.make_async_copy(
            self.block, view(self.out, self.me, "", self.core), self.local
        )

    def first(self):
        me, axis = self.me, self.order[0]
        self.own().start()
        for by in STEPS:
            target = device_at(shifted(me, axis, by))
            remote(self.block, self.piece(me, ""), self.send.at[0], self.recv.at[0], target)

    def second(self):
        self.own().wait()
        take(self.out.at[:3, 0, 0, 0, 0], self.recv.at[0])
        for by in STEPS:
            self.spread(self.me, self.order[0], self.order[1], by, 1, 1)

    def rows(self, way):
        return pl.ds(way * self.half, self.half)

    def third(self):
        take(self.out.at[:3, 0, 0, :, 0], self.recv.at[1])
        axis = self.order[2]
        for number, (by, way) in enumerate(((1, 0), (-1, 1), (1, 1), (-1, 0))):
            self.spread(self.me, self.plane, axis, by, 2, 2 + number, self.rows(way))
        self.share(self.me)

    def far(self):
        axis = self.order[2]
        for way, by in enumerate((1, -1)):
            take(self.out.at[:, 0, 0, :, 0, : self.half], self.recv.at[2 + way])
            spot = shifted(self.me, axis, -by)
            self.spread(spot, self.plane, axis, by, 3, 6, self.rows(way))

    def rest(self):
        for way, by in enumerate((1, -1)):
            take(self.out.at[:, 0, 0, :, 0, : self.half], self.recv.at[4 + way])
            self.share(shifted(self.me, self.order[2], -by))

    def last(self):
        take(self.out.at[:, 0, 0, :, 0], self.recv.at[6])
        self.share(shifted(self.me, self.order[2], 2))

    def done(self):
        take(self.out.at[:, :, :, :, 0], self.recv.at[7])

    def sent(self):
        out = self.out
        take(out.at[:3, 0, 0, 0, 0], self.send.at[0])
        take(out.at[:3, 0, 0, :, 0], self.send.at[1])
        take(out.at[:, :, 0, :, 0], self.send.at[2])
        take(out.at[:, 0, 0, :, 0], self.send.at[3])
        take(out.at[:, :, :, :, 0], self.send.at[4])


class Reduce:
    sends, recvs = 4, 5

    def __init__(self, me, order, acc, near, far, mid, tail, send, recv):
        self.me, self.order, self.acc = me, order, acc
        self.nears, self.fars, self.mid, self.tail = near, far, mid, tail
        self.send, self.recv = send, recv
        self.half = acc.shape[-2] // 2
        self.full = "".join(order[:2])

    def chunk(self, by):
        return shifted(self.me, self.order[2], by)

    def rows(self, way):
        return pl.ds(way * self.half, self.half)

    def add(self, spot, full, first, rows, terms):
        acc = self.acc

        def one(number, carry):
            index, inner = decode(number, spot, full)
            here = index + (pl.ds(first, rows),)
            total = acc[here]
            if len(terms) > 1:
                total = total.astype(F32)
            for ref, lead in terms:
                rows_there = pl.ds(first, rows) if ref.shape[-2] == acc.shape[-2] else slice(None)
                total += ref[(lead,) + inner + (rows_there,)].astype(total.dtype)
            acc[here] = total.astype(acc.dtype)
            return carry

        lax.fori_loop(0, math.prod(bundle_shape(full)), one, 0)

    def near(self, by, way):
        spot = self.chunk(by)
        box = self.nears.at[0 if by == 1 else 1]
        lead = (slice(None),) * (len(self.nears.shape) - 3)
        remote(
            view(self.acc, spot, self.full, None, self.rows(way)),
            box.at[lead + (self.rows(way),)],
            self.send.at[1],
            self.recv.at[2],
            device_at(spot),
        )

    def stage_far(self):
        spot = self.chunk(2)
        for way, by in enumerate((1, -1)):
            remote(
                view(self.acc, spot, self.full, None, self.rows(way)),
                self.fars.at[way],
                self.send.at[0],
                self.recv.at[way],
                device_at(self.chunk(by)),
            )
        for way, by in enumerate((1, -1)):
            self.near(by, 1 - way)

    def stage_near(self):
        for way, by in enumerate((1, -1)):
            take(self.fars.at[way], self.recv.at[way])
            self.add(self.chunk(by), self.full, way * self.half, self.half, [(self.fars, way)])
            self.near(by, way)

    def spread(self, axis, full, target, send, recv):
        for number, by in enumerate(STEPS):
            spot = shifted(self.me, axis, by)
            remote(
                view(self.acc, spot, full),
                target.at[number],
                self.send.at[send],
                self.recv.at[recv],
                device_at(spot),
            )

    def stage_mid(self):
        take(self.nears, self.recv.at[2])
        self.add(self.me, self.full, 0, 2 * self.half, [(self.nears, 0), (self.nears, 1)])
        self.spread(self.order[1], self.order[0], self.mid, 2, 3)

    def stage_tail(self):
        take(self.mid, self.recv.at[3])
        self.add(self.me, self.order[0], 0, 2 * self.half, [(self.mid, i) for i in range(3)])
        self.spread(self.order[0], "", self.tail, 3, 4)

    def stage_out(self):
        take(self.tail, self.recv.at[4])
        index, _ = decode(0, self.me, "")
        total = self.acc[index].astype(F32)
        for number in range(3):
            total += self.tail[number].astype(F32)
        return total

    def sent(self):
        take(self.fars, self.send.at[0])
        take(self.nears, self.send.at[1])
        take(self.mid, self.send.at[2])
        take(self.tail, self.send.at[3])


def reduce_scratch(order, lanes):
    full = bundle_shape(order[:2])
    return [
        pltpu.VMEM((4, 2, 2, 4, 64, lanes), BF16),
        pltpu.VMEM((2,) + full + (64, lanes), BF16),
        pltpu.VMEM((2,) + full + (32, lanes), BF16),
        pltpu.VMEM((3,) + bundle_shape(order[:1]) + (64, lanes), BF16),
        pltpu.VMEM((3, 64, lanes), BF16),
    ]


class Totals:
    def __init__(self, me, sums, inbox, send, recv):
        self.rounds = [[shifted(me, axis, by) for by in STEPS] for axis in "xyz"] + [[sibling(me)]]
        self.sums, self.inbox, self.send, self.recv = sums, inbox, send, recv

    def heard(self, number):
        return self.inbox.at[number, pl.ds(0, len(self.rounds[number]))]

    def speak(self, number):
        for i, spot in enumerate(self.rounds[number]):
            remote(
                self.sums.at[number],
                self.inbox.at[number, i],
                self.send.at[number],
                self.recv.at[number],
                device_at(spot),
            )

    def hear(self, number):
        take(self.heard(number), self.recv.at[number])
        total = self.sums[number]
        for i in range(len(self.rounds[number])):
            total += self.inbox[number, i]
        self.sums[number + 1] = total

    def pass_on(self, number):
        self.hear(number)
        self.speak(number + 1)

    def sent(self):
        for number in range(4):
            take(self.heard(number), self.send.at[number])


def norm_stats(values):
    average = jnp.mean(values, -1, keepdims=True)
    centered = values - average
    inverse = lax.rsqrt(jnp.mean(centered * centered, -1, keepdims=True) + EPSILON)
    return (centered * inverse, inverse)


def norm_back(upstream, normed, inverse, gain_vector):
    scaled = upstream * gain_vector
    return inverse * (
        scaled
        - jnp.mean(scaled, -1, keepdims=True)
        - normed * jnp.mean(scaled * normed, -1, keepdims=True)
    )


def softmax_columns(key_rows, queries, hidden):
    scores = mm(key_rows, queries, NT) + hidden
    powers = jnp.exp((scores - jnp.max(scores, 0, keepdims=True)) * SCALE)
    return powers * (1.0 / jnp.sum(powers, 0, keepdims=True))


def hidden_rows(seq, slot, tokens):
    row = lax.broadcasted_iota(jnp.int32, (seq, 1), 0)
    return jnp.where(lax.rem(row, slot) < tokens, 0.0, -1e30)


def head_lanes(head):
    lane = lax.broadcasted_iota(jnp.int32, (1, 128), 1)
    return jnp.where(lane // HD == head, 1.0, 0.0).astype(BF16)


def thirds(rows):
    return [rows[:, 128 * i : 128 * i + 128] for i in range(3)]


def attend(rows, hidden):
    queries, key_rows, value_rows = thirds(rows)

    def one_head(head, before):
        mine = head_lanes(head)
        probs = softmax_columns(key_rows, queries * mine, hidden).astype(BF16)
        return before + mm(probs, value_rows * mine, TN)

    return lax.fori_loop(0, 2, one_head, jnp.zeros(queries.shape, F32)).astype(BF16)


def attend_back(rows, grads, hidden):
    queries, key_rows, value_rows = thirds(rows)

    def one_head(head, before):
        mine = head_lanes(head)
        own_grads, own_queries = grads * mine, queries * mine
        probs = softmax_columns(key_rows, own_queries, hidden)
        d_probs = mm(value_rows, own_grads, NT)
        inner = jnp.sum(probs * d_probs, 0, keepdims=True)
        d_scores = (probs * (d_probs - inner)).astype(BF16)
        return (
            before[0] + mm(d_scores, key_rows * mine, TN),
            before[1] + mm(d_scores, own_queries),
            before[2] + mm(probs.astype(BF16), own_grads),
        )

    zero = jnp.zeros(queries.shape, F32)
    d_queries, d_keys, d_values = lax.fori_loop(0, 2, one_head, (zero, zero, zero))
    return [
        (d_queries * SCALE).astype(BF16),
        (d_keys * SCALE).astype(BF16),
        d_values.astype(BF16),
    ]


def fill_rows(box, m, values):
    tokens = values.shape[0]
    box[m, :tokens] = values
    box[m, tokens:] = jnp.zeros((box.shape[1] - tokens, values.shape[1]), box.dtype)


class Swap:
    def __init__(self, me, send, recv):
        self.stays = lax.rem(me["z"], 2) == me["c"]
        self.partner = crossed(me)
        self.send, self.recv = send, recv

    def start(self, box, inbox):
        @pl.when(self.stays)
        def _():
            pltpu.make_async_copy(box, inbox, self.recv).start()

        @pl.when(jnp.logical_not(self.stays))
        def _():
            remote(box, inbox, self.send, self.recv, self.partner)

    def sent(self, box):
        @pl.when(jnp.logical_not(self.stays))
        def _():
            take(box, self.send)


def blocks_of(ref, index):
    value = ref[index // 2, lax.rem(index, 2)]
    return value.reshape(-1, value.shape[-1])


def half_planes(ref, value, kind, count):
    padded = jnp.concatenate(
        [value, jnp.zeros((ref.shape[-1] - count, value.shape[1]), value.dtype)], axis=0
    )
    ref[kind] = padded.T.reshape(ref.shape[1:])


SCHEDULE = {
    "start": (("E", "first"),),
    "first": (("A", "first"), ("E", "second"), ("B", "first")),
    "swap": (("E", "third"), ("A", "second"), ("E", "far")),
    "norm": (("A", "third"), ("V", "rest"), ("V", "last"), ("V", "done")),
    "table": (("B", "second"), ("N", "rest"), ("N", "last"), ("A", "far"), ("N", "done")),
    "project": (("A", "rest"), ("B", "third"), ("A", "last")),
    "image 0": (("B", "far"),),
    "image 1": (("B", "rest"),),
    "image 2": (("B", "last"),),
    "reply": (("A", "done"),),
    "half 0": (),
    "half 1": (("B", "done"),),
}


def forward_kernel(*refs):
    (x_ref, cot_ref, valid_ref, qkv_in, out_in, fc1_in, fc2_in), refs = refs[:7], refs[7:]
    small_in, refs = refs[:8], refs[8:]
    (
        d_middle_out,
        vectors,
        sums_out,
        result_out,
        d_attended_out,
        images_out,
        attended_out,
        turned_out,
        act_out,
        qkv_out,
        x_out,
        x_box,
        x_in,
        cot_box,
        cot_in,
        result_box,
        wq,
        wk,
        wv,
        up_a,
        up_b,
        side_a,
        down_xa,
        down_xb,
        down_zb,
        side_own,
        small_own,
        small,
        bias,
        hidden_bias,
        low,
        outbox,
        images,
        attended_box,
        attended,
        middle,
        normed_two,
        low_two,
        turned,
        forward_sum,
        back_sum,
        act_box,
        d_outbox,
        hidden_sums,
        local_sem,
        gather_send,
        gather_recv,
        send_sem,
        recv_sem,
        back_send,
        back_recv,
        store_sem,
        sib_send,
        sib_recv,
        ff_local,
        ff_send,
        ff_recv,
        swap_send,
        swap_recv,
    ) = refs
    me = place()
    core = me["c"]
    t = 2 * me["x"] + core
    other = device_at(sibling(me))
    micro, tokens, width = x_ref.shape
    slot = x_in.shape[1]
    count = micro * slot
    met = greet(me)
    heads = [wq, wk, wv]
    made = []

    def gather(order, block, out):
        i = len(made)
        made.append(
            Gather(me, order, block, out, gather_send.at[i], gather_recv.at[i], local_sem.at[i])
        )
        return made[-1]

    narrow = [gather(ORDERS[i], qkv_in.at[i], heads[i]) for i in range(3)]
    vector = gather(ORDERS[0], small_own, small)
    early = [vector] + narrow
    first_half = [
        gather(ORDERS[2], fc1_in.at[:, :256], up_a),
        gather(ORDERS[0], side_own, side_a),
        gather(ORDERS[1], fc2_in.at[:, :128], down_xa),
    ]
    second_half = [
        gather(ORDERS[0], fc1_in.at[:, 256:], up_b),
        gather(ORDERS[2], fc2_in.at[:, 256:384], down_xb),
        gather(ORDERS[2], fc2_in.at[:, 384:], down_zb),
    ]
    groups = {
        "V": [vector],
        "N": narrow,
        "E": early,
        "A": first_half,
        "B": second_half,
    }

    def run(point):
        for names, stage in SCHEDULE[point]:
            for name in names:
                for part in groups[name]:
                    getattr(part, stage)()

    stores = []

    def store(src, dst):
        copy = pltpu.make_async_copy(src, dst, store_sem.at[len(stores)])
        copy.start()
        stores.append(copy)

    shared = []

    def share(src, dst):
        slot_of = len(shared)
        copy = pltpu.make_async_remote_copy(
            src,
            dst,
            sib_send.at[slot_of],
            sib_recv.at[slot_of],
            device_id=other,
            device_id_type=MESH,
        )
        copy.start()
        shared.append(copy)

    def turn(kind, value):
        half_planes(turned, value, kind, count)
        store(turned.at[kind, :, core], turned_out.at[kind, 0])
        share(turned.at[kind, :, 1 - core], turned_out.at[kind, 1])

    for m in range(micro):
        fill_rows(x_box, m, x_ref[m])
    side_own[:, :128] = out_in[...]
    side_own[:, 128:] = fc2_in[:, 128:256]
    small_own[...] = jnp.zeros_like(small_own)
    for v in range(6):
        small_own[0:1, 8 * v : 8 * v + 8] = small_in[v][...]
    for i in range(2):
        for j in range(2):
            at = 48 + 8 * i + 4 * j
            small_own[0:1, at : at + 4] = small_in[6][i, j : j + 1]
    for i in range(4):
        small_own[0:1, 64 + 8 * i : 72 + 8 * i] = small_in[7][i : i + 1]
    met()
    run("start")
    swaps = [Swap(me, swap_send.at[i], swap_recv.at[i]) for i in range(3)]
    swaps[0].start(x_box, x_in)
    run("first")
    for m in range(micro):
        fill_rows(cot_box, m, (cot_ref[m].astype(F32) * valid_ref[0, m].astype(F32)).astype(BF16))
    run("swap")
    take(x_in, swap_recv.at[0])
    store(x_in, x_out)

    def rows_of(ref):
        return ref[...].reshape(count, width).astype(F32)

    normed, _ = norm_stats(rows_of(x_in))
    run("norm")
    table = jnp.sum(small[...].reshape(128, 32, 128).astype(F32), 1).astype(BF16)
    lane = lax.broadcasted_iota(jnp.int32, (128, 1024), 0)
    column = lax.broadcasted_iota(jnp.int32, (128, 1024), 1)
    owner = jnp.where(lax.rem(lane, 16) * 8 + lane // 16 == column // 8, 1.0, 0.0)
    for v in range(6):
        pick = jnp.where(lane == v * 8 + lax.rem(column, 8), 1.0, 0.0).astype(BF16)
        vectors[v : v + 1, :] = jnp.sum(mm(table, pick) * owner, 0, keepdims=True)
    vectors[6:8, :] = jnp.zeros((2, 1024), F32)

    def spread_bias(lanes, first, major, minor):
        lane = lax.broadcasted_iota(jnp.int32, (128, lanes), 0)
        column = lax.broadcasted_iota(jnp.int32, (128, lanes), 1)
        pick = lane == first + (column // 64) * major + lax.rem(column, 4) * minor
        owner = lax.rem(lane, 16) == lax.rem(column, 64) // 4
        values = mm(table, jnp.where(pick, 1.0, 0.0).astype(BF16))
        return jnp.sum(jnp.where(owner, values, 0.0).reshape(8, 16, lanes), 1)

    hidden_value = spread_bias(512, 64, 1, 8)
    query_bias, value_bias = spread_bias(128, 48, 4, 1), spread_bias(128, 56, 4, 1)
    for i in range(GROUP):
        hidden_bias[i] = hidden_value[i : i + 1]
        bias[i, :, 0:128] = query_bias[i : i + 1]
        bias[i, :, 128:256] = jnp.zeros((1, 128), F32)
        bias[i, :, 256:384] = value_bias[i : i + 1]
    low[...] = (normed * vectors[0:1, :] + vectors[1:2, :]).astype(BF16)
    run("table")

    def letter(k, m):
        target = lax.rem(t + k + 1, GROUP)
        return pltpu.make_async_remote_copy(
            outbox.at[target, m],
            images.at[t, m],
            send_sem,
            recv_sem.at[m],
            device_id=member(me, target),
            device_id_type=MESH,
        )

    def project(k, carry):
        target = lax.rem(t + k + 1, GROUP)
        weights = jnp.concatenate([blocks_of(w, target) for w in heads], axis=1)
        result = (mm(low[...], weights) + bias[target]).astype(BF16)
        outbox[target] = result.reshape(outbox.shape[1:])

        @pl.when(k < GROUP - 1)
        def _():
            letter(k, 0).start()

        return carry

    lax.fori_loop(0, GROUP, project, 0)
    for m in range(1, MICRO):
        for k in range(GROUP - 1):
            letter(k, m).start()
    own = pltpu.make_async_copy(outbox.at[t], images.at[t], local_sem.at[len(made)])
    own.start()
    for i in range(3):
        store(heads[i], qkv_out.at[i])
    swaps[1].start(cot_box, cot_in)
    run("project")
    turn(0, low[...])
    own.wait()
    hidden = hidden_rows(GROUP * slot, slot, tokens)

    def reply(m, k):
        target = lax.rem(t + k + 1, GROUP)
        return pltpu.make_async_remote_copy(
            attended_box.at[m, target],
            attended.at[t, m],
            back_send,
            back_recv,
            device_id=member(me, target),
            device_id_type=MESH,
        )

    for m in range(MICRO):
        take(images.at[: GROUP - 1, m], recv_sem.at[m])
        result = attend(images[:, m].reshape(GROUP * slot, 384), hidden)
        attended_box[m] = result.reshape(GROUP, slot, 128)
        for k in range(GROUP - 1):
            reply(m, k).start()
        attended[t, m] = attended_box[m, t]
        run(("image 0", "image 1", "image 2")[m])
        if m == 1:
            take(cot_in, swap_recv.at[1])
            upstream_low = cot_in[...].reshape(count, width)
            sums_out[3:4, :] = jnp.sum(upstream_low.astype(F32), 0, keepdims=True)
            turn(1, upstream_low)
    store(images, images_out)
    take(attended.at[: GROUP - 1], back_recv)
    store(attended, attended_out.at[0])
    share(attended, attended_out.at[1])
    run("reply")
    middle[...] = rows_of(x_in) + vectors[2:3, :]

    def out_weights(pair):
        both = [blocks_of(side_a, 2 * pair + i)[:, :128] for i in range(2)]
        return jnp.concatenate(both, axis=1)

    def out_project(pair, carry):
        both = [attended[2 * pair + i].reshape(count, 128) for i in range(2)]
        middle[...] += mm(jnp.concatenate(both, axis=1), out_weights(pair), NT)
        return carry

    lax.fori_loop(0, GROUP // 2, out_project, 0)
    normed, inverse = norm_stats(middle[...])
    normed_two[...] = normed
    low_two[...] = (normed * vectors[3:4, :] + vectors[4:5, :]).astype(BF16)
    turn(2, low_two[...])
    forward_sum[...] = jnp.zeros_like(forward_sum)
    back_sum[...] = jnp.zeros_like(back_sum)

    def ship(pair, h):
        piece = act_box.at[pl.ds(2 * pair, 2), :, pl.ds(2 * count * h, 2 * count)]
        at = (pl.ds(2 * pair, 2), slice(None), pl.ds(2 * count * h, 2 * count))
        pltpu.make_async_copy(piece, act_out.at[(0,) + at], ff_local).start()
        remote(piece, act_out.at[(1,) + at], ff_send, ff_recv, other)

    for h in range(2):
        run(("half 0", "half 1")[h])

        def feed_forward(pair, carry):
            slabs = [2 * pair, 2 * pair + 1]
            up_weight = jnp.concatenate([blocks_of((up_a, up_b)[h], i) for i in slabs], axis=1)
            down = []
            for i in slabs:
                down.append(blocks_of((down_xa, down_xb)[h], i))
                down.append(blocks_of(side_a, i)[:, 128:] if h == 0 else blocks_of(down_zb, i))
            down_weight = jnp.concatenate(down, axis=1)
            biases = [hidden_bias[i, :, 256 * h : 256 * h + 256] for i in slabs]
            up_proj = mm(low_two[...], up_weight) + jnp.concatenate(biases, axis=1)
            gate = jax.nn.sigmoid(1.702 * up_proj)
            activated = (up_proj * gate).astype(BF16)
            d_act = mm(cot_in[...].reshape(count, width), down_weight)
            d_up = (d_act * (gate + 1.702 * up_proj * gate * (1.0 - gate))).astype(BF16)
            column_sums = jnp.sum(d_up.astype(F32), 0, keepdims=True)
            for n, i in enumerate(slabs):
                for j in range(2):
                    at = pl.ds(count * (2 * h + j), count)
                    lanes = slice(256 * n + 128 * j, 256 * n + 128 * (j + 1))
                    act_box[i, 0, at] = activated[:, lanes]
                    act_box[i, 1, at] = d_up[:, lanes]
                hidden_sums[i, :, 256 * h : 256 * h + 256] = column_sums[:, 256 * n : 256 * n + 256]
            ship(pair, h)
            forward_sum[...] += mm(activated, down_weight, NT)
            back_sum[...] += mm(d_up, up_weight, NT)
            return carry

        lax.fori_loop(0, GROUP // 2, feed_forward, 0)
    output = (middle[...] + forward_sum[...] + vectors[5:6, :]).astype(BF16)
    result_box[...] = output.reshape(result_box.shape)
    swaps[2].start(result_box, result_out)
    d_norm = back_sum[...]
    normed = normed_two[...]
    d_middle = rows_of(cot_in) + norm_back(
        d_norm, normed, inverse, vectors[3:4, :]
    )
    d_middle_out[...] = d_middle
    low[...] = d_middle.astype(BF16)

    def project_back(pair, carry):
        both = mm(low[...], out_weights(pair)).astype(BF16)
        for i in range(2):
            d_outbox[2 * pair + i] = both[:, 128 * i : 128 * i + 128].reshape(d_outbox.shape[1:])
        return carry

    lax.fori_loop(0, GROUP // 2, project_back, 0)
    store(d_outbox, d_attended_out)
    turn(3, low[...])
    sums_out[0:1, :] = jnp.sum(d_middle, 0, keepdims=True)
    sums_out[1:2, :] = jnp.sum(d_norm * normed, 0, keepdims=True)
    sums_out[2:3, :] = jnp.sum(d_norm, 0, keepdims=True)
    for i in range(GROUP):
        at = 4 + i // 2
        sums_out[at : at + 1, 512 * (i % 2) : 512 * (i % 2) + 512] = hidden_sums[i]
    for swap, box in zip(swaps, (x_box, cot_box, result_box)):
        swap.sent(box)
    take(result_out, swap_recv.at[2])
    for copy in shared:
        copy.wait()
    take(act_box, ff_local)
    take(act_box, ff_send)
    take(act_box, ff_recv)
    for part in made:
        part.sent()
    take(outbox.at[: GROUP - 1], send_sem)
    take(attended_box.at[:, : GROUP - 1], back_send)
    for copy in stores:
        copy.wait()


ANY = pl.BlockSpec(memory_space=pl.ANY)
VMEM = pl.BlockSpec(memory_space=pltpu.VMEM)
SMEM = pl.BlockSpec(memory_space=pltpu.SMEM)


def forward(x, cotangent, valid, qkv_block, out_block, fc1_block, fc2_block, small, slot):
    width = x.shape[-1]
    count = MICRO * slot
    rows = (MICRO, slot, width)
    images = (GROUP, MICRO, slot, 384)
    attended = (GROUP, MICRO, slot, 128)
    acts = (2, GROUP, 2, 4 * count, 128)
    return pl.pallas_call(
        forward_kernel,
        out_shape=[
            jax.ShapeDtypeStruct((count, width), F32),
            jax.ShapeDtypeStruct((8, width), F32),
            jax.ShapeDtypeStruct((8, width), F32),
            jax.ShapeDtypeStruct(rows, BF16),
            jax.ShapeDtypeStruct(attended, BF16),
            jax.ShapeDtypeStruct(images, BF16),
            jax.ShapeDtypeStruct((2,) + attended, BF16),
            jax.ShapeDtypeStruct((4, 2, 8, 64, 256), BF16),
            jax.ShapeDtypeStruct(acts, BF16),
            jax.ShapeDtypeStruct((3,) + LEAD + (64, 128), BF16),
            jax.ShapeDtypeStruct(rows, BF16),
        ],
        in_specs=[VMEM, VMEM, SMEM, ANY, VMEM, ANY, VMEM] + [VMEM] * 8,
        out_specs=[VMEM] * 3 + [ANY] * 8,
        scratch_shapes=[
            pltpu.VMEM(rows, BF16),
            pltpu.VMEM(rows, BF16),
            pltpu.VMEM(rows, BF16),
            pltpu.VMEM(rows, BF16),
            pltpu.VMEM(rows, BF16),
            pltpu.VMEM(LEAD + (64, 128), BF16),
            pltpu.VMEM(LEAD + (64, 128), BF16),
            pltpu.VMEM(LEAD + (64, 128), BF16),
            pltpu.VMEM(LEAD + (64, 256), BF16),
            pltpu.VMEM(LEAD + (64, 256), BF16),
            pltpu.VMEM(LEAD + (64, 256), BF16),
            pltpu.VMEM(LEAD + (64, 128), BF16),
            pltpu.VMEM(LEAD + (64, 128), BF16),
            pltpu.VMEM(LEAD + (64, 128), BF16),
            pltpu.VMEM((64, 256), BF16),
            pltpu.VMEM((32, 128), BF16),
            pltpu.VMEM(LEAD + (32, 128), BF16),
            pltpu.VMEM((GROUP, 1, 384), F32),
            pltpu.VMEM((GROUP, 1, 512), F32),
            pltpu.VMEM((count, width), BF16),
            pltpu.VMEM(images, BF16),
            pltpu.VMEM(images, BF16),
            pltpu.VMEM((MICRO, GROUP, slot, 128), BF16),
            pltpu.VMEM(attended, BF16),
            pltpu.VMEM((count, width), F32),
            pltpu.VMEM((count, width), F32),
            pltpu.VMEM((count, width), BF16),
            pltpu.VMEM((4, 8, 2, 64, 256), BF16),
            pltpu.VMEM((count, width), F32),
            pltpu.VMEM((count, width), F32),
            pltpu.VMEM(acts[1:], BF16),
            pltpu.VMEM(attended, BF16),
            pltpu.VMEM((GROUP, 1, 512), F32),
            pltpu.SemaphoreType.DMA((12,)),
            pltpu.SemaphoreType.DMA((10, Gather.sends)),
            pltpu.SemaphoreType.DMA((10, Gather.recvs)),
            pltpu.SemaphoreType.DMA,
            pltpu.SemaphoreType.DMA((MICRO,)),
            pltpu.SemaphoreType.DMA,
            pltpu.SemaphoreType.DMA,
            pltpu.SemaphoreType.DMA((11,)),
            pltpu.SemaphoreType.DMA((5,)),
            pltpu.SemaphoreType.DMA((5,)),
            pltpu.SemaphoreType.DMA,
            pltpu.SemaphoreType.DMA,
            pltpu.SemaphoreType.DMA,
            pltpu.SemaphoreType.DMA((3,)),
            pltpu.SemaphoreType.DMA((3,)),
        ],
        compiler_params=pltpu.CompilerParams(
            collective_id=0, has_side_effects=True, vmem_limit_bytes=VMEM_LIMIT
        ),
        name="forward",
    )(x, cotangent, valid, qkv_block, out_block, fc1_block, fc2_block, *small)


def backward_kernel(*refs):
    (
        d_attended_in,
        images_in,
        attended_in,
        turned_in,
        act_in,
        qkv_in,
        x_in,
        d_middle_ref,
        vectors_ref,
        sums_ref,
        qkv_grad,
        out_grad,
        fc1_grad,
        fc2_grad,
        totals_out,
        input_grad_out,
        rows,
        box,
        pool,
        turned,
        attended,
        images,
        d_attended,
        outbox,
        d_images,
        d_norm,
        sums,
        sums_in,
        *rest,
    ) = refs
    scratch, sems = rest[: 5 * len(REDUCED)], rest[5 * len(REDUCED) :]
    (
        load_sem,
        reduce_send,
        reduce_recv,
        send_sem,
        recv_sem,
        back_send,
        back_recv,
        sib_send,
        sib_recv,
        sum_send,
        sum_recv,
        swap_send,
        swap_recv,
    ) = sems
    me = place()
    t = 2 * me["x"] + me["c"]
    other = device_at(sibling(me))
    met = greet(me)
    slot = rows.shape[1]
    count = MICRO * slot
    parts = [
        Reduce(
            me,
            REDUCED[i][0],
            *scratch[5 * i : 5 * i + 5],
            reduce_send.at[i],
            reduce_recv.at[i],
        )
        for i in range(len(REDUCED))
    ]
    late = parts[-3:]
    wide = parts[:-3]
    totals = [
        Totals(me, sums.at[i], sums_in.at[i], sum_send.at[i], sum_recv.at[i]) for i in range(2)
    ]
    loads = {}

    def load(name, src, dst):
        loads[name] = pltpu.make_async_copy(src, dst, load_sem.at[len(loads)])
        loads[name].start()

    kept = pl.ds(0, 4 * count)
    load("turned", turned_in, turned)
    for i in range(2):
        load(("dup", i), act_in.at[i, :, 1], pool.at[2 + i, :, kept])
    load("images", images_in, images)
    load("own", d_attended_in.at[t], d_attended.at[t])
    for i in range(2):
        load(("act", i), act_in.at[i, :, 0], pool.at[i, :, kept])
    load("attended", attended_in, attended)
    load("rows", x_in, rows)
    sums[0, 0] = sums_ref[...]

    def both_cores(kind, values):
        total = 0.0
        for i in range(2):
            left = turned[kind, i].reshape(512, 256)[:, :count]
            total += mm(left, values[i])
        return total.astype(BF16)

    def pooled(first, index, lanes):
        return [
            jnp.concatenate(
                [pool[first + i, index, count * j : count * (j + 1)] for j in lanes], axis=1
            )
            for i in range(2)
        ]

    def spot_of(index):
        return (index // 2, lax.rem(index, 2))

    def fill(part, index, lanes, value):
        acc = part.acc
        acc[spot_of(index) + (slice(None),) * 3 + (lanes,)] = value.reshape(
            acc.shape[2:-1] + (value.shape[-1],)
        )

    def grads_up(half):
        def one(index, carry):
            value = both_cores(2, pooled(2, index, (2 * half, 2 * half + 1)))
            fill(wide[half], index, slice(0, 256), value)
            return carry

        return one

    def grads_down(index, carry):
        value = both_cores(1, pooled(0, index, range(4)))
        fill(wide[2], index, slice(0, 128), value[:, :128])
        fill(wide[3], index, slice(0, 256), value[:, 128:384])
        fill(wide[4], index, slice(0, 128), value[:, 384:])
        value = both_cores(3, [attended[i, index].reshape(count, 128) for i in range(2)])
        fill(wide[4], index, slice(128, 256), value)
        return carry

    loads["turned"].wait()
    for i in range(2):
        loads["dup", i].wait()
    met()
    for m in range(MICRO):
        for k in range(GROUP - 1):
            target = lax.rem(t + k + 1, GROUP)
            remote(
                d_attended_in.at[target, m],
                d_attended.at[t, m],
                send_sem,
                recv_sem.at[m],
                member(me, target),
            )
    lax.fori_loop(0, GROUP, grads_up(0), 0)
    wide[0].stage_far()
    totals[0].speak(0)
    lax.fori_loop(0, GROUP, grads_up(1), 0)
    wide[1].stage_far()
    loads["images"].wait()
    loads["own"].wait()
    hidden = hidden_rows(GROUP * slot, slot, TOKENS)

    def reply(m, k):
        target = lax.rem(t + k + 1, GROUP)
        return pltpu.make_async_remote_copy(
            outbox.at[m, target],
            d_images.at[0, t, m],
            back_send,
            back_recv.at[k],
            device_id=member(me, target),
            device_id_type=MESH,
        )

    for m in range(MICRO):
        take(d_attended.at[: GROUP - 1, m], recv_sem.at[m])
        results = attend_back(
            images[:, m].reshape(GROUP * slot, 384),
            d_attended[:, m].reshape(GROUP * slot, 128),
            hidden,
        )
        for i in range(3):
            outbox[m, :, :, 128 * i : 128 * i + 128] = results[i].reshape(GROUP, slot, 128)
        for k in range(GROUP - 1):
            reply(m, k).start()
        d_images[0, t, m] = outbox[m, t]
        if m == 0:
            for i in range(2):
                loads["act", i].wait()
            loads["attended"].wait()
            lax.fori_loop(0, GROUP, grads_down, 0)
            for part in wide[2:]:
                part.stage_far()
            for i in range(3):
                load(("weight", i), qkv_in.at[i], pool.at[i])
            wide[0].stage_near()
            totals[0].pass_on(0)
        if m == 1:
            wide[1].stage_near()
            totals[0].pass_on(1)
    for part in wide[2:]:
        part.stage_near()
    loads["rows"].wait()
    normed, inverse = norm_stats(rows[...].reshape(count, rows.shape[-1]).astype(F32))
    totals[0].pass_on(2)
    wide[0].stage_mid()

    def share(k):
        source = lax.rem(t + k + 1, GROUP)
        remote(d_images.at[0, source], d_images.at[1, source], sib_send, sib_recv, other)

    share(GROUP - 1)
    for k in reversed(range(GROUP - 1)):
        take(d_images.at[0, 0], back_recv.at[GROUP - 2 - k])
        share(k)
    wide[1].stage_mid()
    take(d_images.at[1], sib_recv)

    def grads_late(index, carry):
        value = both_cores(0, [d_images[i, index].reshape(count, 384) for i in range(2)])
        for i, part in enumerate(late):
            fill(part, index, slice(None), value[:, 128 * i : 128 * i + 128])
        return carry

    lax.fori_loop(0, GROUP, grads_late, 0)
    for part in late:
        part.stage_far()
    for part in wide[2:]:
        part.stage_mid()
    for i in range(3):
        loads["weight", i].wait()
    d_norm[...] = jnp.zeros_like(d_norm)

    def project_back(index, carry):
        weights = jnp.concatenate([pool[i, index] for i in range(3)], axis=1)
        d_norm[...] += mm(d_images[0, index].reshape(count, 384), weights, NT)
        return carry

    lax.fori_loop(0, GROUP, project_back, 0)
    for part in late:
        part.stage_near()
    for part in wide[:2]:
        part.stage_tail()
    gradient = d_norm[...]
    sums[1, 0, 0:1, :] = jnp.sum(gradient * normed, 0, keepdims=True)
    sums[1, 0, 1:2, :] = jnp.sum(gradient, 0, keepdims=True)
    for index in range(GROUP):
        grads = jnp.sum(d_images[0, index].reshape(count, 384).astype(F32), 0, keepdims=True)
        sums[1, 0, 2:3, 128 * index : 128 * index + 128] = grads[:, :128]
        sums[1, 0, 3:4, 128 * index : 128 * index + 128] = grads[:, 256:]
    sums[1, 0, 4:8, :] = jnp.zeros((4, sums.shape[-1]), F32)
    totals[1].speak(0)
    totals[0].hear(3)
    result = d_middle_ref[...] + norm_back(gradient, normed, inverse, vectors_ref[0:1, :])
    box[...] = result.astype(BF16).reshape(box.shape)
    swap = Swap(me, swap_send, swap_recv)
    swap.start(box, input_grad_out)
    totals[1].pass_on(0)
    for part in late:
        part.stage_mid()
    for part in wide[2:]:
        part.stage_tail()
    totals[1].pass_on(1)
    for part in late:
        part.stage_tail()
    fc1_grad[:, :256] = wide[0].stage_out()
    fc1_grad[:, 256:] = wide[1].stage_out()
    fc2_grad[:, :128] = wide[2].stage_out()
    fc2_grad[:, 128:384] = wide[3].stage_out()
    value = wide[4].stage_out()
    fc2_grad[:, 384:] = value[:, :128]
    out_grad[...] = value[:, 128:]
    totals[1].pass_on(2)
    for i in range(3):
        qkv_grad[i] = late[i].stage_out()
    totals[1].hear(3)
    totals_out[0:8, :] = sums[0, 4]
    totals_out[8:16, :] = sums[1, 4]
    for part in parts:
        part.sent()
    for total in totals:
        total.sent()
    take(d_images.at[1], sib_send)
    take(outbox.at[:, : GROUP - 1], back_send)
    take(d_attended.at[: GROUP - 1], send_sem)
    swap.sent(box)
    take(input_grad_out, swap_recv)


REDUCED = (
    (ORDERS[2], 256),
    (ORDERS[0], 256),
    (ORDERS[1], 128),
    (ORDERS[2], 256),
    (ORDERS[0], 256),
    (ORDERS[0], 128),
    (ORDERS[1], 128),
    (ORDERS[2], 128),
)


def backward(d_attended, images, attended, turned, act, qkv, x, d_middle, vectors, sums):
    width = x.shape[-1]
    slot = x.shape[1]
    count = MICRO * slot
    scratch = []
    for order, lanes in REDUCED:
        scratch += reduce_scratch(order, lanes)
    return pl.pallas_call(
        backward_kernel,
        out_shape=[
            jax.ShapeDtypeStruct((3, 64, 128), F32),
            jax.ShapeDtypeStruct((64, 128), F32),
            jax.ShapeDtypeStruct((64, 512), F32),
            jax.ShapeDtypeStruct((64, 512), F32),
            jax.ShapeDtypeStruct((16, width), F32),
            jax.ShapeDtypeStruct(x.shape, BF16),
        ],
        in_specs=[ANY] * 7 + [VMEM] * 3,
        out_specs=[VMEM] * 5 + [ANY],
        scratch_shapes=[
            pltpu.VMEM(x.shape, BF16),
            pltpu.VMEM(x.shape, BF16),
            pltpu.VMEM((4, GROUP, width, 128), BF16),
            pltpu.VMEM(turned.shape, BF16),
            pltpu.VMEM(attended.shape, BF16),
            pltpu.VMEM(images.shape, BF16),
            pltpu.VMEM(d_attended.shape, BF16),
            pltpu.VMEM((MICRO, GROUP, slot, 384), BF16),
            pltpu.VMEM((2,) + images.shape, BF16),
            pltpu.VMEM((count, width), F32),
            pltpu.VMEM((2, 5, 8, width), F32),
            pltpu.VMEM((2, 4, 3, 8, width), F32),
        ]
        + scratch
        + [
            pltpu.SemaphoreType.DMA((12,)),
            pltpu.SemaphoreType.DMA((len(REDUCED), Reduce.sends)),
            pltpu.SemaphoreType.DMA((len(REDUCED), Reduce.recvs)),
            pltpu.SemaphoreType.DMA,
            pltpu.SemaphoreType.DMA((MICRO,)),
            pltpu.SemaphoreType.DMA,
            pltpu.SemaphoreType.DMA((GROUP,)),
            pltpu.SemaphoreType.DMA,
            pltpu.SemaphoreType.DMA,
            pltpu.SemaphoreType.DMA((2, 4)),
            pltpu.SemaphoreType.DMA((2, 4)),
            pltpu.SemaphoreType.DMA,
            pltpu.SemaphoreType.DMA,
        ],
        compiler_params=pltpu.CompilerParams(
            collective_id=1, has_side_effects=True, vmem_limit_bytes=VMEM_LIMIT
        ),
        name="backward",
    )(d_attended, images, attended, turned, act, qkv, x, d_middle, vectors, sums)


def finish_kernel(
    result,
    input_grad,
    qkv_grad,
    out_grad,
    fc1_grad,
    fc2_grad,
    totals,
    result_out,
    input_grad_out,
    qkv_out,
    out_out,
    fc1_out,
    fc2_out,
    vectors_out,
    pair_out,
    hidden_out,
):
    f, t = lax.axis_index("fsdp"), lax.axis_index("tp")
    tokens = result_out.shape[1]
    result_out[...] = result[:, :tokens]
    input_grad_out[...] = input_grad[:, :tokens]
    qkv_out[...] = qkv_grad[...]
    out_out[...] = out_grad[...]
    fc1_out[...] = fc1_grad[...]
    fc2_out[...] = fc2_grad[...]
    width = totals.shape[-1]
    own = pltpu.roll(totals[...], lax.rem(width - (f * 8 + t) * 8, width), 1)
    for number, row in enumerate((8, 9, 0, 1, 2, 3)):
        vectors_out[number] = own[row : row + 1, :8]
    own = pltpu.roll(totals[...], lax.rem(width - t * 128 - f * 4, width), 1)
    for kind in range(2):
        for head in range(2):
            pair_out[kind, head : head + 1, :] = own[
                10 + kind : 11 + kind, HD * head : HD * head + 4
            ]
    row = totals[4:8, :]
    mine = lax.broadcasted_iota(jnp.int32, row.shape, 0) == t // 2
    row = jnp.sum(jnp.where(mine, row, 0.0), 0, keepdims=True)
    row = pltpu.roll(
        jnp.broadcast_to(row, (8, width)), lax.rem(width - 512 * lax.rem(t, 2) - f * 4, width), 1
    )
    for j in range(8):
        hidden_out[j : j + 1, :] = row[0:1, 64 * j : 64 * j + 4]


def finish(result, input_grad, qkv_grad, out_grad, fc1_grad, fc2_grad, totals):
    arrays = (result, input_grad, qkv_grad, out_grad, fc1_grad, fc2_grad)
    rows = jax.ShapeDtypeStruct((MICRO, TOKENS, result.shape[-1]), BF16)
    shapes = [rows, rows] + [jax.ShapeDtypeStruct(a.shape, a.dtype) for a in arrays[2:]]
    shapes += [
        jax.ShapeDtypeStruct((6, 1, 8), F32),
        jax.ShapeDtypeStruct((2, 2, 4), F32),
        jax.ShapeDtypeStruct((8, 4), F32),
    ]
    return pl.pallas_call(
        finish_kernel,
        out_shape=shapes,
        in_specs=[VMEM] * 7,
        out_specs=[VMEM] * 9,
        compiler_params=pltpu.CompilerParams(vmem_limit_bytes=VMEM_LIMIT),
        name="finish",
    )(*arrays, totals)


def per_device(
    inputs,
    cotangent,
    valid_slots,
    ln1_gain,
    ln1_bias,
    qkv_weight,
    qv_bias,
    out_weight,
    out_bias,
    ln2_gain,
    ln2_bias,
    fc1_weight,
    fc1_bias,
    fc2_weight,
    fc2_bias,
):
    micro, _, tokens, width = inputs.shape
    slot = -(-tokens // 16) * 16
    x = inputs.reshape(micro, tokens, width)
    small = [ln1_gain, ln1_bias, out_bias, ln2_gain, ln2_bias, fc2_bias]
    small = [v.reshape(1, 8) for v in small] + [qv_bias, fc1_bias.T]
    (
        d_middle,
        vectors,
        sums,
        result,
        d_attended,
        images,
        attended,
        turned,
        act,
        qkv,
        x_rows,
    ) = forward(
        x,
        cotangent.reshape(x.shape),
        valid_slots.T,
        qkv_weight,
        out_weight.T,
        fc1_weight,
        fc2_weight.T,
        small,
        slot,
    )
    qkv_grad, out_grad, fc1_grad, fc2_grad, total, input_grad = backward(
        d_attended,
        images,
        attended,
        turned,
        act,
        qkv.reshape(3, GROUP, width, 128),
        x_rows,
        d_middle,
        vectors,
        sums,
    )
    result, input_grad, qkv_grad, out_grad, fc1_grad, fc2_grad, own, pair, hidden_grad = finish(
        result, input_grad, qkv_grad, out_grad, fc1_grad, fc2_grad, total
    )
    own = [own[i].reshape(8) for i in range(6)]
    return (
        result.reshape(inputs.shape),
        input_grad.reshape(inputs.shape),
        own[0],
        own[1],
        qkv_grad,
        pair,
        out_grad.T,
        own[2],
        own[3],
        own[4],
        fc1_grad,
        hidden_grad,
        fc2_grad.T,
        own[5],
    )


def solution(mesh):
    in_specs = (
        P(None, "fsdp", "tp", None),
        P(None, "fsdp", "tp", None),
        P(None, "fsdp"),
        P(("fsdp", "tp")),
        P(("fsdp", "tp")),
        P(None, "fsdp", "tp"),
        P(None, "tp", "fsdp"),
        P("tp", "fsdp"),
        P(("fsdp", "tp")),
        P(("fsdp", "tp")),
        P(("fsdp", "tp")),
        P("fsdp", "tp"),
        P("tp", "fsdp"),
        P("tp", "fsdp"),
        P(("fsdp", "tp")),
    )
    out_specs = (
        P(None, "fsdp", "tp", None),
        P(None, "fsdp", "tp", None),
        P(("fsdp", "tp")),
        P(("fsdp", "tp")),
        P(None, "fsdp", "tp"),
        P(None, "tp", "fsdp"),
        P("tp", "fsdp"),
        P(("fsdp", "tp")),
        P(("fsdp", "tp")),
        P(("fsdp", "tp")),
        P("fsdp", "tp"),
        P("tp", "fsdp"),
        P("tp", "fsdp"),
        P(("fsdp", "tp")),
    )
    return jax.shard_map(
        per_device, mesh=mesh, in_specs=in_specs, out_specs=out_specs, check_vma=False
    )
```

```python
import functools
import math

import jax
import jax.numpy as jnp
from jax import lax
from jax.experimental import pallas as pl
from jax.experimental.pallas import tpu as pltpu
from jax.sharding import PartitionSpec as P

MESH = pl.DeviceIdType.MESH
HD = 64
SCALE = 1.0 / math.sqrt(HD)
EPSILON = 1e-05
BF16 = jnp.bfloat16
F32 = jnp.float32
VMEM_LIMIT = 62 * 2**20
MICRO, GROUP, TOKENS = 3, 8, 72
ORDERS = (("x", "y", "z"), ("y", "z", "x"), ("z", "x", "y"))
SIZES = {"x": (4,), "z": (2, 2), "y": (4,)}
LEAD = (4, 2, 2, 4, 2)
STEPS = (1, -1, 2)
NN = (((1,), (0,)), ((), ()))
NT = (((1,), (1,)), ((), ()))
TN = (((0,), (0,)), ((), ()))


def mm(a, b, dims=NN):
    return lax.dot_general(a, b, dims, preferred_element_type=F32)


def place():
    f, t = lax.axis_index("fsdp"), lax.axis_index("tp")
    return {
        "x": t // 2,
        "y": lax.rem(f // 2, 4),
        "z": (f // 8) * 2 + lax.rem(t, 2),
        "c": lax.rem(f, 2),
    }


def device_at(spot):
    return (
        (spot["z"] // 2) * 8 + spot["y"] * 2 + spot["c"],
        spot["x"] * 2 + lax.rem(spot["z"], 2),
    )


def shifted(spot, axis, by):
    return {**spot, axis: lax.rem(spot[axis] + by + 4, 4)}


def sibling(spot):
    return {**spot, "c": 1 - spot["c"]}


def member(me, number):
    return device_at({**me, "x": number // 2, "c": lax.rem(number, 2)})


def crossed(me):
    return device_at({**me, "z": me["z"] + 1 - 2 * lax.rem(me["z"], 2), "c": 1 - me["c"]})


def greet(me):
    rank = 2 * me["x"] + me["c"]
    devices = [member(me, lax.rem(rank + step, GROUP)) for step in range(1, GROUP)]
    devices += [device_at(shifted(me, axis, by)) for axis in "yz" for by in STEPS]
    devices += [crossed(me)]
    barrier = pltpu.get_barrier_semaphore()
    for device in devices:
        pl.semaphore_signal(barrier, inc=1, device_id=device, device_id_type=MESH)
    return lambda: pl.semaphore_wait(barrier, len(devices))


def view(ref, spot, full, core=None, rows=slice(None)):
    whole = slice(None)
    index = [
        whole if "x" in full else spot["x"],
        whole if "z" in full else lax.rem(spot["z"], 2),
        whole if "z" in full else spot["z"] // 2,
        whole if "y" in full else spot["y"],
    ]
    if core is not None:
        index.append(core)
    return ref.at[tuple(index) + (rows,)]


def decode(number, spot, full):
    at = {}
    for axis in "yzx":
        if axis in full:
            parts = []
            for size in reversed(SIZES[axis]):
                parts.append(lax.rem(number, size))
                number = number // size
            at[axis] = tuple(reversed(parts))
    fixed = {"x": (spot["x"],), "z": (lax.rem(spot["z"], 2), spot["z"] // 2), "y": (spot["y"],)}
    index, inner = (), ()
    for axis in "xzy":
        index += at.get(axis, fixed[axis])
        inner += at.get(axis, ())
    return index, inner


def bundle_shape(full):
    shape = ()
    for axis in "xzy":
        shape += SIZES[axis] if axis in full else ()
    return shape


def remote(src, dst, send, recv, device):
    copy = pltpu.make_async_remote_copy(
        src, dst, send, recv, device_id=device, device_id_type=MESH
    )
    copy.start()
    return copy


def take(ref, semaphore):
    pltpu.make_async_copy(ref, ref, semaphore).wait()


class Gather:
    sends, recvs = 5, 8

    def __init__(self, me, order, block, out, send, recv, local):
        self.me, self.order, self.block, self.out = me, order, block, out
        self.send, self.recv, self.local = send, recv, local
        self.core = me["c"]
        self.half = out.shape[-2] // 2
        self.plane = "".join(order[:2])

    def piece(self, spot, full, rows=slice(None)):
        return view(self.out, spot, full, self.core, rows)

    def spread(self, spot, full, axis, by, send, recv, rows=slice(None)):
        piece = self.piece(spot, full, rows)
        target = device_at(shifted(self.me, axis, by))
        remote(piece, piece, self.send.at[send], self.recv.at[recv], target)

    def share(self, spot):
        piece = self.piece(spot, self.plane)
        remote(piece, piece, self.send.at[4], self.recv.at[7], device_at(sibling(self.me)))

    def own(self):
        return pltpu.make_async_copy(
            self.block, view(self.out, self.me, "", self.core), self.local
        )

    def first(self):
        me, axis = self.me, self.order[0]
        self.own().start()
        for by in STEPS:
            target = device_at(shifted(me, axis, by))
            remote(self.block, self.piece(me, ""), self.send.at[0], self.recv.at[0], target)

    def second(self):
        self.own().wait()
        take(self.out.at[:3, 0, 0, 0, 0], self.recv.at[0])
        for by in STEPS:
            self.spread(self.me, self.order[0], self.order[1], by, 1, 1)

    def rows(self, way):
        return pl.ds(way * self.half, self.half)

    def third(self):
        take(self.out.at[:3, 0, 0, :, 0], self.recv.at[1])
        axis = self.order[2]
        for number, (by, way) in enumerate(((1, 0), (-1, 1), (1, 1), (-1, 0))):
            self.spread(self.me, self.plane, axis, by, 2, 2 + number, self.rows(way))
        self.share(self.me)

    def far(self):
        axis = self.order[2]
        for way, by in enumerate((1, -1)):
            take(self.out.at[:, 0, 0, :, 0, : self.half], self.recv.at[2 + way])
            spot = shifted(self.me, axis, -by)
            self.spread(spot, self.plane, axis, by, 3, 6, self.rows(way))

    def rest(self):
        for way, by in enumerate((1, -1)):
            take(self.out.at[:, 0, 0, :, 0, : self.half], self.recv.at[4 + way])
            self.share(shifted(self.me, self.order[2], -by))

    def last(self):
        take(self.out.at[:, 0, 0, :, 0], self.recv.at[6])
        self.share(shifted(self.me, self.order[2], 2))

    def done(self):
        take(self.out.at[:, :, :, :, 0], self.recv.at[7])

    def sent(self):
        out = self.out
        take(out.at[:3, 0, 0, 0, 0], self.send.at[0])
        take(out.at[:3, 0, 0, :, 0], self.send.at[1])
        take(out.at[:, :, 0, :, 0], self.send.at[2])
        take(out.at[:, 0, 0, :, 0], self.send.at[3])
        take(out.at[:, :, :, :, 0], self.send.at[4])


class Reduce:
    sends, recvs = 4, 5

    def __init__(self, me, order, acc, near, far, mid, tail, send, recv):
        self.me, self.order, self.acc = me, order, acc
        self.nears, self.fars, self.mid, self.tail = near, far, mid, tail
        self.send, self.recv = send, recv
        self.half = acc.shape[-2] // 2
        self.full = "".join(order[:2])

    def chunk(self, by):
        return shifted(self.me, self.order[2], by)

    def rows(self, way):
        return pl.ds(way * self.half, self.half)

    def add(self, spot, full, first, rows, terms):
        acc = self.acc

        def one(number, carry):
            index, inner = decode(number, spot, full)
            here = index + (pl.ds(first, rows),)
            total = acc[here]
            if len(terms) > 1:
                total = total.astype(F32)
            for ref, lead in terms:
                rows_there = pl.ds(first, rows) if ref.shape[-2] == acc.shape[-2] else slice(None)
                total += ref[(lead,) + inner + (rows_there,)].astype(total.dtype)
            acc[here] = total.astype(acc.dtype)
            return carry

        lax.fori_loop(0, math.prod(bundle_shape(full)), one, 0)

    def near(self, by, way):
        spot = self.chunk(by)
        box = self.nears.at[0 if by == 1 else 1]
        lead = (slice(None),) * (len(self.nears.shape) - 3)
        remote(
            view(self.acc, spot, self.full, None, self.rows(way)),
            box.at[lead + (self.rows(way),)],
            self.send.at[1],
            self.recv.at[2],
            device_at(spot),
        )

    def stage_far(self):
        spot = self.chunk(2)
        for way, by in enumerate((1, -1)):
            remote(
                view(self.acc, spot, self.full, None, self.rows(way)),
                self.fars.at[way],
                self.send.at[0],
                self.recv.at[way],
                device_at(self.chunk(by)),
            )
        for way, by in enumerate((1, -1)):
            self.near(by, 1 - way)

    def stage_near(self):
        for way, by in enumerate((1, -1)):
            take(self.fars.at[way], self.recv.at[way])
            self.add(self.chunk(by), self.full, way * self.half, self.half, [(self.fars, way)])
            self.near(by, way)

    def spread(self, axis, full, target, send, recv):
        for number, by in enumerate(STEPS):
            spot = shifted(self.me, axis, by)
            remote(
                view(self.acc, spot, full),
                target.at[number],
                self.send.at[send],
                self.recv.at[recv],
                device_at(spot),
            )

    def stage_mid(self):
        take(self.nears, self.recv.at[2])
        self.add(self.me, self.full, 0, 2 * self.half, [(self.nears, 0), (self.nears, 1)])
        self.spread(self.order[1], self.order[0], self.mid, 2, 3)

    def stage_tail(self):
        take(self.mid, self.recv.at[3])
        self.add(self.me, self.order[0], 0, 2 * self.half, [(self.mid, i) for i in range(3)])
        self.spread(self.order[0], "", self.tail, 3, 4)

    def stage_out(self):
        take(self.tail, self.recv.at[4])
        index, _ = decode(0, self.me, "")
        total = self.acc[index].astype(F32)
        for number in range(3):
            total += self.tail[number].astype(F32)
        return total

    def sent(self):
        take(self.fars, self.send.at[0])
        take(self.nears, self.send.at[1])
        take(self.mid, self.send.at[2])
        take(self.tail, self.send.at[3])


def reduce_scratch(order, lanes):
    full = bundle_shape(order[:2])
    return [
        pltpu.VMEM((4, 2, 2, 4, 64, lanes), BF16),
        pltpu.VMEM((2,) + full + (64, lanes), BF16),
        pltpu.VMEM((2,) + full + (32, lanes), BF16),
        pltpu.VMEM((3,) + bundle_shape(order[:1]) + (64, lanes), BF16),
        pltpu.VMEM((3, 64, lanes), BF16),
    ]


class Totals:
    def __init__(self, me, sums, inbox, send, recv):
        self.rounds = [[shifted(me, axis, by) for by in STEPS] for axis in "xyz"] + [[sibling(me)]]
        self.sums, self.inbox, self.send, self.recv = sums, inbox, send, recv

    def heard(self, number):
        return self.inbox.at[number, pl.ds(0, len(self.rounds[number]))]

    def speak(self, number):
        for i, spot in enumerate(self.rounds[number]):
            remote(
                self.sums.at[number],
                self.inbox.at[number, i],
                self.send.at[number],
                self.recv.at[number],
                device_at(spot),
            )

    def hear(self, number):
        take(self.heard(number), self.recv.at[number])
        total = self.sums[number]
        for i in range(len(self.rounds[number])):
            total += self.inbox[number, i]
        self.sums[number + 1] = total

    def pass_on(self, number):
        self.hear(number)
        self.speak(number + 1)

    def sent(self):
        for number in range(4):
            take(self.heard(number), self.send.at[number])


def norm_stats(values):
    average = jnp.mean(values, -1, keepdims=True)
    centered = values - average
    inverse = lax.rsqrt(jnp.mean(centered * centered, -1, keepdims=True) + EPSILON)
    return (centered * inverse, inverse)


def norm_back(upstream, normed, inverse, gain_vector):
    scaled = upstream * gain_vector
    return inverse * (
        scaled
        - jnp.mean(scaled, -1, keepdims=True)
        - normed * jnp.mean(scaled * normed, -1, keepdims=True)
    )


def softmax_columns(key_rows, queries, hidden):
    scores = mm(key_rows, queries, NT) + hidden
    powers = jnp.exp((scores - jnp.max(scores, 0, keepdims=True)) * SCALE)
    return powers * (1.0 / jnp.sum(powers, 0, keepdims=True))


def hidden_rows(seq, slot, tokens):
    row = lax.broadcasted_iota(jnp.int32, (seq, 1), 0)
    return jnp.where(lax.rem(row, slot) < tokens, 0.0, -1e30)


def head_lanes(head):
    lane = lax.broadcasted_iota(jnp.int32, (1, 128), 1)
    return jnp.where(lane // HD == head, 1.0, 0.0).astype(BF16)


def thirds(rows):
    return [rows[:, 128 * i : 128 * i + 128] for i in range(3)]


def attend(rows, hidden):
    queries, key_rows, value_rows = thirds(rows)

    def one_head(head, before):
        mine = head_lanes(head)
        probs = softmax_columns(key_rows, queries * mine, hidden).astype(BF16)
        return before + mm(probs, value_rows * mine, TN)

    return lax.fori_loop(0, 2, one_head, jnp.zeros(queries.shape, F32)).astype(BF16)


def attend_back(rows, grads, hidden):
    queries, key_rows, value_rows = thirds(rows)

    def one_head(head, before):
        mine = head_lanes(head)
        own_grads, own_queries = grads * mine, queries * mine
        probs = softmax_columns(key_rows, own_queries, hidden)
        d_probs = mm(value_rows, own_grads, NT)
        inner = jnp.sum(probs * d_probs, 0, keepdims=True)
        d_scores = (probs * (d_probs - inner)).astype(BF16)
        return (
            before[0] + mm(d_scores, key_rows * mine, TN),
            before[1] + mm(d_scores, own_queries),
            before[2] + mm(probs.astype(BF16), own_grads),
        )

    zero = jnp.zeros(queries.shape, F32)
    d_queries, d_keys, d_values = lax.fori_loop(0, 2, one_head, (zero, zero, zero))
    return [
        (d_queries * SCALE).astype(BF16),
        (d_keys * SCALE).astype(BF16),
        d_values.astype(BF16),
    ]


def fill_rows(box, m, values):
    tokens = values.shape[0]
    box[m, :tokens] = values
    box[m, tokens:] = jnp.zeros((box.shape[1] - tokens, values.shape[1]), box.dtype)


class Swap:
    def __init__(self, me, send, recv):
        self.stays = lax.rem(me["z"], 2) == me["c"]
        self.partner = crossed(me)
        self.send, self.recv = send, recv

    def start(self, box, inbox):
        @pl.when(self.stays)
        def _():
            pltpu.make_async_copy(box, inbox, self.recv).start()

        @pl.when(jnp.logical_not(self.stays))
        def _():
            remote(box, inbox, self.send, self.recv, self.partner)

    def sent(self, box):
        @pl.when(jnp.logical_not(self.stays))
        def _():
            take(box, self.send)


def blocks_of(ref, index):
    value = ref[index // 2, lax.rem(index, 2)]
    return value.reshape(-1, value.shape[-1])


def half_planes(ref, value, kind, count):
    padded = jnp.concatenate(
        [value, jnp.zeros((ref.shape[-1] - count, value.shape[1]), value.dtype)], axis=0
    )
    ref[kind] = padded.T.reshape(ref.shape[1:])


SCHEDULE = {
    "start": (("E", "first"),),
    "first": (("A", "first"), ("E", "second"), ("B", "first")),
    "swap": (("E", "third"), ("A", "second"), ("E", "far")),
    "norm": (("A", "third"), ("V", "rest"), ("V", "last"), ("V", "done")),
    "table": (("B", "second"), ("N", "rest"), ("N", "last"), ("A", "far"), ("N", "done")),
    "project": (("A", "rest"), ("B", "third")),
    "image 0": (("A", "last"),),
    "image 1": (("B", "far"),),
    "image 2": (("B", "rest"),),
    "reply": (("A", "done"), ("B", "last")),
    "half 0": (),
    "half 1": (("B", "done"),),
}


def forward_kernel(*refs):
    (x_ref, cot_ref, valid_ref, qkv_in, out_in, fc1_in, fc2_in), refs = refs[:7], refs[7:]
    small_in, refs = refs[:8], refs[8:]
    (
        d_middle_out,
        vectors,
        sums_out,
        result_out,
        d_attended_out,
        images_out,
        attended_out,
        turned_out,
        act_out,
        qkv_out,
        x_out,
        x_box,
        x_in,
        cot_box,
        cot_in,
        result_box,
        wq,
        wk,
        wv,
        up_a,
        up_b,
        side_a,
        down_xa,
        down_xb,
        down_zb,
        side_own,
        small_own,
        small,
        bias,
        hidden_bias,
        low,
        outbox,
        images,
        attended_box,
        attended,
        middle,
        normed_two,
        low_two,
        turned,
        forward_sum,
        back_sum,
        act_box,
        d_outbox,
        hidden_sums,
        local_sem,
        gather_send,
        gather_recv,
        send_sem,
        recv_sem,
        back_send,
        back_recv,
        store_sem,
        sib_send,
        sib_recv,
        ff_local,
        ff_send,
        ff_recv,
        swap_send,
        swap_recv,
    ) = refs
    me = place()
    core = me["c"]
    t = 2 * me["x"] + core
    other = device_at(sibling(me))
    micro, tokens, width = x_ref.shape
    slot = x_in.shape[1]
    count = micro * slot
    met = greet(me)
    heads = [wq, wk, wv]
    made = []

    def gather(order, block, out):
        i = len(made)
        made.append(
            Gather(me, order, block, out, gather_send.at[i], gather_recv.at[i], local_sem.at[i])
        )
        return made[-1]

    narrow = [gather(ORDERS[i], qkv_in.at[i], heads[i]) for i in range(3)]
    vector = gather(ORDERS[0], small_own, small)
    early = [vector] + narrow
    first_half = [
        gather(ORDERS[2], fc1_in.at[:, :256], up_a),
        gather(ORDERS[0], side_own, side_a),
        gather(ORDERS[1], fc2_in.at[:, :128], down_xa),
    ]
    second_half = [
        gather(ORDERS[0], fc1_in.at[:, 256:], up_b),
        gather(ORDERS[2], fc2_in.at[:, 256:384], down_xb),
        gather(ORDERS[2], fc2_in.at[:, 384:], down_zb),
    ]
    groups = {
        "V": [vector],
        "N": narrow,
        "E": early,
        "A": first_half,
        "B": second_half,
    }

    def run(point):
        for names, stage in SCHEDULE[point]:
            for name in names:
                for part in groups[name]:
                    getattr(part, stage)()

    stores = []

    def store(src, dst):
        copy = pltpu.make_async_copy(src, dst, store_sem.at[len(stores)])
        copy.start()
        stores.append(copy)

    shared = []

    def share(src, dst):
        slot_of = len(shared)
        copy = pltpu.make_async_remote_copy(
            src,
            dst,
            sib_send.at[slot_of],
            sib_recv.at[slot_of],
            device_id=other,
            device_id_type=MESH,
        )
        copy.start()
        shared.append(copy)

    def turn(kind, value):
        half_planes(turned, value, kind, count)
        store(turned.at[kind, :, core], turned_out.at[kind, 0])
        share(turned.at[kind, :, 1 - core], turned_out.at[kind, 1])

    for m in range(micro):
        fill_rows(x_box, m, x_ref[m])
    side_own[:, :128] = out_in[...]
    side_own[:, 128:] = fc2_in[:, 128:256]
    small_own[...] = jnp.zeros_like(small_own)
    for v in range(6):
        small_own[0:1, 8 * v : 8 * v + 8] = small_in[v][...]
    for i in range(2):
        for j in range(2):
            at = 48 + 8 * i + 4 * j
            small_own[0:1, at : at + 4] = small_in[6][i, j : j + 1]
    for i in range(4):
        small_own[0:1, 64 + 8 * i : 72 + 8 * i] = small_in[7][i : i + 1]
    met()
    run("start")
    swaps = [Swap(me, swap_send.at[i], swap_recv.at[i]) for i in range(3)]
    swaps[0].start(x_box, x_in)
    run("first")
    for m in range(micro):
        fill_rows(cot_box, m, (cot_ref[m].astype(F32) * valid_ref[0, m].astype(F32)).astype(BF16))
    run("swap")
    take(x_in, swap_recv.at[0])
    store(x_in, x_out)

    def rows_of(ref):
        return ref[...].reshape(count, width).astype(F32)

    normed, _ = norm_stats(rows_of(x_in))
    run("norm")
    table = jnp.sum(small[...].reshape(128, 32, 128).astype(F32), 1).astype(BF16)
    lane = lax.broadcasted_iota(jnp.int32, (128, 1024), 0)
    column = lax.broadcasted_iota(jnp.int32, (128, 1024), 1)
    owner = jnp.where(lax.rem(lane, 16) * 8 + lane // 16 == column // 8, 1.0, 0.0)
    for v in range(6):
        pick = jnp.where(lane == v * 8 + lax.rem(column, 8), 1.0, 0.0).astype(BF16)
        vectors[v : v + 1, :] = jnp.sum(mm(table, pick) * owner, 0, keepdims=True)
    vectors[6:8, :] = jnp.zeros((2, 1024), F32)

    def spread_bias(lanes, first, major, minor):
        lane = lax.broadcasted_iota(jnp.int32, (128, lanes), 0)
        column = lax.broadcasted_iota(jnp.int32, (128, lanes), 1)
        pick = lane == first + (column // 64) * major + lax.rem(column, 4) * minor
        owner = lax.rem(lane, 16) == lax.rem(column, 64) // 4
        values = mm(table, jnp.where(pick, 1.0, 0.0).astype(BF16))
        return jnp.sum(jnp.where(owner, values, 0.0).reshape(8, 16, lanes), 1)

    hidden_value = spread_bias(512, 64, 1, 8)
    query_bias, value_bias = spread_bias(128, 48, 4, 1), spread_bias(128, 56, 4, 1)
    for i in range(GROUP):
        hidden_bias[i] = hidden_value[i : i + 1]
        bias[i, :, 0:128] = query_bias[i : i + 1]
        bias[i, :, 128:256] = jnp.zeros((1, 128), F32)
        bias[i, :, 256:384] = value_bias[i : i + 1]
    low[...] = (normed * vectors[0:1, :] + vectors[1:2, :]).astype(BF16)
    run("table")

    def letter(k, m):
        target = lax.rem(t + k + 1, GROUP)
        return pltpu.make_async_remote_copy(
            outbox.at[target, m],
            images.at[t, m],
            send_sem,
            recv_sem.at[m],
            device_id=member(me, target),
            device_id_type=MESH,
        )

    def project(k, carry):
        target = lax.rem(t + k + 1, GROUP)
        weights = jnp.concatenate([blocks_of(w, target) for w in heads], axis=1)
        result = (mm(low[...], weights) + bias[target]).astype(BF16)
        outbox[target] = result.reshape(outbox.shape[1:])

        @pl.when(k < GROUP - 1)
        def _():
            letter(k, 0).start()

        return carry

    lax.fori_loop(0, GROUP, project, 0)
    for m in range(1, MICRO):
        for k in range(GROUP - 1):
            letter(k, m).start()
    own = pltpu.make_async_copy(outbox.at[t], images.at[t], local_sem.at[len(made)])
    own.start()
    for i in range(3):
        store(heads[i], qkv_out.at[i])
    swaps[1].start(cot_box, cot_in)
    run("project")
    turn(0, low[...])
    own.wait()
    hidden = hidden_rows(GROUP * slot, slot, tokens)

    def reply(m, k):
        target = lax.rem(t + k + 1, GROUP)
        return pltpu.make_async_remote_copy(
            attended_box.at[m, target],
            attended.at[t, m],
            back_send,
            back_recv,
            device_id=member(me, target),
            device_id_type=MESH,
        )

    for m in range(MICRO):
        take(images.at[: GROUP - 1, m], recv_sem.at[m])
        result = attend(images[:, m].reshape(GROUP * slot, 384), hidden)
        attended_box[m] = result.reshape(GROUP, slot, 128)
        for k in range(GROUP - 1):
            reply(m, k).start()
        attended[t, m] = attended_box[m, t]
        run(("image 0", "image 1", "image 2")[m])
        if m == 1:
            take(cot_in, swap_recv.at[1])
            upstream_low = cot_in[...].reshape(count, width)
            sums_out[3:4, :] = jnp.sum(upstream_low.astype(F32), 0, keepdims=True)
            turn(1, upstream_low)
    store(images, images_out)
    take(attended.at[: GROUP - 1], back_recv)
    store(attended, attended_out.at[0])
    share(attended, attended_out.at[1])
    run("reply")
    middle[...] = rows_of(x_in) + vectors[2:3, :]

    def out_weights(pair):
        both = [blocks_of(side_a, 2 * pair + i)[:, :128] for i in range(2)]
        return jnp.concatenate(both, axis=1)

    def out_project(pair, carry):
        both = [attended[2 * pair + i].reshape(count, 128) for i in range(2)]
        middle[...] += mm(jnp.concatenate(both, axis=1), out_weights(pair), NT)
        return carry

    lax.fori_loop(0, GROUP // 2, out_project, 0)
    normed, inverse = norm_stats(middle[...])
    normed_two[...] = normed
    low_two[...] = (normed * vectors[3:4, :] + vectors[4:5, :]).astype(BF16)
    turn(2, low_two[...])
    forward_sum[...] = jnp.zeros_like(forward_sum)
    back_sum[...] = jnp.zeros_like(back_sum)

    def ship(pair, h):
        piece = act_box.at[pl.ds(2 * pair, 2), :, pl.ds(2 * count * h, 2 * count)]
        at = (pl.ds(2 * pair, 2), slice(None), pl.ds(2 * count * h, 2 * count))
        pltpu.make_async_copy(piece, act_out.at[(0,) + at], ff_local).start()
        remote(piece, act_out.at[(1,) + at], ff_send, ff_recv, other)

    for h in range(2):
        run(("half 0", "half 1")[h])

        def feed_forward(pair, carry):
            slabs = [2 * pair, 2 * pair + 1]
            up_weight = jnp.concatenate([blocks_of((up_a, up_b)[h], i) for i in slabs], axis=1)
            down = []
            for i in slabs:
                down.append(blocks_of((down_xa, down_xb)[h], i))
                down.append(blocks_of(side_a, i)[:, 128:] if h == 0 else blocks_of(down_zb, i))
            down_weight = jnp.concatenate(down, axis=1)
            biases = [hidden_bias[i, :, 256 * h : 256 * h + 256] for i in slabs]
            up_proj = mm(low_two[...], up_weight) + jnp.concatenate(biases, axis=1)
            gate = jax.nn.sigmoid(1.702 * up_proj)
            activated = (up_proj * gate).astype(BF16)
            d_act = mm(cot_in[...].reshape(count, width), down_weight)
            d_up = (d_act * (gate + 1.702 * up_proj * gate * (1.0 - gate))).astype(BF16)
            column_sums = jnp.sum(d_up.astype(F32), 0, keepdims=True)
            for n, i in enumerate(slabs):
                for j in range(2):
                    at = pl.ds(count * (2 * h + j), count)
                    lanes = slice(256 * n + 128 * j, 256 * n + 128 * (j + 1))
                    act_box[i, 0, at] = activated[:, lanes]
                    act_box[i, 1, at] = d_up[:, lanes]
                hidden_sums[i, :, 256 * h : 256 * h + 256] = column_sums[:, 256 * n : 256 * n + 256]
            ship(pair, h)
            forward_sum[...] += mm(activated, down_weight, NT)
            back_sum[...] += mm(d_up, up_weight, NT)
            return carry

        lax.fori_loop(0, GROUP // 2, feed_forward, 0)
    output = (middle[...] + forward_sum[...] + vectors[5:6, :]).astype(BF16)
    result_box[...] = output.reshape(result_box.shape)
    swaps[2].start(result_box, result_out)
    d_norm = back_sum[...]
    normed = normed_two[...]
    d_middle = rows_of(cot_in) + norm_back(
        d_norm, normed, inverse, vectors[3:4, :]
    )
    d_middle_out[...] = d_middle
    low[...] = d_middle.astype(BF16)

    def project_back(pair, carry):
        both = mm(low[...], out_weights(pair)).astype(BF16)
        for i in range(2):
            d_outbox[2 * pair + i] = both[:, 128 * i : 128 * i + 128].reshape(d_outbox.shape[1:])
        return carry

    lax.fori_loop(0, GROUP // 2, project_back, 0)
    store(d_outbox, d_attended_out)
    turn(3, low[...])
    sums_out[0:1, :] = jnp.sum(d_middle, 0, keepdims=True)
    sums_out[1:2, :] = jnp.sum(d_norm * normed, 0, keepdims=True)
    sums_out[2:3, :] = jnp.sum(d_norm, 0, keepdims=True)
    for i in range(GROUP):
        at = 4 + i // 2
        sums_out[at : at + 1, 512 * (i % 2) : 512 * (i % 2) + 512] = hidden_sums[i]
    for swap, box in zip(swaps, (x_box, cot_box, result_box)):
        swap.sent(box)
    take(result_out, swap_recv.at[2])
    for copy in shared:
        copy.wait()
    take(act_box, ff_local)
    take(act_box, ff_send)
    take(act_box, ff_recv)
    for part in made:
        part.sent()
    take(outbox.at[: GROUP - 1], send_sem)
    take(attended_box.at[:, : GROUP - 1], back_send)
    for copy in stores:
        copy.wait()


ANY = pl.BlockSpec(memory_space=pl.ANY)
VMEM = pl.BlockSpec(memory_space=pltpu.VMEM)
SMEM = pl.BlockSpec(memory_space=pltpu.SMEM)


def forward(x, cotangent, valid, qkv_block, out_block, fc1_block, fc2_block, small, slot):
    width = x.shape[-1]
    count = MICRO * slot
    rows = (MICRO, slot, width)
    images = (GROUP, MICRO, slot, 384)
    attended = (GROUP, MICRO, slot, 128)
    acts = (2, GROUP, 2, 4 * count, 128)
    return pl.pallas_call(
        forward_kernel,
        out_shape=[
            jax.ShapeDtypeStruct((count, width), F32),
            jax.ShapeDtypeStruct((8, width), F32),
            jax.ShapeDtypeStruct((8, width), F32),
            jax.ShapeDtypeStruct(rows, BF16),
            jax.ShapeDtypeStruct(attended, BF16),
            jax.ShapeDtypeStruct(images, BF16),
            jax.ShapeDtypeStruct((2,) + attended, BF16),
            jax.ShapeDtypeStruct((4, 2, 8, 64, 256), BF16),
            jax.ShapeDtypeStruct(acts, BF16),
            jax.ShapeDtypeStruct((3,) + LEAD + (64, 128), BF16),
            jax.ShapeDtypeStruct(rows, BF16),
        ],
        in_specs=[VMEM, VMEM, SMEM, ANY, VMEM, ANY, VMEM] + [VMEM] * 8,
        out_specs=[VMEM] * 3 + [ANY] * 8,
        scratch_shapes=[
            pltpu.VMEM(rows, BF16),
            pltpu.VMEM(rows, BF16),
            pltpu.VMEM(rows, BF16),
            pltpu.VMEM(rows, BF16),
            pltpu.VMEM(rows, BF16),
            pltpu.VMEM(LEAD + (64, 128), BF16),
            pltpu.VMEM(LEAD + (64, 128), BF16),
            pltpu.VMEM(LEAD + (64, 128), BF16),
            pltpu.VMEM(LEAD + (64, 256), BF16),
            pltpu.VMEM(LEAD + (64, 256), BF16),
            pltpu.VMEM(LEAD + (64, 256), BF16),
            pltpu.VMEM(LEAD + (64, 128), BF16),
            pltpu.VMEM(LEAD + (64, 128), BF16),
            pltpu.VMEM(LEAD + (64, 128), BF16),
            pltpu.VMEM((64, 256), BF16),
            pltpu.VMEM((32, 128), BF16),
            pltpu.VMEM(LEAD + (32, 128), BF16),
            pltpu.VMEM((GROUP, 1, 384), F32),
            pltpu.VMEM((GROUP, 1, 512), F32),
            pltpu.VMEM((count, width), BF16),
            pltpu.VMEM(images, BF16),
            pltpu.VMEM(images, BF16),
            pltpu.VMEM((MICRO, GROUP, slot, 128), BF16),
            pltpu.VMEM(attended, BF16),
            pltpu.VMEM((count, width), F32),
            pltpu.VMEM((count, width), F32),
            pltpu.VMEM((count, width), BF16),
            pltpu.VMEM((4, 8, 2, 64, 256), BF16),
            pltpu.VMEM((count, width), F32),
            pltpu.VMEM((count, width), F32),
            pltpu.VMEM(acts[1:], BF16),
            pltpu.VMEM(attended, BF16),
            pltpu.VMEM((GROUP, 1, 512), F32),
            pltpu.SemaphoreType.DMA((12,)),
            pltpu.SemaphoreType.DMA((10, Gather.sends)),
            pltpu.SemaphoreType.DMA((10, Gather.recvs)),
            pltpu.SemaphoreType.DMA,
            pltpu.SemaphoreType.DMA((MICRO,)),
            pltpu.SemaphoreType.DMA,
            pltpu.SemaphoreType.DMA,
            pltpu.SemaphoreType.DMA((11,)),
            pltpu.SemaphoreType.DMA((5,)),
            pltpu.SemaphoreType.DMA((5,)),
            pltpu.SemaphoreType.DMA,
            pltpu.SemaphoreType.DMA,
            pltpu.SemaphoreType.DMA,
            pltpu.SemaphoreType.DMA((3,)),
            pltpu.SemaphoreType.DMA((3,)),
        ],
        compiler_params=pltpu.CompilerParams(
            collective_id=0, has_side_effects=True, vmem_limit_bytes=VMEM_LIMIT
        ),
        name="forward",
    )(x, cotangent, valid, qkv_block, out_block, fc1_block, fc2_block, *small)


BACK_SCHEDULE = {
    "image 0": (("down", 0), (0, -1), ("U", "stage_near")),
    "image 1": (("V", "stage_near"), (0, 0)),
    "image 2": (("D", "stage_near"), (0, 1)),
    "norm": (("U", "stage_mid"), ("V", "stage_mid"), ("D", "stage_mid"), (0, 2)),
    "late": ((0, 3), ("L", "stage_near")),
    "rows": (
        (1, 0),
        ("L", "stage_mid"),
        (1, 1),
        ("U", "stage_tail"),
        ("V", "stage_tail"),
        ("D", "stage_tail"),
        ("L", "stage_tail"),
        (1, 2),
    ),
    "wide": (),
    "end": ((1, 3),),
}


def backward_kernel(*refs):
    (
        d_attended_in,
        images_in,
        attended_in,
        turned_in,
        act_in,
        qkv_in,
        x_in,
        d_middle_ref,
        vectors_ref,
        sums_ref,
        qkv_grad,
        out_grad,
        fc1_grad,
        fc2_grad,
        totals_out,
        input_grad_out,
        rows,
        box,
        pool,
        turned,
        attended,
        images,
        d_attended,
        outbox,
        d_images,
        d_norm,
        sums,
        sums_in,
        *rest,
    ) = refs
    scratch, sems = rest[: 5 * len(REDUCED)], rest[5 * len(REDUCED) :]
    (
        load_sem,
        reduce_send,
        reduce_recv,
        send_sem,
        recv_sem,
        back_send,
        back_recv,
        sib_send,
        sib_recv,
        sum_send,
        sum_recv,
        swap_send,
        swap_recv,
    ) = sems
    me = place()
    t = 2 * me["x"] + me["c"]
    other = device_at(sibling(me))
    met = greet(me)
    slot = rows.shape[1]
    count = MICRO * slot
    parts = [
        Reduce(
            me,
            REDUCED[i][0],
            *scratch[5 * i : 5 * i + 5],
            reduce_send.at[i],
            reduce_recv.at[i],
        )
        for i in range(len(REDUCED))
    ]
    late = parts[-3:]
    wide = parts[:-3]
    totals = [
        Totals(me, sums.at[i], sums_in.at[i], sum_send.at[i], sum_recv.at[i]) for i in range(2)
    ]
    loads = {}

    def load(name, src, dst):
        loads[name] = pltpu.make_async_copy(src, dst, load_sem.at[len(loads)])
        loads[name].start()

    kept = pl.ds(0, 4 * count)
    load("turned", turned_in, turned)
    for i in range(2):
        load(("dup", i), act_in.at[i, :, 1], pool.at[2 + i, :, kept])
    load("images", images_in, images)
    load("own", d_attended_in.at[t], d_attended.at[t])
    for i in range(2):
        load(("act", i), act_in.at[i, :, 0], pool.at[i, :, kept])
    load("attended", attended_in, attended)
    load("rows", x_in, rows)
    sums[0, 0] = sums_ref[...]

    def both_cores(kind, values):
        total = 0.0
        for i in range(2):
            left = turned[kind, i].reshape(512, 256)[:, :count]
            total += mm(left, values[i])
        return total.astype(BF16)

    def pooled(first, index, lanes):
        return [
            jnp.concatenate(
                [pool[first + i, index, count * j : count * (j + 1)] for j in lanes], axis=1
            )
            for i in range(2)
        ]

    def spot_of(index):
        return (index // 2, lax.rem(index, 2))

    def fill(part, index, lanes, value):
        acc = part.acc
        acc[spot_of(index) + (slice(None),) * 3 + (lanes,)] = value.reshape(
            acc.shape[2:-1] + (value.shape[-1],)
        )

    def grads_up(half):
        def one(index, carry):
            value = both_cores(2, pooled(2, index, (2 * half, 2 * half + 1)))
            fill(wide[half], index, slice(0, 256), value)
            return carry

        return one

    def grads_down(index, carry):
        value = both_cores(1, pooled(0, index, range(4)))
        fill(wide[2], index, slice(0, 128), value[:, :128])
        fill(wide[3], index, slice(0, 256), value[:, 128:384])
        fill(wide[4], index, slice(0, 128), value[:, 384:])
        value = both_cores(3, [attended[i, index].reshape(count, 128) for i in range(2)])
        fill(wide[4], index, slice(128, 256), value)
        return carry

    loads["turned"].wait()
    for i in range(2):
        loads["dup", i].wait()
    met()
    for m in range(MICRO):
        for k in range(GROUP - 1):
            target = lax.rem(t + k + 1, GROUP)
            remote(
                d_attended_in.at[target, m],
                d_attended.at[t, m],
                send_sem,
                recv_sem.at[m],
                member(me, target),
            )
    lax.fori_loop(0, GROUP, grads_up(0), 0)
    wide[0].stage_far()
    lax.fori_loop(0, GROUP, grads_up(1), 0)
    wide[1].stage_far()
    loads["images"].wait()
    loads["own"].wait()
    hidden = hidden_rows(GROUP * slot, slot, TOKENS)

    def reply(m, k):
        target = lax.rem(t + k + 1, GROUP)
        return pltpu.make_async_remote_copy(
            outbox.at[m, target],
            d_images.at[0, t, m],
            back_send,
            back_recv.at[k],
            device_id=member(me, target),
            device_id_type=MESH,
        )

    def down():
        for i in range(2):
            loads["act", i].wait()
        loads["attended"].wait()
        lax.fori_loop(0, GROUP, grads_down, 0)
        for part in wide[2:]:
            part.stage_far()
        for i in range(3):
            load(("weight", i), qkv_in.at[i], pool.at[i])

    groups = {"U": wide[:1], "V": wide[1:2], "D": wide[2:], "L": late}

    def run(point):
        for name, stage in BACK_SCHEDULE[point]:
            if name == "down":
                down()
            elif name in groups:
                for part in groups[name]:
                    getattr(part, stage)()
            elif stage < 0:
                totals[name].speak(0)
            elif stage < 3:
                totals[name].pass_on(stage)
            else:
                totals[name].hear(3)

    for m in range(MICRO):
        take(d_attended.at[: GROUP - 1, m], recv_sem.at[m])
        results = attend_back(
            images[:, m].reshape(GROUP * slot, 384),
            d_attended[:, m].reshape(GROUP * slot, 128),
            hidden,
        )
        for i in range(3):
            outbox[m, :, :, 128 * i : 128 * i + 128] = results[i].reshape(GROUP, slot, 128)
        for k in range(GROUP - 1):
            reply(m, k).start()
        d_images[0, t, m] = outbox[m, t]
        run(("image 0", "image 1", "image 2")[m])
    loads["rows"].wait()
    normed, inverse = norm_stats(rows[...].reshape(count, rows.shape[-1]).astype(F32))
    run("norm")

    def share(k):
        source = lax.rem(t + k + 1, GROUP)
        remote(d_images.at[0, source], d_images.at[1, source], sib_send, sib_recv, other)

    share(GROUP - 1)
    for k in reversed(range(GROUP - 1)):
        take(d_images.at[0, 0], back_recv.at[GROUP - 2 - k])
        share(k)
    for i in range(3):
        loads["weight", i].wait()
    d_norm[...] = jnp.zeros_like(d_norm)

    def project_back(index, carry):
        weights = jnp.concatenate([pool[i, index] for i in range(3)], axis=1)
        d_norm[...] += mm(d_images[0, index].reshape(count, 384), weights, NT)
        return carry

    lax.fori_loop(0, GROUP, project_back, 0)
    take(d_images.at[1], sib_recv)

    def grads_late(index, carry):
        value = both_cores(0, [d_images[i, index].reshape(count, 384) for i in range(2)])
        for i, part in enumerate(late):
            fill(part, index, slice(None), value[:, 128 * i : 128 * i + 128])
        return carry

    lax.fori_loop(0, GROUP, grads_late, 0)
    for part in late:
        part.stage_far()
    gradient = d_norm[...]
    sums[1, 0, 0:1, :] = jnp.sum(gradient * normed, 0, keepdims=True)
    sums[1, 0, 1:2, :] = jnp.sum(gradient, 0, keepdims=True)
    for index in range(GROUP):
        grads = jnp.sum(d_images[0, index].reshape(count, 384).astype(F32), 0, keepdims=True)
        sums[1, 0, 2:3, 128 * index : 128 * index + 128] = grads[:, :128]
        sums[1, 0, 3:4, 128 * index : 128 * index + 128] = grads[:, 256:]
    sums[1, 0, 4:8, :] = jnp.zeros((4, sums.shape[-1]), F32)
    totals[1].speak(0)
    run("late")
    result = d_middle_ref[...] + norm_back(gradient, normed, inverse, vectors_ref[0:1, :])
    box[...] = result.astype(BF16).reshape(box.shape)
    swap = Swap(me, swap_send, swap_recv)
    swap.start(box, input_grad_out)
    run("rows")
    fc1_grad[:, :256] = wide[0].stage_out()
    fc1_grad[:, 256:] = wide[1].stage_out()
    fc2_grad[:, :128] = wide[2].stage_out()
    fc2_grad[:, 128:384] = wide[3].stage_out()
    value = wide[4].stage_out()
    fc2_grad[:, 384:] = value[:, :128]
    out_grad[...] = value[:, 128:]
    run("wide")
    for i in range(3):
        qkv_grad[i] = late[i].stage_out()
    run("end")
    totals_out[0:8, :] = sums[0, 4]
    totals_out[8:16, :] = sums[1, 4]
    for part in parts:
        part.sent()
    for total in totals:
        total.sent()
    take(d_images.at[1], sib_send)
    take(outbox.at[:, : GROUP - 1], back_send)
    take(d_attended.at[: GROUP - 1], send_sem)
    swap.sent(box)
    take(input_grad_out, swap_recv)


REDUCED = (
    (ORDERS[2], 256),
    (ORDERS[0], 256),
    (ORDERS[1], 128),
    (ORDERS[2], 256),
    (ORDERS[0], 256),
    (ORDERS[0], 128),
    (ORDERS[1], 128),
    (ORDERS[2], 128),
)


def backward(d_attended, images, attended, turned, act, qkv, x, d_middle, vectors, sums):
    width = x.shape[-1]
    slot = x.shape[1]
    count = MICRO * slot
    scratch = []
    for order, lanes in REDUCED:
        scratch += reduce_scratch(order, lanes)
    return pl.pallas_call(
        backward_kernel,
        out_shape=[
            jax.ShapeDtypeStruct((3, 64, 128), F32),
            jax.ShapeDtypeStruct((64, 128), F32),
            jax.ShapeDtypeStruct((64, 512), F32),
            jax.ShapeDtypeStruct((64, 512), F32),
            jax.ShapeDtypeStruct((16, width), F32),
            jax.ShapeDtypeStruct(x.shape, BF16),
        ],
        in_specs=[ANY] * 7 + [VMEM] * 3,
        out_specs=[VMEM] * 5 + [ANY],
        scratch_shapes=[
            pltpu.VMEM(x.shape, BF16),
            pltpu.VMEM(x.shape, BF16),
            pltpu.VMEM((4, GROUP, width, 128), BF16),
            pltpu.VMEM(turned.shape, BF16),
            pltpu.VMEM(attended.shape, BF16),
            pltpu.VMEM(images.shape, BF16),
            pltpu.VMEM(d_attended.shape, BF16),
            pltpu.VMEM((MICRO, GROUP, slot, 384), BF16),
            pltpu.VMEM((2,) + images.shape, BF16),
            pltpu.VMEM((count, width), F32),
            pltpu.VMEM((2, 5, 8, width), F32),
            pltpu.VMEM((2, 4, 3, 8, width), F32),
        ]
        + scratch
        + [
            pltpu.SemaphoreType.DMA((12,)),
            pltpu.SemaphoreType.DMA((len(REDUCED), Reduce.sends)),
            pltpu.SemaphoreType.DMA((len(REDUCED), Reduce.recvs)),
            pltpu.SemaphoreType.DMA,
            pltpu.SemaphoreType.DMA((MICRO,)),
            pltpu.SemaphoreType.DMA,
            pltpu.SemaphoreType.DMA((GROUP,)),
            pltpu.SemaphoreType.DMA,
            pltpu.SemaphoreType.DMA,
            pltpu.SemaphoreType.DMA((2, 4)),
            pltpu.SemaphoreType.DMA((2, 4)),
            pltpu.SemaphoreType.DMA,
            pltpu.SemaphoreType.DMA,
        ],
        compiler_params=pltpu.CompilerParams(
            collective_id=1, has_side_effects=True, vmem_limit_bytes=VMEM_LIMIT
        ),
        name="backward",
    )(d_attended, images, attended, turned, act, qkv, x, d_middle, vectors, sums)


def finish_kernel(
    result,
    input_grad,
    qkv_grad,
    out_grad,
    fc1_grad,
    fc2_grad,
    totals,
    result_out,
    input_grad_out,
    qkv_out,
    out_out,
    fc1_out,
    fc2_out,
    vectors_out,
    pair_out,
    hidden_out,
):
    f, t = lax.axis_index("fsdp"), lax.axis_index("tp")
    tokens = result_out.shape[1]
    result_out[...] = result[:, :tokens]
    input_grad_out[...] = input_grad[:, :tokens]
    qkv_out[...] = qkv_grad[...]
    out_out[...] = out_grad[...]
    fc1_out[...] = fc1_grad[...]
    fc2_out[...] = fc2_grad[...]
    width = totals.shape[-1]
    own = pltpu.roll(totals[...], lax.rem(width - (f * 8 + t) * 8, width), 1)
    for number, row in enumerate((8, 9, 0, 1, 2, 3)):
        vectors_out[number] = own[row : row + 1, :8]
    own = pltpu.roll(totals[...], lax.rem(width - t * 128 - f * 4, width), 1)
    for kind in range(2):
        for head in range(2):
            pair_out[kind, head : head + 1, :] = own[
                10 + kind : 11 + kind, HD * head : HD * head + 4
            ]
    row = totals[4:8, :]
    mine = lax.broadcasted_iota(jnp.int32, row.shape, 0) == t // 2
    row = jnp.sum(jnp.where(mine, row, 0.0), 0, keepdims=True)
    row = pltpu.roll(
        jnp.broadcast_to(row, (8, width)), lax.rem(width - 512 * lax.rem(t, 2) - f * 4, width), 1
    )
    for j in range(8):
        hidden_out[j : j + 1, :] = row[0:1, 64 * j : 64 * j + 4]


def finish(result, input_grad, qkv_grad, out_grad, fc1_grad, fc2_grad, totals):
    arrays = (result, input_grad, qkv_grad, out_grad, fc1_grad, fc2_grad)
    rows = jax.ShapeDtypeStruct((MICRO, TOKENS, result.shape[-1]), BF16)
    shapes = [rows, rows] + [jax.ShapeDtypeStruct(a.shape, a.dtype) for a in arrays[2:]]
    shapes += [
        jax.ShapeDtypeStruct((6, 1, 8), F32),
        jax.ShapeDtypeStruct((2, 2, 4), F32),
        jax.ShapeDtypeStruct((8, 4), F32),
    ]
    return pl.pallas_call(
        finish_kernel,
        out_shape=shapes,
        in_specs=[VMEM] * 7,
        out_specs=[VMEM] * 9,
        compiler_params=pltpu.CompilerParams(vmem_limit_bytes=VMEM_LIMIT),
        name="finish",
    )(*arrays, totals)


def per_device(
    inputs,
    cotangent,
    valid_slots,
    ln1_gain,
    ln1_bias,
    qkv_weight,
    qv_bias,
    out_weight,
    out_bias,
    ln2_gain,
    ln2_bias,
    fc1_weight,
    fc1_bias,
    fc2_weight,
    fc2_bias,
):
    micro, _, tokens, width = inputs.shape
    slot = -(-tokens // 16) * 16
    x = inputs.reshape(micro, tokens, width)
    small = [ln1_gain, ln1_bias, out_bias, ln2_gain, ln2_bias, fc2_bias]
    small = [v.reshape(1, 8) for v in small] + [qv_bias, fc1_bias.T]
    (
        d_middle,
        vectors,
        sums,
        result,
        d_attended,
        images,
        attended,
        turned,
        act,
        qkv,
        x_rows,
    ) = forward(
        x,
        cotangent.reshape(x.shape),
        valid_slots.T,
        qkv_weight,
        out_weight.T,
        fc1_weight,
        fc2_weight.T,
        small,
        slot,
    )
    qkv_grad, out_grad, fc1_grad, fc2_grad, total, input_grad = backward(
        d_attended,
        images,
        attended,
        turned,
        act,
        qkv.reshape(3, GROUP, width, 128),
        x_rows,
        d_middle,
        vectors,
        sums,
    )
    result, input_grad, qkv_grad, out_grad, fc1_grad, fc2_grad, own, pair, hidden_grad = finish(
        result, input_grad, qkv_grad, out_grad, fc1_grad, fc2_grad, total
    )
    own = [own[i].reshape(8) for i in range(6)]
    return (
        result.reshape(inputs.shape),
        input_grad.reshape(inputs.shape),
        own[0],
        own[1],
        qkv_grad,
        pair,
        out_grad.T,
        own[2],
        own[3],
        own[4],
        fc1_grad,
        hidden_grad,
        fc2_grad.T,
        own[5],
    )


def solution(mesh):
    in_specs = (
        P(None, "fsdp", "tp", None),
        P(None, "fsdp", "tp", None),
        P(None, "fsdp"),
        P(("fsdp", "tp")),
        P(("fsdp", "tp")),
        P(None, "fsdp", "tp"),
        P(None, "tp", "fsdp"),
        P("tp", "fsdp"),
        P(("fsdp", "tp")),
        P(("fsdp", "tp")),
        P(("fsdp", "tp")),
        P("fsdp", "tp"),
        P("tp", "fsdp"),
        P("tp", "fsdp"),
        P(("fsdp", "tp")),
    )
    out_specs = (
        P(None, "fsdp", "tp", None),
        P(None, "fsdp", "tp", None),
        P(("fsdp", "tp")),
        P(("fsdp", "tp")),
        P(None, "fsdp", "tp"),
        P(None, "tp", "fsdp"),
        P("tp", "fsdp"),
        P(("fsdp", "tp")),
        P(("fsdp", "tp")),
        P(("fsdp", "tp")),
        P("fsdp", "tp"),
        P("tp", "fsdp"),
        P("tp", "fsdp"),
        P(("fsdp", "tp")),
    )
    return jax.shard_map(
        per_device, mesh=mesh, in_specs=in_specs, out_specs=out_specs, check_vma=False
    )
```

```python
import functools
import math

import jax
import jax.numpy as jnp
from jax import lax
from jax.experimental import pallas as pl
from jax.experimental.pallas import tpu as pltpu
from jax.sharding import PartitionSpec as P

MESH = pl.DeviceIdType.MESH
HD = 64
SCALE = 1.0 / math.sqrt(HD)
EPSILON = 1e-05
BF16 = jnp.bfloat16
F32 = jnp.float32
VMEM_LIMIT = 62 * 2**20
MICRO, GROUP, TOKENS = 3, 8, 72
ORDERS = (("x", "y", "z"), ("y", "z", "x"), ("z", "x", "y"))
SIZES = {"x": (4,), "z": (2, 2), "y": (4,)}
LEAD = (4, 2, 2, 4, 2)
STEPS = (1, -1, 2)
NN = (((1,), (0,)), ((), ()))
NT = (((1,), (1,)), ((), ()))
TN = (((0,), (0,)), ((), ()))


def mm(a, b, dims=NN):
    return lax.dot_general(a, b, dims, preferred_element_type=F32)


def place():
    f, t = lax.axis_index("fsdp"), lax.axis_index("tp")
    return {
        "x": t // 2,
        "y": lax.rem(f // 2, 4),
        "z": (f // 8) * 2 + lax.rem(t, 2),
        "c": lax.rem(f, 2),
    }


def device_at(spot):
    return (
        (spot["z"] // 2) * 8 + spot["y"] * 2 + spot["c"],
        spot["x"] * 2 + lax.rem(spot["z"], 2),
    )


def shifted(spot, axis, by):
    return {**spot, axis: lax.rem(spot[axis] + by + 4, 4)}


def sibling(spot):
    return {**spot, "c": 1 - spot["c"]}


def member(me, number):
    return device_at({**me, "x": number // 2, "c": lax.rem(number, 2)})


def crossed(me):
    return device_at({**me, "z": me["z"] + 1 - 2 * lax.rem(me["z"], 2), "c": 1 - me["c"]})


def greet(me):
    rank = 2 * me["x"] + me["c"]
    devices = [member(me, lax.rem(rank + step, GROUP)) for step in range(1, GROUP)]
    devices += [device_at(shifted(me, axis, by)) for axis in "yz" for by in STEPS]
    devices += [crossed(me)]
    barrier = pltpu.get_barrier_semaphore()
    for device in devices:
        pl.semaphore_signal(barrier, inc=1, device_id=device, device_id_type=MESH)
    return lambda: pl.semaphore_wait(barrier, len(devices))


def view(ref, spot, full, core=None, rows=slice(None)):
    whole = slice(None)
    index = [
        whole if "x" in full else spot["x"],
        whole if "z" in full else lax.rem(spot["z"], 2),
        whole if "z" in full else spot["z"] // 2,
        whole if "y" in full else spot["y"],
    ]
    if core is not None:
        index.append(core)
    return ref.at[tuple(index) + (rows,)]


def decode(number, spot, full):
    at = {}
    for axis in "yzx":
        if axis in full:
            parts = []
            for size in reversed(SIZES[axis]):
                parts.append(lax.rem(number, size))
                number = number // size
            at[axis] = tuple(reversed(parts))
    fixed = {"x": (spot["x"],), "z": (lax.rem(spot["z"], 2), spot["z"] // 2), "y": (spot["y"],)}
    index, inner = (), ()
    for axis in "xzy":
        index += at.get(axis, fixed[axis])
        inner += at.get(axis, ())
    return index, inner


def bundle_shape(full):
    shape = ()
    for axis in "xzy":
        shape += SIZES[axis] if axis in full else ()
    return shape


def remote(src, dst, send, recv, device):
    copy = pltpu.make_async_remote_copy(
        src, dst, send, recv, device_id=device, device_id_type=MESH
    )
    copy.start()
    return copy


def take(ref, semaphore):
    pltpu.make_async_copy(ref, ref, semaphore).wait()


class Gather:
    sends, recvs = 5, 8

    def __init__(self, me, order, block, out, send, recv, local):
        self.me, self.order, self.block, self.out = me, order, block, out
        self.send, self.recv, self.local = send, recv, local
        self.core = me["c"]
        self.half = out.shape[-2] // 2
        self.plane = "".join(order[:2])

    def piece(self, spot, full, rows=slice(None)):
        return view(self.out, spot, full, self.core, rows)

    def spread(self, spot, full, axis, by, send, recv, rows=slice(None)):
        piece = self.piece(spot, full, rows)
        target = device_at(shifted(self.me, axis, by))
        remote(piece, piece, self.send.at[send], self.recv.at[recv], target)

    def share(self, spot):
        piece = self.piece(spot, self.plane)
        remote(piece, piece, self.send.at[4], self.recv.at[7], device_at(sibling(self.me)))

    def own(self):
        return pltpu.make_async_copy(
            self.block, view(self.out, self.me, "", self.core), self.local
        )

    def first(self):
        me, axis = self.me, self.order[0]
        self.own().start()
        for by in STEPS:
            target = device_at(shifted(me, axis, by))
            remote(self.block, self.piece(me, ""), self.send.at[0], self.recv.at[0], target)

    def second(self):
        self.own().wait()
        take(self.out.at[:3, 0, 0, 0, 0], self.recv.at[0])
        for by in STEPS:
            self.spread(self.me, self.order[0], self.order[1], by, 1, 1)

    def rows(self, way):
        return pl.ds(way * self.half, self.half)

    def third(self):
        take(self.out.at[:3, 0, 0, :, 0], self.recv.at[1])
        axis = self.order[2]
        for number, (by, way) in enumerate(((1, 0), (-1, 1), (1, 1), (-1, 0))):
            self.spread(self.me, self.plane, axis, by, 2, 2 + number, self.rows(way))
        self.share(self.me)

    def far(self):
        axis = self.order[2]
        for way, by in enumerate((1, -1)):
            take(self.out.at[:, 0, 0, :, 0, : self.half], self.recv.at[2 + way])
            spot = shifted(self.me, axis, -by)
            self.spread(spot, self.plane, axis, by, 3, 6, self.rows(way))

    def rest(self):
        for way, by in enumerate((1, -1)):
            take(self.out.at[:, 0, 0, :, 0, : self.half], self.recv.at[4 + way])
            self.share(shifted(self.me, self.order[2], -by))

    def last(self):
        take(self.out.at[:, 0, 0, :, 0], self.recv.at[6])
        self.share(shifted(self.me, self.order[2], 2))

    def done(self):
        take(self.out.at[:, :, :, :, 0], self.recv.at[7])

    def sent(self):
        out = self.out
        take(out.at[:3, 0, 0, 0, 0], self.send.at[0])
        take(out.at[:3, 0, 0, :, 0], self.send.at[1])
        take(out.at[:, :, 0, :, 0], self.send.at[2])
        take(out.at[:, 0, 0, :, 0], self.send.at[3])
        take(out.at[:, :, :, :, 0], self.send.at[4])


class Reduce:
    sends, recvs = 4, 5

    def __init__(self, me, order, acc, near, far, mid, tail, send, recv):
        self.me, self.order, self.acc = me, order, acc
        self.nears, self.fars, self.mid, self.tail = near, far, mid, tail
        self.send, self.recv = send, recv
        self.half = acc.shape[-2] // 2
        self.full = "".join(order[:2])

    def chunk(self, by):
        return shifted(self.me, self.order[2], by)

    def rows(self, way):
        return pl.ds(way * self.half, self.half)

    def add(self, spot, full, first, rows, terms):
        acc = self.acc

        def one(number, carry):
            index, inner = decode(number, spot, full)
            here = index + (pl.ds(first, rows),)
            total = acc[here]
            if len(terms) > 1:
                total = total.astype(F32)
            for ref, lead in terms:
                rows_there = pl.ds(first, rows) if ref.shape[-2] == acc.shape[-2] else slice(None)
                total += ref[(lead,) + inner + (rows_there,)].astype(total.dtype)
            acc[here] = total.astype(acc.dtype)
            return carry

        lax.fori_loop(0, math.prod(bundle_shape(full)), one, 0)

    def near(self, by, way):
        spot = self.chunk(by)
        box = self.nears.at[0 if by == 1 else 1]
        lead = (slice(None),) * (len(self.nears.shape) - 3)
        remote(
            view(self.acc, spot, self.full, None, self.rows(way)),
            box.at[lead + (self.rows(way),)],
            self.send.at[1],
            self.recv.at[2],
            device_at(spot),
        )

    def stage_far(self):
        spot = self.chunk(2)
        for way, by in enumerate((1, -1)):
            remote(
                view(self.acc, spot, self.full, None, self.rows(way)),
                self.fars.at[way],
                self.send.at[0],
                self.recv.at[way],
                device_at(self.chunk(by)),
            )
        for way, by in enumerate((1, -1)):
            self.near(by, 1 - way)

    def stage_near(self):
        for way, by in enumerate((1, -1)):
            take(self.fars.at[way], self.recv.at[way])
            self.add(self.chunk(by), self.full, way * self.half, self.half, [(self.fars, way)])
            self.near(by, way)

    def spread(self, axis, full, target, send, recv):
        for number, by in enumerate(STEPS):
            spot = shifted(self.me, axis, by)
            remote(
                view(self.acc, spot, full),
                target.at[number],
                self.send.at[send],
                self.recv.at[recv],
                device_at(spot),
            )

    def stage_mid(self):
        take(self.nears, self.recv.at[2])
        self.add(self.me, self.full, 0, 2 * self.half, [(self.nears, 0), (self.nears, 1)])
        self.spread(self.order[1], self.order[0], self.mid, 2, 3)

    def stage_tail(self):
        take(self.mid, self.recv.at[3])
        self.add(self.me, self.order[0], 0, 2 * self.half, [(self.mid, i) for i in range(3)])
        self.spread(self.order[0], "", self.tail, 3, 4)

    def stage_out(self):
        take(self.tail, self.recv.at[4])
        index, _ = decode(0, self.me, "")
        total = self.acc[index].astype(F32)
        for number in range(3):
            total += self.tail[number].astype(F32)
        return total

    def sent(self):
        take(self.fars, self.send.at[0])
        take(self.nears, self.send.at[1])
        take(self.mid, self.send.at[2])
        take(self.tail, self.send.at[3])


def reduce_scratch(order, lanes):
    full = bundle_shape(order[:2])
    return [
        pltpu.VMEM((4, 2, 2, 4, 64, lanes), BF16),
        pltpu.VMEM((2,) + full + (64, lanes), BF16),
        pltpu.VMEM((2,) + full + (32, lanes), BF16),
        pltpu.VMEM((3,) + bundle_shape(order[:1]) + (64, lanes), BF16),
        pltpu.VMEM((3, 64, lanes), BF16),
    ]


class Totals:
    def __init__(self, me, sums, inbox, send, recv):
        self.rounds = [[shifted(me, axis, by) for by in STEPS] for axis in "xyz"] + [[sibling(me)]]
        self.sums, self.inbox, self.send, self.recv = sums, inbox, send, recv

    def heard(self, number):
        return self.inbox.at[number, pl.ds(0, len(self.rounds[number]))]

    def speak(self, number):
        for i, spot in enumerate(self.rounds[number]):
            remote(
                self.sums.at[number],
                self.inbox.at[number, i],
                self.send.at[number],
                self.recv.at[number],
                device_at(spot),
            )

    def hear(self, number):
        take(self.heard(number), self.recv.at[number])
        total = self.sums[number]
        for i in range(len(self.rounds[number])):
            total += self.inbox[number, i]
        self.sums[number + 1] = total

    def pass_on(self, number):
        self.hear(number)
        self.speak(number + 1)

    def sent(self):
        for number in range(4):
            take(self.heard(number), self.send.at[number])


def norm_stats(values):
    average = jnp.mean(values, -1, keepdims=True)
    centered = values - average
    inverse = lax.rsqrt(jnp.mean(centered * centered, -1, keepdims=True) + EPSILON)
    return (centered * inverse, inverse)


def norm_back(upstream, normed, inverse, gain_vector):
    scaled = upstream * gain_vector
    return inverse * (
        scaled
        - jnp.mean(scaled, -1, keepdims=True)
        - normed * jnp.mean(scaled * normed, -1, keepdims=True)
    )


def softmax_columns(key_rows, queries, hidden):
    scores = mm(key_rows, queries, NT) + hidden
    powers = jnp.exp((scores - jnp.max(scores, 0, keepdims=True)) * SCALE)
    return powers * (1.0 / jnp.sum(powers, 0, keepdims=True))


def hidden_rows(seq, slot, tokens):
    row = lax.broadcasted_iota(jnp.int32, (seq, 1), 0)
    return jnp.where(lax.rem(row, slot) < tokens, 0.0, -1e30)


def head_lanes(head):
    lane = lax.broadcasted_iota(jnp.int32, (1, 128), 1)
    return jnp.where(lane // HD == head, 1.0, 0.0).astype(BF16)


def thirds(rows):
    return [rows[:, 128 * i : 128 * i + 128] for i in range(3)]


def attend(rows, hidden):
    queries, key_rows, value_rows = thirds(rows)

    def one_head(head, before):
        mine = head_lanes(head)
        probs = softmax_columns(key_rows, queries * mine, hidden).astype(BF16)
        return before + mm(probs, value_rows * mine, TN)

    return lax.fori_loop(0, 2, one_head, jnp.zeros(queries.shape, F32)).astype(BF16)


def attend_back(rows, grads, hidden):
    queries, key_rows, value_rows = thirds(rows)

    def one_head(head, before):
        mine = head_lanes(head)
        own_grads, own_queries = grads * mine, queries * mine
        probs = softmax_columns(key_rows, own_queries, hidden)
        d_probs = mm(value_rows, own_grads, NT)
        inner = jnp.sum(probs * d_probs, 0, keepdims=True)
        d_scores = (probs * (d_probs - inner)).astype(BF16)
        return (
            before[0] + mm(d_scores, key_rows * mine, TN),
            before[1] + mm(d_scores, own_queries),
            before[2] + mm(probs.astype(BF16), own_grads),
        )

    zero = jnp.zeros(queries.shape, F32)
    d_queries, d_keys, d_values = lax.fori_loop(0, 2, one_head, (zero, zero, zero))
    return [
        (d_queries * SCALE).astype(BF16),
        (d_keys * SCALE).astype(BF16),
        d_values.astype(BF16),
    ]


def fill_rows(box, m, values):
    tokens = values.shape[0]
    box[m, :tokens] = values
    box[m, tokens:] = jnp.zeros((box.shape[1] - tokens, values.shape[1]), box.dtype)


class Swap:
    def __init__(self, me, send, recv):
        self.stays = lax.rem(me["z"], 2) == me["c"]
        self.partner = crossed(me)
        self.send, self.recv = send, recv

    def start(self, box, inbox):
        @pl.when(self.stays)
        def _():
            pltpu.make_async_copy(box, inbox, self.recv).start()

        @pl.when(jnp.logical_not(self.stays))
        def _():
            remote(box, inbox, self.send, self.recv, self.partner)

    def sent(self, box):
        @pl.when(jnp.logical_not(self.stays))
        def _():
            take(box, self.send)


def blocks_of(ref, index):
    value = ref[index // 2, lax.rem(index, 2)]
    return value.reshape(-1, value.shape[-1])


def half_planes(ref, value, kind, count):
    padded = jnp.concatenate(
        [value, jnp.zeros((ref.shape[-1] - count, value.shape[1]), value.dtype)], axis=0
    )
    ref[kind] = padded.T.reshape(ref.shape[1:])


SLABS = 4
SCHEDULE = {
    "start": (("E", "first"),),
    "first": (("A", "first"), ("E", "second"), ("B", "first")),
    "swap": (("E", "third"), ("A", "second"), ("E", "far")),
    "norm": (("A", "third"), ("V", "rest"), ("V", "last"), ("V", "done")),
    "table": (("B", "second"), ("N", "rest"), ("N", "last"), ("A", "far"), ("N", "done")),
    "project": (("A", "rest"), ("B", "third")),
    "image 0": (("A", "last"), ("E", "sent")),
    "image 1": (("B", "far"),),
    "image 2": (("B", "rest"),),
    "reply": (("A", "done"), ("B", "last"), ("A", "sent")),
    "half 0": (),
    "half 1": (("B", "done"),),
}


def forward_kernel(*refs):
    (x_ref, cot_ref, valid_ref, qkv_in, out_in, fc1_in, fc2_in), refs = refs[:7], refs[7:]
    small_in, refs = refs[:8], refs[8:]
    (
        d_middle_out,
        vectors,
        sums_out,
        result_out,
        d_attended_out,
        images_out,
        attended_out,
        turned_out,
        act_out,
        qkv_out,
        x_out,
        x_box,
        x_in,
        cot_box,
        cot_in,
        result_box,
        wq,
        wk,
        wv,
        up_a,
        up_b,
        side_a,
        down_xa,
        down_b,
        side_own,
        small_own,
        small,
        bias,
        hidden_bias,
        low,
        outbox,
        images,
        attended_box,
        attended,
        middle,
        normed_two,
        low_two,
        turned,
        forward_sum,
        back_sum,
        act_box,
        d_outbox,
        hidden_sums,
        local_sem,
        gather_send,
        gather_recv,
        send_sem,
        recv_sem,
        back_send,
        back_recv,
        store_sem,
        sib_send,
        sib_recv,
        ff_local,
        ff_send,
        ff_recv,
        swap_send,
        swap_recv,
    ) = refs
    me = place()
    core = me["c"]
    t = 2 * me["x"] + core
    other = device_at(sibling(me))
    micro, tokens, width = x_ref.shape
    slot = x_in.shape[1]
    count = micro * slot
    met = greet(me)
    heads = [wq, wk, wv]
    made = []

    def gather(order, block, out):
        i = len(made)
        made.append(
            Gather(me, order, block, out, gather_send.at[i], gather_recv.at[i], local_sem.at[i])
        )
        return made[-1]

    narrow = [gather(ORDERS[i], qkv_in.at[i], heads[i]) for i in range(3)]
    vector = gather(ORDERS[0], small_own, small)
    early = [vector] + narrow
    first_half = [
        gather(ORDERS[2], fc1_in.at[:, :256], up_a),
        gather(ORDERS[0], side_own, side_a),
        gather(ORDERS[1], fc2_in.at[:, :128], down_xa),
    ]
    second_half = [
        gather(ORDERS[0], fc1_in.at[:, 256:], up_b),
        gather(ORDERS[2], fc2_in.at[:, 256:], down_b),
    ]
    groups = {
        "V": [vector],
        "N": narrow,
        "E": early,
        "A": first_half,
        "B": second_half,
    }

    def run(point):
        for names, stage in SCHEDULE[point]:
            for name in names:
                for part in groups[name]:
                    getattr(part, stage)()

    stores = []

    def store(src, dst):
        copy = pltpu.make_async_copy(src, dst, store_sem.at[len(stores)])
        copy.start()
        stores.append(copy)

    shared = []

    def share(src, dst):
        slot_of = len(shared)
        copy = pltpu.make_async_remote_copy(
            src,
            dst,
            sib_send.at[slot_of],
            sib_recv.at[slot_of],
            device_id=other,
            device_id_type=MESH,
        )
        copy.start()
        shared.append(copy)

    def turn(kind, value):
        half_planes(turned, value, kind, count)
        store(turned.at[kind, :, core], turned_out.at[kind, 0])
        share(turned.at[kind, :, 1 - core], turned_out.at[kind, 1])

    for m in range(micro):
        fill_rows(x_box, m, x_ref[m])
    side_own[:, :128] = out_in[...]
    side_own[:, 128:] = fc2_in[:, 128:256]
    small_own[...] = jnp.zeros_like(small_own)
    for v in range(6):
        small_own[0:1, 8 * v : 8 * v + 8] = small_in[v][...]
    for i in range(2):
        for j in range(2):
            at = 48 + 8 * i + 4 * j
            small_own[0:1, at : at + 4] = small_in[6][i, j : j + 1]
    for i in range(4):
        small_own[0:1, 64 + 8 * i : 72 + 8 * i] = small_in[7][i : i + 1]
    met()
    run("start")
    swaps = [Swap(me, swap_send.at[i], swap_recv.at[i]) for i in range(3)]
    swaps[0].start(x_box, x_in)
    run("first")
    for m in range(micro):
        fill_rows(cot_box, m, (cot_ref[m].astype(F32) * valid_ref[0, m].astype(F32)).astype(BF16))
    run("swap")
    take(x_in, swap_recv.at[0])
    store(x_in, x_out)

    def rows_of(ref):
        return ref[...].reshape(count, width).astype(F32)

    normed, _ = norm_stats(rows_of(x_in))
    run("norm")
    table = jnp.sum(small[...].reshape(128, 32, 128).astype(F32), 1).astype(BF16)
    lane = lax.broadcasted_iota(jnp.int32, (128, 1024), 0)
    column = lax.broadcasted_iota(jnp.int32, (128, 1024), 1)
    owner = jnp.where(lax.rem(lane, 16) * 8 + lane // 16 == column // 8, 1.0, 0.0)
    for v in range(6):
        pick = jnp.where(lane == v * 8 + lax.rem(column, 8), 1.0, 0.0).astype(BF16)
        vectors[v : v + 1, :] = jnp.sum(mm(table, pick) * owner, 0, keepdims=True)
    vectors[6:8, :] = jnp.zeros((2, 1024), F32)

    def spread_bias(lanes, first, major, minor):
        lane = lax.broadcasted_iota(jnp.int32, (128, lanes), 0)
        column = lax.broadcasted_iota(jnp.int32, (128, lanes), 1)
        pick = lane == first + (column // 64) * major + lax.rem(column, 4) * minor
        owner = lax.rem(lane, 16) == lax.rem(column, 64) // 4
        values = mm(table, jnp.where(pick, 1.0, 0.0).astype(BF16))
        return jnp.sum(jnp.where(owner, values, 0.0).reshape(8, 16, lanes), 1)

    hidden_value = spread_bias(512, 64, 1, 8)
    query_bias, value_bias = spread_bias(128, 48, 4, 1), spread_bias(128, 56, 4, 1)
    for i in range(GROUP):
        hidden_bias[i] = hidden_value[i : i + 1]
        bias[i, :, 0:128] = query_bias[i : i + 1]
        bias[i, :, 128:256] = jnp.zeros((1, 128), F32)
        bias[i, :, 256:384] = value_bias[i : i + 1]
    low[...] = (normed * vectors[0:1, :] + vectors[1:2, :]).astype(BF16)
    run("table")

    def letter(k, m):
        target = lax.rem(t + k + 1, GROUP)
        return pltpu.make_async_remote_copy(
            outbox.at[target, m],
            images.at[t, m],
            send_sem,
            recv_sem.at[m],
            device_id=member(me, target),
            device_id_type=MESH,
        )

    def project(k, carry):
        target = lax.rem(t + k + 1, GROUP)
        weights = jnp.concatenate([blocks_of(w, target) for w in heads], axis=1)
        result = (mm(low[...], weights) + bias[target]).astype(BF16)
        outbox[target] = result.reshape(outbox.shape[1:])

        @pl.when(k < GROUP - 1)
        def _():
            letter(k, 0).start()

        return carry

    lax.fori_loop(0, GROUP, project, 0)
    for m in range(1, MICRO):
        for k in range(GROUP - 1):
            letter(k, m).start()
    own = pltpu.make_async_copy(outbox.at[t], images.at[t], local_sem.at[len(made)])
    own.start()
    for i in range(3):
        store(heads[i], qkv_out.at[i])
    swaps[1].start(cot_box, cot_in)
    run("project")
    turn(0, low[...])
    own.wait()
    hidden = hidden_rows(GROUP * slot, slot, tokens)

    def reply(m, k):
        target = lax.rem(t + k + 1, GROUP)
        return pltpu.make_async_remote_copy(
            attended_box.at[m, target],
            attended.at[t, m],
            back_send,
            back_recv,
            device_id=member(me, target),
            device_id_type=MESH,
        )

    for m in range(MICRO):
        take(images.at[: GROUP - 1, m], recv_sem.at[m])
        result = attend(images[:, m].reshape(GROUP * slot, 384), hidden)
        attended_box[m] = result.reshape(GROUP, slot, 128)
        for k in range(GROUP - 1):
            reply(m, k).start()
        attended[t, m] = attended_box[m, t]
        run(("image 0", "image 1", "image 2")[m])
        if m == 1:
            take(cot_in, swap_recv.at[1])
            upstream_low = cot_in[...].reshape(count, width)
            sums_out[3:4, :] = jnp.sum(upstream_low.astype(F32), 0, keepdims=True)
            turn(1, upstream_low)
    store(images, images_out)
    take(attended.at[: GROUP - 1], back_recv)
    store(attended, attended_out.at[0])
    share(attended, attended_out.at[1])
    run("reply")
    middle[...] = rows_of(x_in) + vectors[2:3, :]

    def out_weights(pair):
        both = [blocks_of(side_a, 2 * pair + i)[:, :128] for i in range(2)]
        return jnp.concatenate(both, axis=1)

    def out_project(pair, carry):
        both = [attended[2 * pair + i].reshape(count, 128) for i in range(2)]
        middle[...] += mm(jnp.concatenate(both, axis=1), out_weights(pair), NT)
        return carry

    lax.fori_loop(0, GROUP // 2, out_project, 0)
    normed, inverse = norm_stats(middle[...])
    normed_two[...] = normed
    low_two[...] = (normed * vectors[3:4, :] + vectors[4:5, :]).astype(BF16)
    turn(2, low_two[...])
    forward_sum[...] = jnp.zeros_like(forward_sum)
    back_sum[...] = jnp.zeros_like(back_sum)

    def ship(step, h):
        at = (pl.ds(SLABS * step, SLABS), slice(None), pl.ds(2 * count * h, 2 * count))
        piece = act_box.at[at]
        pltpu.make_async_copy(piece, act_out.at[(0,) + at], ff_local).start()
        remote(piece, act_out.at[(1,) + at], ff_send, ff_recv, other)

    for h in range(2):
        run(("half 0", "half 1")[h])

        def feed_forward(step, carry):
            slabs = [SLABS * step + n for n in range(SLABS)]
            up_weight = jnp.concatenate([blocks_of((up_a, up_b)[h], i) for i in slabs], axis=1)
            down = []
            for i in slabs:
                if h == 0:
                    down += [blocks_of(down_xa, i), blocks_of(side_a, i)[:, 128:]]
                else:
                    down.append(blocks_of(down_b, i))
            down_weight = jnp.concatenate(down, axis=1)
            biases = [hidden_bias[i, :, 256 * h : 256 * h + 256] for i in slabs]
            up_proj = mm(low_two[...], up_weight) + jnp.concatenate(biases, axis=1)
            gate = jax.nn.sigmoid(1.702 * up_proj)
            activated = (up_proj * gate).astype(BF16)
            d_act = mm(cot_in[...].reshape(count, width), down_weight)
            d_up = (d_act * (gate + 1.702 * up_proj * gate * (1.0 - gate))).astype(BF16)
            column_sums = jnp.sum(d_up.astype(F32), 0, keepdims=True)
            for n, i in enumerate(slabs):
                for j in range(2):
                    at = pl.ds(count * (2 * h + j), count)
                    lanes = slice(256 * n + 128 * j, 256 * n + 128 * (j + 1))
                    act_box[i, 0, at] = activated[:, lanes]
                    act_box[i, 1, at] = d_up[:, lanes]
                hidden_sums[i, :, 256 * h : 256 * h + 256] = column_sums[:, 256 * n : 256 * n + 256]
            ship(step, h)
            forward_sum[...] += mm(activated, down_weight, NT)
            back_sum[...] += mm(d_up, up_weight, NT)
            return carry

        lax.fori_loop(0, GROUP // SLABS, feed_forward, 0)
    output = (middle[...] + forward_sum[...] + vectors[5:6, :]).astype(BF16)
    result_box[...] = output.reshape(result_box.shape)
    swaps[2].start(result_box, result_out)
    d_norm = back_sum[...]
    normed = normed_two[...]
    d_middle = rows_of(cot_in) + norm_back(
        d_norm, normed, inverse, vectors[3:4, :]
    )
    d_middle_out[...] = d_middle
    low[...] = d_middle.astype(BF16)

    def project_back(pair, carry):
        both = mm(low[...], out_weights(pair)).astype(BF16)
        for i in range(2):
            d_outbox[2 * pair + i] = both[:, 128 * i : 128 * i + 128].reshape(d_outbox.shape[1:])
        return carry

    lax.fori_loop(0, GROUP // 2, project_back, 0)
    store(d_outbox, d_attended_out)
    turn(3, low[...])
    sums_out[0:1, :] = jnp.sum(d_middle, 0, keepdims=True)
    sums_out[1:2, :] = jnp.sum(d_norm * normed, 0, keepdims=True)
    sums_out[2:3, :] = jnp.sum(d_norm, 0, keepdims=True)
    for i in range(GROUP):
        at = 4 + i // 2
        sums_out[at : at + 1, 512 * (i % 2) : 512 * (i % 2) + 512] = hidden_sums[i]
    for swap, box in zip(swaps, (x_box, cot_box, result_box)):
        swap.sent(box)
    take(result_out, swap_recv.at[2])
    for copy in shared:
        copy.wait()
    take(act_box, ff_local)
    take(act_box, ff_send)
    take(act_box, ff_recv)
    for part in second_half:
        part.sent()
    take(outbox.at[: GROUP - 1], send_sem)
    take(attended_box.at[:, : GROUP - 1], back_send)
    for copy in stores:
        copy.wait()


ANY = pl.BlockSpec(memory_space=pl.ANY)
VMEM = pl.BlockSpec(memory_space=pltpu.VMEM)
SMEM = pl.BlockSpec(memory_space=pltpu.SMEM)


def forward(x, cotangent, valid, qkv_block, out_block, fc1_block, fc2_block, small, slot):
    width = x.shape[-1]
    count = MICRO * slot
    rows = (MICRO, slot, width)
    images = (GROUP, MICRO, slot, 384)
    attended = (GROUP, MICRO, slot, 128)
    acts = (2, GROUP, 2, 4 * count, 128)
    return pl.pallas_call(
        forward_kernel,
        out_shape=[
            jax.ShapeDtypeStruct((count, width), F32),
            jax.ShapeDtypeStruct((8, width), F32),
            jax.ShapeDtypeStruct((8, width), F32),
            jax.ShapeDtypeStruct(rows, BF16),
            jax.ShapeDtypeStruct(attended, BF16),
            jax.ShapeDtypeStruct(images, BF16),
            jax.ShapeDtypeStruct((2,) + attended, BF16),
            jax.ShapeDtypeStruct((4, 2, 8, 64, 256), BF16),
            jax.ShapeDtypeStruct(acts, BF16),
            jax.ShapeDtypeStruct((3,) + LEAD + (64, 128), BF16),
            jax.ShapeDtypeStruct(rows, BF16),
        ],
        in_specs=[VMEM, VMEM, SMEM, ANY, VMEM, ANY, VMEM] + [VMEM] * 8,
        out_specs=[VMEM] * 3 + [ANY] * 8,
        scratch_shapes=[
            pltpu.VMEM(rows, BF16),
            pltpu.VMEM(rows, BF16),
            pltpu.VMEM(rows, BF16),
            pltpu.VMEM(rows, BF16),
            pltpu.VMEM(rows, BF16),
            pltpu.VMEM(LEAD + (64, 128), BF16),
            pltpu.VMEM(LEAD + (64, 128), BF16),
            pltpu.VMEM(LEAD + (64, 128), BF16),
            pltpu.VMEM(LEAD + (64, 256), BF16),
            pltpu.VMEM(LEAD + (64, 256), BF16),
            pltpu.VMEM(LEAD + (64, 256), BF16),
            pltpu.VMEM(LEAD + (64, 128), BF16),
            pltpu.VMEM(LEAD + (64, 256), BF16),
            pltpu.VMEM((64, 256), BF16),
            pltpu.VMEM((32, 128), BF16),
            pltpu.VMEM(LEAD + (32, 128), BF16),
            pltpu.VMEM((GROUP, 1, 384), F32),
            pltpu.VMEM((GROUP, 1, 512), F32),
            pltpu.VMEM((count, width), BF16),
            pltpu.VMEM(images, BF16),
            pltpu.VMEM(images, BF16),
            pltpu.VMEM((MICRO, GROUP, slot, 128), BF16),
            pltpu.VMEM(attended, BF16),
            pltpu.VMEM((count, width), F32),
            pltpu.VMEM((count, width), F32),
            pltpu.VMEM((count, width), BF16),
            pltpu.VMEM((4, 8, 2, 64, 256), BF16),
            pltpu.VMEM((count, width), F32),
            pltpu.VMEM((count, width), F32),
            pltpu.VMEM(acts[1:], BF16),
            pltpu.VMEM(attended, BF16),
            pltpu.VMEM((GROUP, 1, 512), F32),
            pltpu.SemaphoreType.DMA((12,)),
            pltpu.SemaphoreType.DMA((10, Gather.sends)),
            pltpu.SemaphoreType.DMA((10, Gather.recvs)),
            pltpu.SemaphoreType.DMA,
            pltpu.SemaphoreType.DMA((MICRO,)),
            pltpu.SemaphoreType.DMA,
            pltpu.SemaphoreType.DMA,
            pltpu.SemaphoreType.DMA((11,)),
            pltpu.SemaphoreType.DMA((5,)),
            pltpu.SemaphoreType.DMA((5,)),
            pltpu.SemaphoreType.DMA,
            pltpu.SemaphoreType.DMA,
            pltpu.SemaphoreType.DMA,
            pltpu.SemaphoreType.DMA((3,)),
            pltpu.SemaphoreType.DMA((3,)),
        ],
        compiler_params=pltpu.CompilerParams(
            collective_id=0, has_side_effects=True, vmem_limit_bytes=VMEM_LIMIT
        ),
        name="forward",
    )(x, cotangent, valid, qkv_block, out_block, fc1_block, fc2_block, *small)


BACK_SCHEDULE = {
    "early": True,
    "image 0": (("down", 0), (0, -1), ("U", "stage_near")),
    "image 1": (("V", "stage_near"), (0, 0)),
    "image 2": (("D", "stage_near"), (0, 1)),
    "norm": (("U", "stage_mid"), ("V", "stage_mid"), ("D", "stage_mid"), (0, 2)),
    "late": ((0, 3), ("L", "stage_near")),
    "rows": (
        (1, 0),
        ("L", "stage_mid"),
        (1, 1),
        ("U", "stage_tail"),
        ("V", "stage_tail"),
        ("D", "stage_tail"),
        ("L", "stage_tail"),
        (1, 2),
    ),
    "wide": (("U", "sent"), ("V", "sent"), ("D", "sent")),
    "end": ((1, 3),),
}


def backward_kernel(*refs):
    (
        d_attended_in,
        images_in,
        attended_in,
        turned_in,
        act_in,
        qkv_in,
        x_in,
        d_middle_ref,
        vectors_ref,
        sums_ref,
        qkv_grad,
        out_grad,
        fc1_grad,
        fc2_grad,
        totals_out,
        input_grad_out,
        rows,
        box,
        pool,
        turned,
        attended,
        images,
        d_attended,
        outbox,
        d_images,
        d_norm,
        sums,
        sums_in,
        *rest,
    ) = refs
    scratch, sems = rest[: 5 * len(REDUCED)], rest[5 * len(REDUCED) :]
    (
        load_sem,
        reduce_send,
        reduce_recv,
        send_sem,
        recv_sem,
        back_send,
        back_recv,
        sib_send,
        sib_recv,
        sum_send,
        sum_recv,
        swap_send,
        swap_recv,
    ) = sems
    me = place()
    t = 2 * me["x"] + me["c"]
    other = device_at(sibling(me))
    met = greet(me)
    slot = rows.shape[1]
    count = MICRO * slot
    parts = [
        Reduce(
            me,
            REDUCED[i][0],
            *scratch[5 * i : 5 * i + 5],
            reduce_send.at[i],
            reduce_recv.at[i],
        )
        for i in range(len(REDUCED))
    ]
    late = parts[-3:]
    wide = parts[:-3]
    totals = [
        Totals(me, sums.at[i], sums_in.at[i], sum_send.at[i], sum_recv.at[i]) for i in range(2)
    ]
    loads = {}

    def load(name, src, dst):
        loads[name] = pltpu.make_async_copy(src, dst, load_sem.at[len(loads)])
        loads[name].start()

    kept = pl.ds(0, 4 * count)
    load("turned", turned_in, turned)
    for i in range(2):
        load(("dup", i), act_in.at[i, :, 1], pool.at[2 + i, :, kept])
    load("images", images_in, images)
    load("own", d_attended_in.at[t], d_attended.at[t])
    for i in range(2):
        load(("act", i), act_in.at[i, :, 0], pool.at[i, :, kept])
    load("attended", attended_in, attended)
    load("rows", x_in, rows)
    sums[0, 0] = sums_ref[...]

    def both_cores(kind, values):
        total = 0.0
        for i in range(2):
            left = turned[kind, i].reshape(512, 256)[:, :count]
            total += mm(left, values[i])
        return total.astype(BF16)

    def pooled(first, index, lanes):
        return [
            jnp.concatenate(
                [pool[first + i, index, count * j : count * (j + 1)] for j in lanes], axis=1
            )
            for i in range(2)
        ]

    def spot_of(index):
        return (index // 2, lax.rem(index, 2))

    def fill(part, index, lanes, value):
        acc = part.acc
        acc[spot_of(index) + (slice(None),) * 3 + (lanes,)] = value.reshape(
            acc.shape[2:-1] + (value.shape[-1],)
        )

    def grads_up(half):
        def one(index, carry):
            value = both_cores(2, pooled(2, index, (2 * half, 2 * half + 1)))
            fill(wide[half], index, slice(0, 256), value)
            return carry

        return one

    def grads_down(index, carry):
        value = both_cores(1, pooled(0, index, range(4)))
        fill(wide[2], index, slice(0, 128), value[:, :128])
        fill(wide[3], index, slice(0, 256), value[:, 128:384])
        fill(wide[4], index, slice(0, 128), value[:, 384:])
        value = both_cores(3, [attended[i, index].reshape(count, 128) for i in range(2)])
        fill(wide[4], index, slice(128, 256), value)
        return carry

    loads["turned"].wait()
    for i in range(2):
        loads["dup", i].wait()
    met()
    for m in range(MICRO):
        for k in range(GROUP - 1):
            target = lax.rem(t + k + 1, GROUP)
            remote(
                d_attended_in.at[target, m],
                d_attended.at[t, m],
                send_sem,
                recv_sem.at[m],
                member(me, target),
            )
    lax.fori_loop(0, GROUP, grads_up(0), 0)
    wide[0].stage_far()
    if BACK_SCHEDULE["early"]:
        lax.fori_loop(0, GROUP, grads_up(1), 0)
        wide[1].stage_far()
    loads["images"].wait()
    loads["own"].wait()
    hidden = hidden_rows(GROUP * slot, slot, TOKENS)

    def reply(m, k):
        target = lax.rem(t + k + 1, GROUP)
        return pltpu.make_async_remote_copy(
            outbox.at[m, target],
            d_images.at[0, t, m],
            back_send,
            back_recv.at[k],
            device_id=member(me, target),
            device_id_type=MESH,
        )

    def down():
        for i in range(2):
            loads["act", i].wait()
        loads["attended"].wait()
        lax.fori_loop(0, GROUP, grads_down, 0)
        for part in wide[2:]:
            part.stage_far()
        for i in range(3):
            load(("weight", i), qkv_in.at[i], pool.at[i])

    groups = {"U": wide[:1], "V": wide[1:2], "D": wide[2:], "L": late}

    def run(point):
        for name, stage in BACK_SCHEDULE[point]:
            if name == "down":
                down()
            elif name == "up":
                lax.fori_loop(0, GROUP, grads_up(1), 0)
                wide[1].stage_far()
            elif name in groups:
                for part in groups[name]:
                    getattr(part, stage)()
            elif stage < 0:
                totals[name].speak(0)
            elif stage < 3:
                totals[name].pass_on(stage)
            else:
                totals[name].hear(3)

    for m in range(MICRO):
        take(d_attended.at[: GROUP - 1, m], recv_sem.at[m])
        results = attend_back(
            images[:, m].reshape(GROUP * slot, 384),
            d_attended[:, m].reshape(GROUP * slot, 128),
            hidden,
        )
        for i in range(3):
            outbox[m, :, :, 128 * i : 128 * i + 128] = results[i].reshape(GROUP, slot, 128)
        for k in range(GROUP - 1):
            reply(m, k).start()
        d_images[0, t, m] = outbox[m, t]
        run(("image 0", "image 1", "image 2")[m])
    loads["rows"].wait()
    normed, inverse = norm_stats(rows[...].reshape(count, rows.shape[-1]).astype(F32))
    run("norm")

    def share(k):
        source = lax.rem(t + k + 1, GROUP)
        remote(d_images.at[0, source], d_images.at[1, source], sib_send, sib_recv, other)

    share(GROUP - 1)
    for k in reversed(range(GROUP - 1)):
        take(d_images.at[0, 0], back_recv.at[GROUP - 2 - k])
        share(k)
    for i in range(3):
        loads["weight", i].wait()
    d_norm[...] = jnp.zeros_like(d_norm)

    def project_back(index, carry):
        weights = jnp.concatenate([pool[i, index] for i in range(3)], axis=1)
        d_norm[...] += mm(d_images[0, index].reshape(count, 384), weights, NT)
        return carry

    lax.fori_loop(0, GROUP, project_back, 0)
    take(d_images.at[1], sib_recv)

    def grads_late(index, carry):
        value = both_cores(0, [d_images[i, index].reshape(count, 384) for i in range(2)])
        for i, part in enumerate(late):
            fill(part, index, slice(None), value[:, 128 * i : 128 * i + 128])
        return carry

    lax.fori_loop(0, GROUP, grads_late, 0)
    for part in late:
        part.stage_far()
    gradient = d_norm[...]
    sums[1, 0, 0:1, :] = jnp.sum(gradient * normed, 0, keepdims=True)
    sums[1, 0, 1:2, :] = jnp.sum(gradient, 0, keepdims=True)
    for index in range(GROUP):
        grads = jnp.sum(d_images[0, index].reshape(count, 384).astype(F32), 0, keepdims=True)
        sums[1, 0, 2:3, 128 * index : 128 * index + 128] = grads[:, :128]
        sums[1, 0, 3:4, 128 * index : 128 * index + 128] = grads[:, 256:]
    sums[1, 0, 4:8, :] = jnp.zeros((4, sums.shape[-1]), F32)
    totals[1].speak(0)
    run("late")
    result = d_middle_ref[...] + norm_back(gradient, normed, inverse, vectors_ref[0:1, :])
    box[...] = result.astype(BF16).reshape(box.shape)
    swap = Swap(me, swap_send, swap_recv)
    swap.start(box, input_grad_out)
    run("rows")
    fc1_grad[:, :256] = wide[0].stage_out()
    fc1_grad[:, 256:] = wide[1].stage_out()
    fc2_grad[:, :128] = wide[2].stage_out()
    fc2_grad[:, 128:384] = wide[3].stage_out()
    value = wide[4].stage_out()
    fc2_grad[:, 384:] = value[:, :128]
    out_grad[...] = value[:, 128:]
    run("wide")
    for i in range(3):
        qkv_grad[i] = late[i].stage_out()
    run("end")
    totals_out[0:8, :] = sums[0, 4]
    totals_out[8:16, :] = sums[1, 4]
    for part in late:
        part.sent()
    for total in totals:
        total.sent()
    take(d_images.at[1], sib_send)
    take(outbox.at[:, : GROUP - 1], back_send)
    take(d_attended.at[: GROUP - 1], send_sem)
    swap.sent(box)
    take(input_grad_out, swap_recv)


REDUCED = (
    (ORDERS[2], 256),
    (ORDERS[0], 256),
    (ORDERS[1], 128),
    (ORDERS[2], 256),
    (ORDERS[0], 256),
    (ORDERS[0], 128),
    (ORDERS[1], 128),
    (ORDERS[2], 128),
)


def backward(d_attended, images, attended, turned, act, qkv, x, d_middle, vectors, sums):
    width = x.shape[-1]
    slot = x.shape[1]
    count = MICRO * slot
    scratch = []
    for order, lanes in REDUCED:
        scratch += reduce_scratch(order, lanes)
    return pl.pallas_call(
        backward_kernel,
        out_shape=[
            jax.ShapeDtypeStruct((3, 64, 128), F32),
            jax.ShapeDtypeStruct((64, 128), F32),
            jax.ShapeDtypeStruct((64, 512), F32),
            jax.ShapeDtypeStruct((64, 512), F32),
            jax.ShapeDtypeStruct((16, width), F32),
            jax.ShapeDtypeStruct(x.shape, BF16),
        ],
        in_specs=[ANY] * 7 + [VMEM] * 3,
        out_specs=[VMEM] * 5 + [ANY],
        scratch_shapes=[
            pltpu.VMEM(x.shape, BF16),
            pltpu.VMEM(x.shape, BF16),
            pltpu.VMEM((4, GROUP, width, 128), BF16),
            pltpu.VMEM(turned.shape, BF16),
            pltpu.VMEM(attended.shape, BF16),
            pltpu.VMEM(images.shape, BF16),
            pltpu.VMEM(d_attended.shape, BF16),
            pltpu.VMEM((MICRO, GROUP, slot, 384), BF16),
            pltpu.VMEM((2,) + images.shape, BF16),
            pltpu.VMEM((count, width), F32),
            pltpu.VMEM((2, 5, 8, width), F32),
            pltpu.VMEM((2, 4, 3, 8, width), F32),
        ]
        + scratch
        + [
            pltpu.SemaphoreType.DMA((12,)),
            pltpu.SemaphoreType.DMA((len(REDUCED), Reduce.sends)),
            pltpu.SemaphoreType.DMA((len(REDUCED), Reduce.recvs)),
            pltpu.SemaphoreType.DMA,
            pltpu.SemaphoreType.DMA((MICRO,)),
            pltpu.SemaphoreType.DMA,
            pltpu.SemaphoreType.DMA((GROUP,)),
            pltpu.SemaphoreType.DMA,
            pltpu.SemaphoreType.DMA,
            pltpu.SemaphoreType.DMA((2, 4)),
            pltpu.SemaphoreType.DMA((2, 4)),
            pltpu.SemaphoreType.DMA,
            pltpu.SemaphoreType.DMA,
        ],
        compiler_params=pltpu.CompilerParams(
            collective_id=1, has_side_effects=True, vmem_limit_bytes=VMEM_LIMIT
        ),
        name="backward",
    )(d_attended, images, attended, turned, act, qkv, x, d_middle, vectors, sums)


def finish_kernel(
    result,
    input_grad,
    qkv_grad,
    out_grad,
    fc1_grad,
    fc2_grad,
    totals,
    result_out,
    input_grad_out,
    qkv_out,
    out_out,
    fc1_out,
    fc2_out,
    *rest,
):
    vectors_out, (pair_out, hidden_out) = rest[:6], rest[6:]
    f, t = lax.axis_index("fsdp"), lax.axis_index("tp")
    tokens = result_out.shape[1]
    result_out[...] = result[:, :tokens]
    input_grad_out[...] = input_grad[:, :tokens]
    qkv_out[...] = qkv_grad[...]
    out_out[...] = out_grad[...]
    fc1_out[...] = fc1_grad[...]
    fc2_out[...] = fc2_grad[...]
    width = totals.shape[-1]
    own = pltpu.roll(totals[...], lax.rem(width - (f * 8 + t) * 8, width), 1)
    for number, row in enumerate((8, 9, 0, 1, 2, 3)):
        vectors_out[number][...] = own[row : row + 1, :8]
    own = pltpu.roll(totals[...], lax.rem(width - t * 128 - f * 4, width), 1)
    for kind in range(2):
        for head in range(2):
            pair_out[kind, head : head + 1, :] = own[
                10 + kind : 11 + kind, HD * head : HD * head + 4
            ]
    row = totals[4:8, :]
    mine = lax.broadcasted_iota(jnp.int32, row.shape, 0) == t // 2
    row = jnp.sum(jnp.where(mine, row, 0.0), 0, keepdims=True)
    row = pltpu.roll(
        jnp.broadcast_to(row, (8, width)), lax.rem(width - 512 * lax.rem(t, 2) - f * 4, width), 1
    )
    turned = jnp.concatenate([row[0:1, 64 * j : 64 * j + 128] for j in range(8)], axis=0)
    hidden_out[...] = turned.T[:4]


def finish(result, input_grad, qkv_grad, out_grad, fc1_grad, fc2_grad, totals):
    arrays = (result, input_grad, qkv_grad, out_grad, fc1_grad, fc2_grad)
    rows = jax.ShapeDtypeStruct((MICRO, TOKENS, result.shape[-1]), BF16)
    shapes = [rows, rows] + [jax.ShapeDtypeStruct(a.shape, a.dtype) for a in arrays[2:]]
    shapes += [jax.ShapeDtypeStruct((1, 8), F32)] * 6
    shapes += [
        jax.ShapeDtypeStruct((2, 2, 4), F32),
        jax.ShapeDtypeStruct((4, 8), F32),
    ]
    return pl.pallas_call(
        finish_kernel,
        out_shape=shapes,
        in_specs=[VMEM] * 7,
        out_specs=[VMEM] * 14,
        compiler_params=pltpu.CompilerParams(vmem_limit_bytes=VMEM_LIMIT),
        name="finish",
    )(*arrays, totals)


def per_device(
    inputs,
    cotangent,
    valid_slots,
    ln1_gain,
    ln1_bias,
    qkv_weight,
    qv_bias,
    out_weight,
    out_bias,
    ln2_gain,
    ln2_bias,
    fc1_weight,
    fc1_bias,
    fc2_weight,
    fc2_bias,
):
    micro, _, tokens, width = inputs.shape
    slot = -(-tokens // 16) * 16
    x = inputs.reshape(micro, tokens, width)
    small = [ln1_gain, ln1_bias, out_bias, ln2_gain, ln2_bias, fc2_bias]
    small = [v.reshape(1, 8) for v in small] + [qv_bias, fc1_bias.T]
    (
        d_middle,
        vectors,
        sums,
        result,
        d_attended,
        images,
        attended,
        turned,
        act,
        qkv,
        x_rows,
    ) = forward(
        x,
        cotangent.reshape(x.shape),
        valid_slots.T,
        qkv_weight,
        out_weight.T,
        fc1_weight,
        fc2_weight.T,
        small,
        slot,
    )
    qkv_grad, out_grad, fc1_grad, fc2_grad, total, input_grad = backward(
        d_attended,
        images,
        attended,
        turned,
        act,
        qkv.reshape(3, GROUP, width, 128),
        x_rows,
        d_middle,
        vectors,
        sums,
    )
    result, input_grad, qkv_grad, out_grad, fc1_grad, fc2_grad, *own, pair, hidden_grad = finish(
        result, input_grad, qkv_grad, out_grad, fc1_grad, fc2_grad, total
    )
    own = [own[i].reshape(8) for i in range(6)]
    return (
        result.reshape(inputs.shape),
        input_grad.reshape(inputs.shape),
        own[0],
        own[1],
        qkv_grad,
        pair,
        out_grad.T,
        own[2],
        own[3],
        own[4],
        fc1_grad,
        hidden_grad.T,
        fc2_grad.T,
        own[5],
    )


def solution(mesh):
    in_specs = (
        P(None, "fsdp", "tp", None),
        P(None, "fsdp", "tp", None),
        P(None, "fsdp"),
        P(("fsdp", "tp")),
        P(("fsdp", "tp")),
        P(None, "fsdp", "tp"),
        P(None, "tp", "fsdp"),
        P("tp", "fsdp"),
        P(("fsdp", "tp")),
        P(("fsdp", "tp")),
        P(("fsdp", "tp")),
        P("fsdp", "tp"),
        P("tp", "fsdp"),
        P("tp", "fsdp"),
        P(("fsdp", "tp")),
    )
    out_specs = (
        P(None, "fsdp", "tp", None),
        P(None, "fsdp", "tp", None),
        P(("fsdp", "tp")),
        P(("fsdp", "tp")),
        P(None, "fsdp", "tp"),
        P(None, "tp", "fsdp"),
        P("tp", "fsdp"),
        P(("fsdp", "tp")),
        P(("fsdp", "tp")),
        P(("fsdp", "tp")),
        P("fsdp", "tp"),
        P("tp", "fsdp"),
        P("tp", "fsdp"),
        P(("fsdp", "tp")),
    )
    return jax.shard_map(
        per_device, mesh=mesh, in_specs=in_specs, out_specs=out_specs, check_vma=False
    )
```

```python
import functools
import math

import jax
import jax.numpy as jnp
from jax import lax
from jax.experimental import pallas as pl
from jax.experimental.pallas import tpu as pltpu
from jax.sharding import PartitionSpec as P

MESH = pl.DeviceIdType.MESH
HD = 64
SCALE = 1.0 / math.sqrt(HD)
EPSILON = 1e-05
BF16 = jnp.bfloat16
F32 = jnp.float32
VMEM_LIMIT = 62 * 2**20
MICRO, GROUP, TOKENS = 3, 8, 72
ORDERS = (("x", "y", "z"), ("y", "z", "x"), ("z", "x", "y"))
SIZES = {"x": (4,), "z": (2, 2), "y": (4,)}
LEAD = (4, 2, 2, 4, 2)
STEPS = (1, -1, 2)
NN = (((1,), (0,)), ((), ()))
NT = (((1,), (1,)), ((), ()))
TN = (((0,), (0,)), ((), ()))


def mm(a, b, dims=NN):
    return lax.dot_general(a, b, dims, preferred_element_type=F32)


def place():
    f, t = lax.axis_index("fsdp"), lax.axis_index("tp")
    return {
        "x": t // 2,
        "y": lax.rem(f // 2, 4),
        "z": (f // 8) * 2 + lax.rem(t, 2),
        "c": lax.rem(f, 2),
    }


def device_at(spot):
    return (
        (spot["z"] // 2) * 8 + spot["y"] * 2 + spot["c"],
        spot["x"] * 2 + lax.rem(spot["z"], 2),
    )


def shifted(spot, axis, by):
    return {**spot, axis: lax.rem(spot[axis] + by + 4, 4)}


def sibling(spot):
    return {**spot, "c": 1 - spot["c"]}


def member(me, number):
    return device_at({**me, "x": number // 2, "c": lax.rem(number, 2)})


def crossed(me):
    return device_at({**me, "z": me["z"] + 1 - 2 * lax.rem(me["z"], 2), "c": 1 - me["c"]})


def greet(me):
    rank = 2 * me["x"] + me["c"]
    devices = [member(me, lax.rem(rank + step, GROUP)) for step in range(1, GROUP)]
    devices += [device_at(shifted(me, axis, by)) for axis in "yz" for by in STEPS]
    devices += [crossed(me)]
    barrier = pltpu.get_barrier_semaphore()
    for device in devices:
        pl.semaphore_signal(barrier, inc=1, device_id=device, device_id_type=MESH)
    return lambda: pl.semaphore_wait(barrier, len(devices))


def view(ref, spot, full, core=None, rows=slice(None)):
    whole = slice(None)
    index = [
        whole if "x" in full else spot["x"],
        whole if "z" in full else lax.rem(spot["z"], 2),
        whole if "z" in full else spot["z"] // 2,
        whole if "y" in full else spot["y"],
    ]
    if core is not None:
        index.append(core)
    return ref.at[tuple(index) + (rows,)]


def decode(number, spot, full):
    at = {}
    for axis in "yzx":
        if axis in full:
            parts = []
            for size in reversed(SIZES[axis]):
                parts.append(lax.rem(number, size))
                number = number // size
            at[axis] = tuple(reversed(parts))
    fixed = {"x": (spot["x"],), "z": (lax.rem(spot["z"], 2), spot["z"] // 2), "y": (spot["y"],)}
    index, inner = (), ()
    for axis in "xzy":
        index += at.get(axis, fixed[axis])
        inner += at.get(axis, ())
    return index, inner


def bundle_shape(full):
    shape = ()
    for axis in "xzy":
        shape += SIZES[axis] if axis in full else ()
    return shape


def remote(src, dst, send, recv, device):
    copy = pltpu.make_async_remote_copy(
        src, dst, send, recv, device_id=device, device_id_type=MESH
    )
    copy.start()
    return copy


def take(ref, semaphore):
    pltpu.make_async_copy(ref, ref, semaphore).wait()


class Gather:
    sends, recvs = 5, 8

    def __init__(self, me, order, block, out, send, recv, local):
        self.me, self.order, self.block, self.out = me, order, block, out
        self.send, self.recv, self.local = send, recv, local
        self.core = me["c"]
        self.half = out.shape[-2] // 2
        self.plane = "".join(order[:2])

    def piece(self, spot, full, rows=slice(None)):
        return view(self.out, spot, full, self.core, rows)

    def spread(self, spot, full, axis, by, send, recv, rows=slice(None)):
        piece = self.piece(spot, full, rows)
        target = device_at(shifted(self.me, axis, by))
        remote(piece, piece, self.send.at[send], self.recv.at[recv], target)

    def share(self, spot):
        piece = self.piece(spot, self.plane)
        remote(piece, piece, self.send.at[4], self.recv.at[7], device_at(sibling(self.me)))

    def own(self):
        return pltpu.make_async_copy(
            self.block, view(self.out, self.me, "", self.core), self.local
        )

    def first(self):
        me, axis = self.me, self.order[0]
        self.own().start()
        for by in STEPS:
            target = device_at(shifted(me, axis, by))
            remote(self.block, self.piece(me, ""), self.send.at[0], self.recv.at[0], target)

    def second(self):
        self.own().wait()
        take(self.out.at[:3, 0, 0, 0, 0], self.recv.at[0])
        for by in STEPS:
            self.spread(self.me, self.order[0], self.order[1], by, 1, 1)

    def rows(self, way):
        return pl.ds(way * self.half, self.half)

    def third(self):
        take(self.out.at[:3, 0, 0, :, 0], self.recv.at[1])
        axis = self.order[2]
        for number, (by, way) in enumerate(((1, 0), (-1, 1), (1, 1), (-1, 0))):
            self.spread(self.me, self.plane, axis, by, 2, 2 + number, self.rows(way))
        self.share(self.me)

    def far(self):
        axis = self.order[2]
        for way, by in enumerate((1, -1)):
            take(self.out.at[:, 0, 0, :, 0, : self.half], self.recv.at[2 + way])
            spot = shifted(self.me, axis, -by)
            self.spread(spot, self.plane, axis, by, 3, 6, self.rows(way))

    def rest(self):
        for way, by in enumerate((1, -1)):
            take(self.out.at[:, 0, 0, :, 0, : self.half], self.recv.at[4 + way])
            self.share(shifted(self.me, self.order[2], -by))

    def last(self):
        take(self.out.at[:, 0, 0, :, 0], self.recv.at[6])
        self.share(shifted(self.me, self.order[2], 2))

    def done(self):
        take(self.out.at[:, :, :, :, 0], self.recv.at[7])

    def sent(self):
        out = self.out
        take(out.at[:3, 0, 0, 0, 0], self.send.at[0])
        take(out.at[:3, 0, 0, :, 0], self.send.at[1])
        take(out.at[:, :, 0, :, 0], self.send.at[2])
        take(out.at[:, 0, 0, :, 0], self.send.at[3])
        take(out.at[:, :, :, :, 0], self.send.at[4])


class Reduce:
    sends, recvs = 4, 5

    def __init__(self, me, order, acc, near, far, mid, tail, send, recv):
        self.me, self.order, self.acc = me, order, acc
        self.nears, self.fars, self.mid, self.tail = near, far, mid, tail
        self.send, self.recv = send, recv
        self.half = acc.shape[-2] // 2
        self.full = "".join(order[:2])

    def chunk(self, by):
        return shifted(self.me, self.order[2], by)

    def rows(self, way):
        return pl.ds(way * self.half, self.half)

    def add(self, spot, full, first, rows, terms):
        acc = self.acc

        def one(number, carry):
            index, inner = decode(number, spot, full)
            here = index + (pl.ds(first, rows),)
            total = acc[here]
            if len(terms) > 1:
                total = total.astype(F32)
            for ref, lead in terms:
                rows_there = pl.ds(first, rows) if ref.shape[-2] == acc.shape[-2] else slice(None)
                total += ref[(lead,) + inner + (rows_there,)].astype(total.dtype)
            acc[here] = total.astype(acc.dtype)
            return carry

        lax.fori_loop(0, math.prod(bundle_shape(full)), one, 0)

    def near(self, by, way):
        spot = self.chunk(by)
        box = self.nears.at[0 if by == 1 else 1]
        lead = (slice(None),) * (len(self.nears.shape) - 3)
        remote(
            view(self.acc, spot, self.full, None, self.rows(way)),
            box.at[lead + (self.rows(way),)],
            self.send.at[1],
            self.recv.at[2],
            device_at(spot),
        )

    def stage_far(self):
        spot = self.chunk(2)
        for way, by in enumerate((1, -1)):
            remote(
                view(self.acc, spot, self.full, None, self.rows(way)),
                self.fars.at[way],
                self.send.at[0],
                self.recv.at[way],
                device_at(self.chunk(by)),
            )
        for way, by in enumerate((1, -1)):
            self.near(by, 1 - way)

    def stage_near(self):
        for way, by in enumerate((1, -1)):
            take(self.fars.at[way], self.recv.at[way])
            self.add(self.chunk(by), self.full, way * self.half, self.half, [(self.fars, way)])
            self.near(by, way)

    def spread(self, axis, full, target, send, recv):
        for number, by in enumerate(STEPS):
            spot = shifted(self.me, axis, by)
            remote(
                view(self.acc, spot, full),
                target.at[number],
                self.send.at[send],
                self.recv.at[recv],
                device_at(spot),
            )

    def stage_mid(self):
        take(self.nears, self.recv.at[2])
        self.add(self.me, self.full, 0, 2 * self.half, [(self.nears, 0), (self.nears, 1)])
        self.spread(self.order[1], self.order[0], self.mid, 2, 3)

    def stage_tail(self):
        take(self.mid, self.recv.at[3])
        self.add(self.me, self.order[0], 0, 2 * self.half, [(self.mid, i) for i in range(3)])
        self.spread(self.order[0], "", self.tail, 3, 4)

    def stage_out(self):
        take(self.tail, self.recv.at[4])
        index, _ = decode(0, self.me, "")
        total = self.acc[index].astype(F32)
        for number in range(3):
            total += self.tail[number].astype(F32)
        return total

    def sent(self):
        take(self.fars, self.send.at[0])
        take(self.nears, self.send.at[1])
        take(self.mid, self.send.at[2])
        take(self.tail, self.send.at[3])


def reduce_scratch(order, lanes):
    full = bundle_shape(order[:2])
    return [
        pltpu.VMEM((4, 2, 2, 4, 64, lanes), BF16),
        pltpu.VMEM((2,) + full + (64, lanes), BF16),
        pltpu.VMEM((2,) + full + (32, lanes), BF16),
        pltpu.VMEM((3,) + bundle_shape(order[:1]) + (64, lanes), BF16),
        pltpu.VMEM((3, 64, lanes), BF16),
    ]


class Totals:
    def __init__(self, me, sums, inbox, send, recv):
        self.rounds = [[shifted(me, axis, by) for by in STEPS] for axis in "xyz"] + [[sibling(me)]]
        self.sums, self.inbox, self.send, self.recv = sums, inbox, send, recv

    def heard(self, number):
        return self.inbox.at[number, pl.ds(0, len(self.rounds[number]))]

    def speak(self, number):
        for i, spot in enumerate(self.rounds[number]):
            remote(
                self.sums.at[number],
                self.inbox.at[number, i],
                self.send.at[number],
                self.recv.at[number],
                device_at(spot),
            )

    def hear(self, number):
        take(self.heard(number), self.recv.at[number])
        total = self.sums[number]
        for i in range(len(self.rounds[number])):
            total += self.inbox[number, i]
        self.sums[number + 1] = total

    def pass_on(self, number):
        self.hear(number)
        self.speak(number + 1)

    def sent(self):
        for number in range(4):
            take(self.heard(number), self.send.at[number])


def norm_stats(values):
    average = jnp.mean(values, -1, keepdims=True)
    centered = values - average
    inverse = lax.rsqrt(jnp.mean(centered * centered, -1, keepdims=True) + EPSILON)
    return (centered * inverse, inverse)


def norm_back(upstream, normed, inverse, gain_vector):
    scaled = upstream * gain_vector
    return inverse * (
        scaled
        - jnp.mean(scaled, -1, keepdims=True)
        - normed * jnp.mean(scaled * normed, -1, keepdims=True)
    )


def softmax_columns(key_rows, queries, hidden):
    scores = mm(key_rows, queries, NT) + hidden
    powers = jnp.exp((scores - jnp.max(scores, 0, keepdims=True)) * SCALE)
    return powers * (1.0 / jnp.sum(powers, 0, keepdims=True))


def hidden_rows(seq, slot, tokens):
    row = lax.broadcasted_iota(jnp.int32, (seq, 1), 0)
    return jnp.where(lax.rem(row, slot) < tokens, 0.0, -1e30)


def head_lanes(head):
    lane = lax.broadcasted_iota(jnp.int32, (1, 128), 1)
    return jnp.where(lane // HD == head, 1.0, 0.0).astype(BF16)


def thirds(rows):
    return [rows[:, 128 * i : 128 * i + 128] for i in range(3)]


def attend(rows, hidden):
    queries, key_rows, value_rows = thirds(rows)

    def one_head(head, before):
        mine = head_lanes(head)
        probs = softmax_columns(key_rows, queries * mine, hidden).astype(BF16)
        return before + mm(probs, value_rows * mine, TN)

    return lax.fori_loop(0, 2, one_head, jnp.zeros(queries.shape, F32)).astype(BF16)


def attend_back(rows, grads, hidden):
    queries, key_rows, value_rows = thirds(rows)

    def one_head(head, before):
        mine = head_lanes(head)
        own_grads, own_queries = grads * mine, queries * mine
        probs = softmax_columns(key_rows, own_queries, hidden)
        d_probs = mm(value_rows, own_grads, NT)
        inner = jnp.sum(probs * d_probs, 0, keepdims=True)
        d_scores = (probs * (d_probs - inner)).astype(BF16)
        return (
            before[0] + mm(d_scores, key_rows * mine, TN),
            before[1] + mm(d_scores, own_queries),
            before[2] + mm(probs.astype(BF16), own_grads),
        )

    zero = jnp.zeros(queries.shape, F32)
    d_queries, d_keys, d_values = lax.fori_loop(0, 2, one_head, (zero, zero, zero))
    return [
        (d_queries * SCALE).astype(BF16),
        (d_keys * SCALE).astype(BF16),
        d_values.astype(BF16),
    ]


def fill_rows(box, m, values):
    tokens = values.shape[0]
    box[m, :tokens] = values
    box[m, tokens:] = jnp.zeros((box.shape[1] - tokens, values.shape[1]), box.dtype)


class Swap:
    def __init__(self, me, send, recv):
        self.stays = lax.rem(me["z"], 2) == me["c"]
        self.partner = crossed(me)
        self.send, self.recv = send, recv

    def start(self, box, inbox):
        @pl.when(self.stays)
        def _():
            pltpu.make_async_copy(box, inbox, self.recv).start()

        @pl.when(jnp.logical_not(self.stays))
        def _():
            remote(box, inbox, self.send, self.recv, self.partner)

    def sent(self, box):
        @pl.when(jnp.logical_not(self.stays))
        def _():
            take(box, self.send)


def blocks_of(ref, index):
    value = ref[index // 2, lax.rem(index, 2)]
    return value.reshape(-1, value.shape[-1])


def half_planes(ref, value, kind, count):
    padded = jnp.concatenate(
        [value, jnp.zeros((ref.shape[-1] - count, value.shape[1]), value.dtype)], axis=0
    )
    ref[kind] = padded.T.reshape(ref.shape[1:])


SLABS = 4
SCHEDULE = {
    "start": (("E", "first"),),
    "first": (("A", "first"), ("E", "second"), ("B", "first")),
    "swap": (("E", "third"), ("A", "second"), ("E", "far"), ("A", "third")),
    "norm": (("V", "rest"), ("V", "last"), ("V", "done")),
    "table": (("N", "rest"), ("N", "last"), ("B", "second"), ("A", "far"), ("N", "done")),
    "project": (("B", "third"), ("A", "rest")),
    "image 0": (("A", "last"), ("E", "sent")),
    "image 1": (("B", "far"),),
    "image 2": (("B", "rest"),),
    "reply": (("A", "done"), ("B", "last"), ("A", "sent")),
    "half 0": (),
    "half 1": (("B", "done"),),
}


def forward_kernel(*refs):
    (x_ref, cot_ref, valid_ref, qkv_in, out_in, fc1_in, fc2_in), refs = refs[:7], refs[7:]
    small_in, refs = refs[:8], refs[8:]
    (
        d_middle_out,
        vectors,
        sums_out,
        result_out,
        d_attended_out,
        images_out,
        attended_out,
        turned_out,
        act_out,
        qkv_out,
        x_out,
        x_box,
        x_in,
        cot_box,
        cot_in,
        result_box,
        wq,
        wk,
        wv,
        up_a,
        up_b,
        side_a,
        down_xa,
        down_b,
        side_own,
        small_own,
        small,
        bias,
        hidden_bias,
        low,
        outbox,
        images,
        attended_box,
        attended,
        middle,
        normed_two,
        low_two,
        turned,
        forward_sum,
        back_sum,
        act_box,
        d_outbox,
        hidden_sums,
        local_sem,
        gather_send,
        gather_recv,
        send_sem,
        recv_sem,
        back_send,
        back_recv,
        store_sem,
        sib_send,
        sib_recv,
        ff_local,
        ff_send,
        ff_recv,
        swap_send,
        swap_recv,
    ) = refs
    me = place()
    core = me["c"]
    t = 2 * me["x"] + core
    other = device_at(sibling(me))
    micro, tokens, width = x_ref.shape
    slot = x_in.shape[1]
    count = micro * slot
    met = greet(me)
    heads = [wq, wk, wv]
    made = []

    def gather(order, block, out):
        i = len(made)
        made.append(
            Gather(me, order, block, out, gather_send.at[i], gather_recv.at[i], local_sem.at[i])
        )
        return made[-1]

    narrow = [gather(ORDERS[i], qkv_in.at[i], heads[i]) for i in range(3)]
    vector = gather(ORDERS[0], small_own, small)
    early = [vector] + narrow
    first_half = [
        gather(ORDERS[2], fc1_in.at[:, :256], up_a),
        gather(ORDERS[0], side_own, side_a),
        gather(ORDERS[1], fc2_in.at[:, :128], down_xa),
    ]
    second_half = [
        gather(ORDERS[0], fc1_in.at[:, 256:], up_b),
        gather(ORDERS[2], fc2_in.at[:, 256:], down_b),
    ]
    groups = {
        "V": [vector],
        "N": narrow,
        "E": early,
        "A": first_half,
        "B": second_half,
    }

    def run(point):
        for names, stage in SCHEDULE[point]:
            for name in names:
                for part in groups[name]:
                    getattr(part, stage)()

    stores = []

    def store(src, dst):
        copy = pltpu.make_async_copy(src, dst, store_sem.at[len(stores)])
        copy.start()
        stores.append(copy)

    shared = []

    def share(src, dst):
        slot_of = len(shared)
        copy = pltpu.make_async_remote_copy(
            src,
            dst,
            sib_send.at[slot_of],
            sib_recv.at[slot_of],
            device_id=other,
            device_id_type=MESH,
        )
        copy.start()
        shared.append(copy)

    def turn(kind, value):
        half_planes(turned, value, kind, count)
        store(turned.at[kind, :, core], turned_out.at[kind, 0])
        share(turned.at[kind, :, 1 - core], turned_out.at[kind, 1])

    for m in range(micro):
        fill_rows(x_box, m, x_ref[m])
    side_own[:, :128] = out_in[...]
    side_own[:, 128:] = fc2_in[:, 128:256]
    small_own[...] = jnp.zeros_like(small_own)
    for v in range(6):
        small_own[0:1, 8 * v : 8 * v + 8] = small_in[v][...]
    for i in range(2):
        for j in range(2):
            at = 48 + 8 * i + 4 * j
            small_own[0:1, at : at + 4] = small_in[6][i, j : j + 1]
    for i in range(4):
        small_own[0:1, 64 + 8 * i : 72 + 8 * i] = small_in[7][i : i + 1]
    met()
    run("start")
    swaps = [Swap(me, swap_send.at[i], swap_recv.at[i]) for i in range(3)]
    swaps[0].start(x_box, x_in)
    run("first")
    for m in range(micro):
        fill_rows(cot_box, m, (cot_ref[m].astype(F32) * valid_ref[0, m].astype(F32)).astype(BF16))
    run("swap")
    take(x_in, swap_recv.at[0])
    store(x_in, x_out)

    def rows_of(ref):
        return ref[...].reshape(count, width).astype(F32)

    normed, _ = norm_stats(rows_of(x_in))
    run("norm")
    table = jnp.sum(small[...].reshape(128, 32, 128).astype(F32), 1).astype(BF16)
    lane = lax.broadcasted_iota(jnp.int32, (128, 1024), 0)
    column = lax.broadcasted_iota(jnp.int32, (128, 1024), 1)
    owner = jnp.where(lax.rem(lane, 16) * 8 + lane // 16 == column // 8, 1.0, 0.0)
    for v in range(6):
        pick = jnp.where(lane == v * 8 + lax.rem(column, 8), 1.0, 0.0).astype(BF16)
        vectors[v : v + 1, :] = jnp.sum(mm(table, pick) * owner, 0, keepdims=True)
    vectors[6:8, :] = jnp.zeros((2, 1024), F32)

    def spread_bias(lanes, first, major, minor):
        lane = lax.broadcasted_iota(jnp.int32, (128, lanes), 0)
        column = lax.broadcasted_iota(jnp.int32, (128, lanes), 1)
        pick = lane == first + (column // 64) * major + lax.rem(column, 4) * minor
        owner = lax.rem(lane, 16) == lax.rem(column, 64) // 4
        values = mm(table, jnp.where(pick, 1.0, 0.0).astype(BF16))
        return jnp.sum(jnp.where(owner, values, 0.0).reshape(8, 16, lanes), 1)

    hidden_value = spread_bias(512, 64, 1, 8)
    query_bias, value_bias = spread_bias(128, 48, 4, 1), spread_bias(128, 56, 4, 1)
    for i in range(GROUP):
        hidden_bias[i] = hidden_value[i : i + 1]
        bias[i, :, 0:128] = query_bias[i : i + 1]
        bias[i, :, 128:256] = jnp.zeros((1, 128), F32)
        bias[i, :, 256:384] = value_bias[i : i + 1]
    low[...] = (normed * vectors[0:1, :] + vectors[1:2, :]).astype(BF16)
    run("table")

    def letter(k, m):
        target = lax.rem(t + k + 1, GROUP)
        return pltpu.make_async_remote_copy(
            outbox.at[target, m],
            images.at[t, m],
            send_sem,
            recv_sem.at[m],
            device_id=member(me, target),
            device_id_type=MESH,
        )

    def project(k, carry):
        target = lax.rem(t + k + 1, GROUP)
        weights = jnp.concatenate([blocks_of(w, target) for w in heads], axis=1)
        result = (mm(low[...], weights) + bias[target]).astype(BF16)
        outbox[target] = result.reshape(outbox.shape[1:])

        @pl.when(k < GROUP - 1)
        def _():
            letter(k, 0).start()

        return carry

    lax.fori_loop(0, GROUP, project, 0)
    for m in range(1, MICRO):
        for k in range(GROUP - 1):
            letter(k, m).start()
    own = pltpu.make_async_copy(outbox.at[t], images.at[t], local_sem.at[len(made)])
    own.start()
    for i in range(3):
        store(heads[i], qkv_out.at[i])
    swaps[1].start(cot_box, cot_in)
    run("project")
    turn(0, low[...])
    own.wait()
    hidden = hidden_rows(GROUP * slot, slot, tokens)

    def reply(m, k):
        target = lax.rem(t + k + 1, GROUP)
        return pltpu.make_async_remote_copy(
            attended_box.at[m, target],
            attended.at[t, m],
            back_send,
            back_recv,
            device_id=member(me, target),
            device_id_type=MESH,
        )

    for m in range(MICRO):
        take(images.at[: GROUP - 1, m], recv_sem.at[m])
        result = attend(images[:, m].reshape(GROUP * slot, 384), hidden)
        attended_box[m] = result.reshape(GROUP, slot, 128)
        for k in range(GROUP - 1):
            reply(m, k).start()
        attended[t, m] = attended_box[m, t]
        run(("image 0", "image 1", "image 2")[m])
        if m == 1:
            take(cot_in, swap_recv.at[1])
            upstream_low = cot_in[...].reshape(count, width)
            sums_out[3:4, :] = jnp.sum(upstream_low.astype(F32), 0, keepdims=True)
            turn(1, upstream_low)
    store(images, images_out)
    take(attended.at[: GROUP - 1], back_recv)
    store(attended, attended_out.at[0])
    share(attended, attended_out.at[1])
    run("reply")
    middle[...] = rows_of(x_in) + vectors[2:3, :]

    def out_weights(pair):
        both = [blocks_of(side_a, 2 * pair + i)[:, :128] for i in range(2)]
        return jnp.concatenate(both, axis=1)

    def out_project(pair, carry):
        both = [attended[2 * pair + i].reshape(count, 128) for i in range(2)]
        middle[...] += mm(jnp.concatenate(both, axis=1), out_weights(pair), NT)
        return carry

    lax.fori_loop(0, GROUP // 2, out_project, 0)
    normed, inverse = norm_stats(middle[...])
    normed_two[...] = normed
    low_two[...] = (normed * vectors[3:4, :] + vectors[4:5, :]).astype(BF16)
    turn(2, low_two[...])
    forward_sum[...] = jnp.zeros_like(forward_sum)
    back_sum[...] = jnp.zeros_like(back_sum)

    def ship(step, h):
        at = (pl.ds(SLABS * step, SLABS), slice(None), pl.ds(2 * count * h, 2 * count))
        piece = act_box.at[at]
        pltpu.make_async_copy(piece, act_out.at[(0,) + at], ff_local).start()
        remote(piece, act_out.at[(1,) + at], ff_send, ff_recv, other)

    for h in range(2):
        run(("half 0", "half 1")[h])

        def feed_forward(step, carry):
            slabs = [SLABS * step + n for n in range(SLABS)]
            up_weight = jnp.concatenate([blocks_of((up_a, up_b)[h], i) for i in slabs], axis=1)
            down = []
            for i in slabs:
                if h == 0:
                    down += [blocks_of(down_xa, i), blocks_of(side_a, i)[:, 128:]]
                else:
                    down.append(blocks_of(down_b, i))
            down_weight = jnp.concatenate(down, axis=1)
            biases = [hidden_bias[i, :, 256 * h : 256 * h + 256] for i in slabs]
            up_proj = mm(low_two[...], up_weight) + jnp.concatenate(biases, axis=1)
            gate = jax.nn.sigmoid(1.702 * up_proj)
            activated = (up_proj * gate).astype(BF16)
            d_act = mm(cot_in[...].reshape(count, width), down_weight)
            d_up = (d_act * (gate + 1.702 * up_proj * gate * (1.0 - gate))).astype(BF16)
            column_sums = jnp.sum(d_up.astype(F32), 0, keepdims=True)
            for n, i in enumerate(slabs):
                for j in range(2):
                    at = pl.ds(count * (2 * h + j), count)
                    lanes = slice(256 * n + 128 * j, 256 * n + 128 * (j + 1))
                    act_box[i, 0, at] = activated[:, lanes]
                    act_box[i, 1, at] = d_up[:, lanes]
                hidden_sums[i, :, 256 * h : 256 * h + 256] = column_sums[:, 256 * n : 256 * n + 256]
            ship(step, h)
            forward_sum[...] += mm(activated, down_weight, NT)
            back_sum[...] += mm(d_up, up_weight, NT)
            return carry

        lax.fori_loop(0, GROUP // SLABS, feed_forward, 0)
    output = (middle[...] + forward_sum[...] + vectors[5:6, :]).astype(BF16)
    result_box[...] = output.reshape(result_box.shape)
    swaps[2].start(result_box, result_out)
    d_norm = back_sum[...]
    normed = normed_two[...]
    d_middle = rows_of(cot_in) + norm_back(
        d_norm, normed, inverse, vectors[3:4, :]
    )
    d_middle_out[...] = d_middle
    low[...] = d_middle.astype(BF16)

    def project_back(pair, carry):
        both = mm(low[...], out_weights(pair)).astype(BF16)
        for i in range(2):
            d_outbox[2 * pair + i] = both[:, 128 * i : 128 * i + 128].reshape(d_outbox.shape[1:])
        return carry

    lax.fori_loop(0, GROUP // 2, project_back, 0)
    store(d_outbox, d_attended_out)
    turn(3, low[...])
    sums_out[0:1, :] = jnp.sum(d_middle, 0, keepdims=True)
    sums_out[1:2, :] = jnp.sum(d_norm * normed, 0, keepdims=True)
    sums_out[2:3, :] = jnp.sum(d_norm, 0, keepdims=True)
    for i in range(GROUP):
        at = 4 + i // 2
        sums_out[at : at + 1, 512 * (i % 2) : 512 * (i % 2) + 512] = hidden_sums[i]
    for swap, box in zip(swaps, (x_box, cot_box, result_box)):
        swap.sent(box)
    take(result_out, swap_recv.at[2])
    for copy in shared:
        copy.wait()
    take(act_box, ff_local)
    take(act_box, ff_send)
    take(act_box, ff_recv)
    for part in second_half:
        part.sent()
    take(outbox.at[: GROUP - 1], send_sem)
    take(attended_box.at[:, : GROUP - 1], back_send)
    for copy in stores:
        copy.wait()


ANY = pl.BlockSpec(memory_space=pl.ANY)
VMEM = pl.BlockSpec(memory_space=pltpu.VMEM)
SMEM = pl.BlockSpec(memory_space=pltpu.SMEM)


def forward(x, cotangent, valid, qkv_block, out_block, fc1_block, fc2_block, small, slot):
    width = x.shape[-1]
    count = MICRO * slot
    rows = (MICRO, slot, width)
    images = (GROUP, MICRO, slot, 384)
    attended = (GROUP, MICRO, slot, 128)
    acts = (2, GROUP, 2, 4 * count, 128)
    return pl.pallas_call(
        forward_kernel,
        out_shape=[
            jax.ShapeDtypeStruct((count, width), F32),
            jax.ShapeDtypeStruct((8, width), F32),
            jax.ShapeDtypeStruct((8, width), F32),
            jax.ShapeDtypeStruct(rows, BF16),
            jax.ShapeDtypeStruct(attended, BF16),
            jax.ShapeDtypeStruct(images, BF16),
            jax.ShapeDtypeStruct((2,) + attended, BF16),
            jax.ShapeDtypeStruct((4, 2, 8, 64, 256), BF16),
            jax.ShapeDtypeStruct(acts, BF16),
            jax.ShapeDtypeStruct((3,) + LEAD + (64, 128), BF16),
            jax.ShapeDtypeStruct(rows, BF16),
        ],
        in_specs=[VMEM, VMEM, SMEM, ANY, VMEM, ANY, VMEM] + [VMEM] * 8,
        out_specs=[VMEM] * 3 + [ANY] * 8,
        scratch_shapes=[
            pltpu.VMEM(rows, BF16),
            pltpu.VMEM(rows, BF16),
            pltpu.VMEM(rows, BF16),
            pltpu.VMEM(rows, BF16),
            pltpu.VMEM(rows, BF16),
            pltpu.VMEM(LEAD + (64, 128), BF16),
            pltpu.VMEM(LEAD + (64, 128), BF16),
            pltpu.VMEM(LEAD + (64, 128), BF16),
            pltpu.VMEM(LEAD + (64, 256), BF16),
            pltpu.VMEM(LEAD + (64, 256), BF16),
            pltpu.VMEM(LEAD + (64, 256), BF16),
            pltpu.VMEM(LEAD + (64, 128), BF16),
            pltpu.VMEM(LEAD + (64, 256), BF16),
            pltpu.VMEM((64, 256), BF16),
            pltpu.VMEM((32, 128), BF16),
            pltpu.VMEM(LEAD + (32, 128), BF16),
            pltpu.VMEM((GROUP, 1, 384), F32),
            pltpu.VMEM((GROUP, 1, 512), F32),
            pltpu.VMEM((count, width), BF16),
            pltpu.VMEM(images, BF16),
            pltpu.VMEM(images, BF16),
            pltpu.VMEM((MICRO, GROUP, slot, 128), BF16),
            pltpu.VMEM(attended, BF16),
            pltpu.VMEM((count, width), F32),
            pltpu.VMEM((count, width), F32),
            pltpu.VMEM((count, width), BF16),
            pltpu.VMEM((4, 8, 2, 64, 256), BF16),
            pltpu.VMEM((count, width), F32),
            pltpu.VMEM((count, width), F32),
            pltpu.VMEM(acts[1:], BF16),
            pltpu.VMEM(attended, BF16),
            pltpu.VMEM((GROUP, 1, 512), F32),
            pltpu.SemaphoreType.DMA((12,)),
            pltpu.SemaphoreType.DMA((10, Gather.sends)),
            pltpu.SemaphoreType.DMA((10, Gather.recvs)),
            pltpu.SemaphoreType.DMA,
            pltpu.SemaphoreType.DMA((MICRO,)),
            pltpu.SemaphoreType.DMA,
            pltpu.SemaphoreType.DMA,
            pltpu.SemaphoreType.DMA((11,)),
            pltpu.SemaphoreType.DMA((5,)),
            pltpu.SemaphoreType.DMA((5,)),
            pltpu.SemaphoreType.DMA,
            pltpu.SemaphoreType.DMA,
            pltpu.SemaphoreType.DMA,
            pltpu.SemaphoreType.DMA((3,)),
            pltpu.SemaphoreType.DMA((3,)),
        ],
        compiler_params=pltpu.CompilerParams(
            collective_id=0, has_side_effects=True, vmem_limit_bytes=VMEM_LIMIT
        ),
        name="forward",
    )(x, cotangent, valid, qkv_block, out_block, fc1_block, fc2_block, *small)


BACK_SCHEDULE = {
    "early": True,
    "image 0": (("down", 0), (0, -1), ("U", "stage_near")),
    "image 1": (("V", "stage_near"), (0, 0)),
    "image 2": (("D", "stage_near"), (0, 1)),
    "norm": (("U", "stage_mid"), ("V", "stage_mid"), ("D", "stage_mid"), (0, 2)),
    "late": ((0, 3), ("L", "stage_near")),
    "rows": (
        (1, 0),
        ("L", "stage_mid"),
        (1, 1),
        ("U", "stage_tail"),
        ("V", "stage_tail"),
        ("D", "stage_tail"),
        ("L", "stage_tail"),
        (1, 2),
    ),
    "wide": (("U", "sent"), ("V", "sent"), ("D", "sent")),
    "end": ((1, 3),),
}


def backward_kernel(*refs):
    (
        d_attended_in,
        images_in,
        attended_in,
        turned_in,
        act_in,
        qkv_in,
        x_in,
        d_middle_ref,
        vectors_ref,
        sums_ref,
        qkv_grad,
        out_grad,
        fc1_grad,
        fc2_grad,
        totals_out,
        input_grad_out,
        rows,
        box,
        pool,
        turned,
        attended,
        images,
        d_attended,
        outbox,
        d_images,
        d_norm,
        sums,
        sums_in,
        *rest,
    ) = refs
    scratch, sems = rest[: 5 * len(REDUCED)], rest[5 * len(REDUCED) :]
    (
        load_sem,
        reduce_send,
        reduce_recv,
        send_sem,
        recv_sem,
        back_send,
        back_recv,
        sib_send,
        sib_recv,
        sum_send,
        sum_recv,
        swap_send,
        swap_recv,
    ) = sems
    me = place()
    t = 2 * me["x"] + me["c"]
    other = device_at(sibling(me))
    met = greet(me)
    slot = rows.shape[1]
    count = MICRO * slot
    parts = [
        Reduce(
            me,
            REDUCED[i][0],
            *scratch[5 * i : 5 * i + 5],
            reduce_send.at[i],
            reduce_recv.at[i],
        )
        for i in range(len(REDUCED))
    ]
    late = parts[-3:]
    wide = parts[:-3]
    totals = [
        Totals(me, sums.at[i], sums_in.at[i], sum_send.at[i], sum_recv.at[i]) for i in range(2)
    ]
    loads = {}

    def load(name, src, dst):
        loads[name] = pltpu.make_async_copy(src, dst, load_sem.at[len(loads)])
        loads[name].start()

    kept = pl.ds(0, 4 * count)
    load("turned", turned_in, turned)
    for i in range(2):
        load(("dup", i), act_in.at[i, :, 1], pool.at[2 + i, :, kept])
    load("images", images_in, images)
    load("own", d_attended_in.at[t], d_attended.at[t])
    for i in range(2):
        load(("act", i), act_in.at[i, :, 0], pool.at[i, :, kept])
    load("attended", attended_in, attended)
    load("rows", x_in, rows)
    sums[0, 0] = sums_ref[...]

    def both_cores(kind, values):
        total = 0.0
        for i in range(2):
            left = turned[kind, i].reshape(512, 256)[:, :count]
            total += mm(left, values[i])
        return total.astype(BF16)

    def pooled(first, index, lanes):
        return [
            jnp.concatenate(
                [pool[first + i, index, count * j : count * (j + 1)] for j in lanes], axis=1
            )
            for i in range(2)
        ]

    def spot_of(index):
        return (index // 2, lax.rem(index, 2))

    def fill(part, index, lanes, value):
        acc = part.acc
        acc[spot_of(index) + (slice(None),) * 3 + (lanes,)] = value.reshape(
            acc.shape[2:-1] + (value.shape[-1],)
        )

    def grads_up(half):
        def one(index, carry):
            value = both_cores(2, pooled(2, index, (2 * half, 2 * half + 1)))
            fill(wide[half], index, slice(0, 256), value)
            return carry

        return one

    def grads_down(index, carry):
        value = both_cores(1, pooled(0, index, range(4)))
        fill(wide[2], index, slice(0, 128), value[:, :128])
        fill(wide[3], index, slice(0, 256), value[:, 128:384])
        fill(wide[4], index, slice(0, 128), value[:, 384:])
        value = both_cores(3, [attended[i, index].reshape(count, 128) for i in range(2)])
        fill(wide[4], index, slice(128, 256), value)
        return carry

    loads["turned"].wait()
    for i in range(2):
        loads["dup", i].wait()
    met()
    for m in range(MICRO):
        for k in range(GROUP - 1):
            target = lax.rem(t + k + 1, GROUP)
            remote(
                d_attended_in.at[target, m],
                d_attended.at[t, m],
                send_sem,
                recv_sem.at[m],
                member(me, target),
            )
    lax.fori_loop(0, GROUP, grads_up(0), 0)
    wide[0].stage_far()
    if BACK_SCHEDULE["early"]:
        lax.fori_loop(0, GROUP, grads_up(1), 0)
        wide[1].stage_far()
    loads["images"].wait()
    loads["own"].wait()
    hidden = hidden_rows(GROUP * slot, slot, TOKENS)

    def reply(m, k):
        target = lax.rem(t + k + 1, GROUP)
        return pltpu.make_async_remote_copy(
            outbox.at[m, target],
            d_images.at[0, t, m],
            back_send,
            back_recv.at[k],
            device_id=member(me, target),
            device_id_type=MESH,
        )

    def down():
        for i in range(2):
            loads["act", i].wait()
        loads["attended"].wait()
        lax.fori_loop(0, GROUP, grads_down, 0)
        for part in wide[2:]:
            part.stage_far()
        for i in range(3):
            load(("weight", i), qkv_in.at[i], pool.at[i])

    groups = {"U": wide[:1], "V": wide[1:2], "D": wide[2:], "L": late}

    def run(point):
        for name, stage in BACK_SCHEDULE[point]:
            if name == "down":
                down()
            elif name == "up":
                lax.fori_loop(0, GROUP, grads_up(1), 0)
                wide[1].stage_far()
            elif name in groups:
                for part in groups[name]:
                    getattr(part, stage)()
            elif stage < 0:
                totals[name].speak(0)
            elif stage < 3:
                totals[name].pass_on(stage)
            else:
                totals[name].hear(3)

    for m in range(MICRO):
        take(d_attended.at[: GROUP - 1, m], recv_sem.at[m])
        results = attend_back(
            images[:, m].reshape(GROUP * slot, 384),
            d_attended[:, m].reshape(GROUP * slot, 128),
            hidden,
        )
        for i in range(3):
            outbox[m, :, :, 128 * i : 128 * i + 128] = results[i].reshape(GROUP, slot, 128)
        for k in range(GROUP - 1):
            reply(m, k).start()
        d_images[0, t, m] = outbox[m, t]
        run(("image 0", "image 1", "image 2")[m])
    loads["rows"].wait()
    normed, inverse = norm_stats(rows[...].reshape(count, rows.shape[-1]).astype(F32))
    run("norm")

    def share(k):
        source = lax.rem(t + k + 1, GROUP)
        remote(d_images.at[0, source], d_images.at[1, source], sib_send, sib_recv, other)

    share(GROUP - 1)
    for k in reversed(range(GROUP - 1)):
        take(d_images.at[0, 0], back_recv.at[GROUP - 2 - k])
        share(k)
    for i in range(3):
        loads["weight", i].wait()
    d_norm[...] = jnp.zeros_like(d_norm)

    def project_back(index, carry):
        weights = jnp.concatenate([pool[i, index] for i in range(3)], axis=1)
        d_norm[...] += mm(d_images[0, index].reshape(count, 384), weights, NT)
        return carry

    lax.fori_loop(0, GROUP, project_back, 0)
    take(d_images.at[1], sib_recv)

    def grads_late(index, carry):
        value = both_cores(0, [d_images[i, index].reshape(count, 384) for i in range(2)])
        for i, part in enumerate(late):
            fill(part, index, slice(None), value[:, 128 * i : 128 * i + 128])
        return carry

    lax.fori_loop(0, GROUP, grads_late, 0)
    for part in late:
        part.stage_far()
    gradient = d_norm[...]
    sums[1, 0, 0:1, :] = jnp.sum(gradient * normed, 0, keepdims=True)
    sums[1, 0, 1:2, :] = jnp.sum(gradient, 0, keepdims=True)
    for index in range(GROUP):
        grads = jnp.sum(d_images[0, index].reshape(count, 384).astype(F32), 0, keepdims=True)
        sums[1, 0, 2:3, 128 * index : 128 * index + 128] = grads[:, :128]
        sums[1, 0, 3:4, 128 * index : 128 * index + 128] = grads[:, 256:]
    sums[1, 0, 4:8, :] = jnp.zeros((4, sums.shape[-1]), F32)
    totals[1].speak(0)
    run("late")
    result = d_middle_ref[...] + norm_back(gradient, normed, inverse, vectors_ref[0:1, :])
    box[...] = result.astype(BF16).reshape(box.shape)
    swap = Swap(me, swap_send, swap_recv)
    swap.start(box, input_grad_out)
    run("rows")
    fc1_grad[:, :256] = wide[0].stage_out()
    fc1_grad[:, 256:] = wide[1].stage_out()
    fc2_grad[:, :128] = wide[2].stage_out()
    fc2_grad[:, 128:384] = wide[3].stage_out()
    value = wide[4].stage_out()
    fc2_grad[:, 384:] = value[:, :128]
    out_grad[...] = value[:, 128:]
    run("wide")
    for i in range(3):
        qkv_grad[i] = late[i].stage_out()
    run("end")
    totals_out[0:8, :] = sums[0, 4]
    totals_out[8:16, :] = sums[1, 4]
    for part in late:
        part.sent()
    for total in totals:
        total.sent()
    take(d_images.at[1], sib_send)
    take(outbox.at[:, : GROUP - 1], back_send)
    take(d_attended.at[: GROUP - 1], send_sem)
    swap.sent(box)
    take(input_grad_out, swap_recv)


REDUCED = (
    (ORDERS[2], 256),
    (ORDERS[0], 256),
    (ORDERS[1], 128),
    (ORDERS[2], 256),
    (ORDERS[0], 256),
    (ORDERS[0], 128),
    (ORDERS[1], 128),
    (ORDERS[2], 128),
)


def backward(d_attended, images, attended, turned, act, qkv, x, d_middle, vectors, sums):
    width = x.shape[-1]
    slot = x.shape[1]
    count = MICRO * slot
    scratch = []
    for order, lanes in REDUCED:
        scratch += reduce_scratch(order, lanes)
    return pl.pallas_call(
        backward_kernel,
        out_shape=[
            jax.ShapeDtypeStruct((3, 64, 128), F32),
            jax.ShapeDtypeStruct((64, 128), F32),
            jax.ShapeDtypeStruct((64, 512), F32),
            jax.ShapeDtypeStruct((64, 512), F32),
            jax.ShapeDtypeStruct((16, width), F32),
            jax.ShapeDtypeStruct(x.shape, BF16),
        ],
        in_specs=[ANY] * 7 + [VMEM] * 3,
        out_specs=[VMEM] * 5 + [ANY],
        scratch_shapes=[
            pltpu.VMEM(x.shape, BF16),
            pltpu.VMEM(x.shape, BF16),
            pltpu.VMEM((4, GROUP, width, 128), BF16),
            pltpu.VMEM(turned.shape, BF16),
            pltpu.VMEM(attended.shape, BF16),
            pltpu.VMEM(images.shape, BF16),
            pltpu.VMEM(d_attended.shape, BF16),
            pltpu.VMEM((MICRO, GROUP, slot, 384), BF16),
            pltpu.VMEM((2,) + images.shape, BF16),
            pltpu.VMEM((count, width), F32),
            pltpu.VMEM((2, 5, 8, width), F32),
            pltpu.VMEM((2, 4, 3, 8, width), F32),
        ]
        + scratch
        + [
            pltpu.SemaphoreType.DMA((12,)),
            pltpu.SemaphoreType.DMA((len(REDUCED), Reduce.sends)),
            pltpu.SemaphoreType.DMA((len(REDUCED), Reduce.recvs)),
            pltpu.SemaphoreType.DMA,
            pltpu.SemaphoreType.DMA((MICRO,)),
            pltpu.SemaphoreType.DMA,
            pltpu.SemaphoreType.DMA((GROUP,)),
            pltpu.SemaphoreType.DMA,
            pltpu.SemaphoreType.DMA,
            pltpu.SemaphoreType.DMA((2, 4)),
            pltpu.SemaphoreType.DMA((2, 4)),
            pltpu.SemaphoreType.DMA,
            pltpu.SemaphoreType.DMA,
        ],
        compiler_params=pltpu.CompilerParams(
            collective_id=1, has_side_effects=True, vmem_limit_bytes=VMEM_LIMIT
        ),
        name="backward",
    )(d_attended, images, attended, turned, act, qkv, x, d_middle, vectors, sums)


def finish_kernel(
    result,
    input_grad,
    qkv_grad,
    out_grad,
    fc1_grad,
    fc2_grad,
    totals,
    result_out,
    input_grad_out,
    qkv_out,
    out_out,
    fc1_out,
    fc2_out,
    *rest,
):
    vectors_out, (pair_out, hidden_out) = rest[:6], rest[6:]
    f, t = lax.axis_index("fsdp"), lax.axis_index("tp")
    tokens = result_out.shape[1]
    result_out[...] = result[:, :tokens]
    input_grad_out[...] = input_grad[:, :tokens]
    qkv_out[...] = qkv_grad[...]
    out_out[...] = out_grad[...]
    fc1_out[...] = fc1_grad[...]
    fc2_out[...] = fc2_grad[...]
    width = totals.shape[-1]
    own = pltpu.roll(totals[...], lax.rem(width - (f * 8 + t) * 8, width), 1)
    for number, row in enumerate((8, 9, 0, 1, 2, 3)):
        vectors_out[number][...] = own[row : row + 1, :8]
    own = pltpu.roll(totals[...], lax.rem(width - t * 128 - f * 4, width), 1)
    for kind in range(2):
        for head in range(2):
            pair_out[kind, head : head + 1, :] = own[
                10 + kind : 11 + kind, HD * head : HD * head + 4
            ]
    row = totals[4:8, :]
    mine = lax.broadcasted_iota(jnp.int32, row.shape, 0) == t // 2
    row = jnp.sum(jnp.where(mine, row, 0.0), 0, keepdims=True)
    row = pltpu.roll(
        jnp.broadcast_to(row, (8, width)), lax.rem(width - 512 * lax.rem(t, 2) - f * 4, width), 1
    )
    turned = jnp.concatenate([row[0:1, 64 * j : 64 * j + 128] for j in range(8)], axis=0)
    hidden_out[...] = turned.T[:4]


def finish(result, input_grad, qkv_grad, out_grad, fc1_grad, fc2_grad, totals):
    arrays = (result, input_grad, qkv_grad, out_grad, fc1_grad, fc2_grad)
    rows = jax.ShapeDtypeStruct((MICRO, TOKENS, result.shape[-1]), BF16)
    shapes = [rows, rows] + [jax.ShapeDtypeStruct(a.shape, a.dtype) for a in arrays[2:]]
    shapes += [jax.ShapeDtypeStruct((1, 8), F32)] * 6
    shapes += [
        jax.ShapeDtypeStruct((2, 2, 4), F32),
        jax.ShapeDtypeStruct((4, 8), F32),
    ]
    return pl.pallas_call(
        finish_kernel,
        out_shape=shapes,
        in_specs=[VMEM] * 7,
        out_specs=[VMEM] * 14,
        compiler_params=pltpu.CompilerParams(vmem_limit_bytes=VMEM_LIMIT),
        name="finish",
    )(*arrays, totals)


def per_device(
    inputs,
    cotangent,
    valid_slots,
    ln1_gain,
    ln1_bias,
    qkv_weight,
    qv_bias,
    out_weight,
    out_bias,
    ln2_gain,
    ln2_bias,
    fc1_weight,
    fc1_bias,
    fc2_weight,
    fc2_bias,
):
    micro, _, tokens, width = inputs.shape
    slot = -(-tokens // 16) * 16
    x = inputs.reshape(micro, tokens, width)
    small = [ln1_gain, ln1_bias, out_bias, ln2_gain, ln2_bias, fc2_bias]
    small = [v.reshape(1, 8) for v in small] + [qv_bias, fc1_bias.T]
    (
        d_middle,
        vectors,
        sums,
        result,
        d_attended,
        images,
        attended,
        turned,
        act,
        qkv,
        x_rows,
    ) = forward(
        x,
        cotangent.reshape(x.shape),
        valid_slots.T,
        qkv_weight,
        out_weight.T,
        fc1_weight,
        fc2_weight.T,
        small,
        slot,
    )
    qkv_grad, out_grad, fc1_grad, fc2_grad, total, input_grad = backward(
        d_attended,
        images,
        attended,
        turned,
        act,
        qkv.reshape(3, GROUP, width, 128),
        x_rows,
        d_middle,
        vectors,
        sums,
    )
    result, input_grad, qkv_grad, out_grad, fc1_grad, fc2_grad, *own, pair, hidden_grad = finish(
        result, input_grad, qkv_grad, out_grad, fc1_grad, fc2_grad, total
    )
    own = [own[i].reshape(8) for i in range(6)]
    return (
        result.reshape(inputs.shape),
        input_grad.reshape(inputs.shape),
        own[0],
        own[1],
        qkv_grad,
        pair,
        out_grad.T,
        own[2],
        own[3],
        own[4],
        fc1_grad,
        hidden_grad.T,
        fc2_grad.T,
        own[5],
    )


def solution(mesh):
    in_specs = (
        P(None, "fsdp", "tp", None),
        P(None, "fsdp", "tp", None),
        P(None, "fsdp"),
        P(("fsdp", "tp")),
        P(("fsdp", "tp")),
        P(None, "fsdp", "tp"),
        P(None, "tp", "fsdp"),
        P("tp", "fsdp"),
        P(("fsdp", "tp")),
        P(("fsdp", "tp")),
        P(("fsdp", "tp")),
        P("fsdp", "tp"),
        P("tp", "fsdp"),
        P("tp", "fsdp"),
        P(("fsdp", "tp")),
    )
    out_specs = (
        P(None, "fsdp", "tp", None),
        P(None, "fsdp", "tp", None),
        P(("fsdp", "tp")),
        P(("fsdp", "tp")),
        P(None, "fsdp", "tp"),
        P(None, "tp", "fsdp"),
        P("tp", "fsdp"),
        P(("fsdp", "tp")),
        P(("fsdp", "tp")),
        P(("fsdp", "tp")),
        P("fsdp", "tp"),
        P("tp", "fsdp"),
        P("tp", "fsdp"),
        P(("fsdp", "tp")),
    )
    return jax.shard_map(
        per_device, mesh=mesh, in_specs=in_specs, out_specs=out_specs, check_vma=False
    )
```
